32 devices in a mesh: dp: 8 (over y, x, core), ctx: 4 (over z).
Axes of the slice: x: 2, y: 2, z: 4, core: 2. Of those that a mesh axis runs over, the one named last changes fastest.
Arguments:
- query: bfloat16 [8, 512, 2560], P('dp', 'ctx'), may hold values from -213 to 213
- key_in: bfloat16 [8, 512, 2560], P('dp', 'ctx'), may hold values from -2 to 2
- value: bfloat16 [8, 512, 2560], P('dp', 'ctx'), may hold values from -6 to 6
- gate_table: float32 [1000, 5120], P(None, 'ctx'), may hold values from 1 to 4
- timestep: int32 [8], P('dp'), may hold values from 0 to 999
- out_weight: bfloat16 [2560, 5120], P('dp', 'ctx'), may hold values from -0.125 to 0.125
- grad_out: bfloat16 [8, 512, 5120], P('dp', None, 'ctx'), may hold values from -0.59765625 to 0.59765625
Outputs:
- branch_out: bfloat16 [8, 512, 5120], P('dp', None, 'ctx')
- grad_query: bfloat16 [8, 512, 2560], P('dp', 'ctx')
- grad_key: bfloat16 [8, 512, 2560], P('dp', 'ctx')
- grad_value: bfloat16 [8, 512, 2560], P('dp', 'ctx')
- grad_weight: float32 [2560, 5120], P('dp', 'ctx')
The draws below stay inside these ranges and needn't reach their ends.
All inputs are finite; a program needn't handle non-finite values.
Results may differ from the reference program's by a relative error of at most 0.035.
Values may be sent and summed in bfloat16 or wider, within the bound.
No kernel may reach another device: no remote copies, remote signals or barrier semaphores. Data moves between devices by JAX's collectives and lax.ppermute only.
A program may use at most 128 MiB of HBM per device.

```python
import jax
import jax.numpy as jnp
from jax import lax

D = 5120
HEAD_DIM = 128
NT = 1000
S_DEV = 128
HW = 2560
L = 512
CLIPS = 8
N_CTX = 4


def base_keys(key):
    return 0.5 * jnp.clip(jax.random.normal(key, (CLIPS, L, HW), jnp.float32), -3.0, 3.0)


def draw_key_in(key, part):
    keys_drawn = base_keys(key)
    return keys_drawn.astype(jnp.bfloat16)


def draw_query(key, part):
    own_key = jax.random.fold_in(key, 5)
    queries = 0.5 * jnp.clip(jax.random.normal(own_key, (CLIPS, L, HW), jnp.float32), -3.0, 3.0)
    return queries.astype(jnp.bfloat16)


def place_ends(values, stream_key, smallest, top_value):
    place = [jax.random.randint(jax.random.fold_in(stream_key, axis), (), 0, length) for axis, length in enumerate(values.shape)]
    longest = values.shape.index(max(values.shape))
    next_to = place[:longest] + [(place[longest] + 1) % values.shape[longest]] + place[longest + 1:]
    return values.at[tuple(place)].set(smallest).at[tuple(next_to)].set(top_value)


def steps_of(rng, dims, split, smallest, high):
    def one(dim, blocks):
        heights = jax.random.uniform(jax.random.fold_in(jax.random.fold_in(rng, 6), dim), (blocks,), jnp.float32, smallest / len(split), high / len(split))
        return jnp.repeat(jnp.exp(heights), dims[dim] // blocks).reshape((-1,) + (1,) * (len(dims) - dim - 1))

    loudness = one(*split[0])
    for cut in split[1:]:
        loudness = loudness * one(*cut)
    return loudness


def normal_values(rng, extent, scale, reach, shards=(), kind=jnp.bfloat16):
    entries = jax.random.normal(rng, extent, jnp.float32) * scale
    if len(shards) > 0:
        entries = steps_of(rng, extent, shards, -0.22, 0.18) * entries
    return jnp.clip(entries, min=-reach, max=reach).astype(kind)


def setup_inputs(seed: int = 0) -> dict:
    key_of = jax.random.split(jax.random.key(seed), 8)
    query = draw_query(jax.random.fold_in(key_of[7], 71), 0)
    key_in = draw_key_in(jax.random.fold_in(key_of[7], 71), 0)
    value = normal_values(key_of[2], (CLIPS, L, HW), 1.0, 6.0, ((0, 8), (1, 4)))
    gate_table = jnp.clip(1.0 + 3.0 * jax.random.uniform(key_of[3], (NT, D), jnp.float32) ** steps_of(key_of[3], (NT, D), ((1, 4),), -0.2, 0.2), 1.0, 4.0)
    timestep = place_ends(jax.random.randint(key_of[4], (CLIPS,), 0, NT), jax.random.fold_in(key_of[4], 1), 0, NT - 1).astype(jnp.int32)
    out_weight = normal_values(key_of[5], (HW, D), HW ** -0.5, 0.125, ((0, 8), (1, 4)))
    grad_out = normal_values(key_of[6], (CLIPS, L, D), 0.1, 0.59765625, ((0, 8), (2, 4)))
    return dict(query=query, key_in=key_in, value=value, gate_table=gate_table, timestep=timestep, out_weight=out_weight, grad_out=grad_out)


def rounded(values):
    return lax.optimization_barrier(values.astype(jnp.bfloat16)).astype(jnp.float32)


def reference(query, key_in, value, gate_table, timestep, out_weight, grad_out):
    head_count = HW // HEAD_DIM
    length = S_DEV * N_CTX
    block_width = D // N_CTX
    score_scale = HEAD_DIM ** -0.5
    gate_rows = gate_table[timestep]

    def one_clip(running, pieces):
        clip_query, clip_keys, clip_values, gate_row, upstream = pieces
        keys_split = clip_keys.astype(jnp.float32).reshape(length, head_count, HEAD_DIM)
        values_split = clip_values.astype(jnp.float32).reshape(length, head_count, HEAD_DIM)

        def probabilities(block_index):
            query_slab = lax.dynamic_slice_in_dim(clip_query, block_index * S_DEV, S_DEV, 0)
            query_slab = query_slab.astype(jnp.float32).reshape(S_DEV, head_count, HEAD_DIM)
            scores = jnp.einsum("qhd,khd->hqk", query_slab, keys_split) * score_scale
            row_max = jnp.max(scores, axis=2, keepdims=True)
            exp_scores = jnp.exp(scores - row_max)
            return query_slab, exp_scores / jnp.sum(exp_scores, axis=2, keepdims=True)

        def forward_block(state_none, block_index):
            query_slab, probability = probabilities(block_index)
            prob_half = rounded(probability)
            attention_slab = jnp.einsum("hqk,khd->qhd", prob_half, values_split)
            return state_none, attention_slab.reshape(S_DEV, HW).astype(jnp.bfloat16)

        blocks = jnp.arange(N_CTX, dtype=jnp.int32)
        state_none, attention = lax.scan(forward_block, jnp.zeros((), jnp.float32), blocks)
        attention = attention.reshape(length, HW)
        projected = jnp.dot(attention, out_weight, preferred_element_type=jnp.float32)
        branch = (projected * gate_row[None, :]).astype(jnp.bfloat16)
        d_proj = (upstream.astype(jnp.float32) * gate_row[None, :]).astype(jnp.bfloat16)

        def column_block(accum, block_index):
            d_part = lax.dynamic_slice_in_dim(d_proj, block_index * block_width, block_width, 1)
            columns = lax.dynamic_slice_in_dim(out_weight, block_index * block_width, block_width, 1)
            term_block = jnp.dot(d_part, columns.T, preferred_element_type=jnp.float32)
            return accum + rounded(term_block), None

        d_attn, unused = lax.scan(column_block, jnp.zeros((length, HW), jnp.float32), blocks)
        d_attn = d_attn.astype(jnp.bfloat16)
        weight_term = jnp.dot(attention.T, d_proj, preferred_element_type=jnp.float32)

        def backward_block(state_pair, block_index):
            key_accum, value_accum = state_pair
            query_slab, probability = probabilities(block_index)
            prob_half = rounded(probability)
            d_slab = lax.dynamic_slice_in_dim(d_attn, block_index * S_DEV, S_DEV, 0)
            d_slab = d_slab.astype(jnp.float32).reshape(S_DEV, head_count, HEAD_DIM)
            out_slab = lax.dynamic_slice_in_dim(attention, block_index * S_DEV, S_DEV, 0)
            out_slab = out_slab.astype(jnp.float32).reshape(S_DEV, head_count, HEAD_DIM)
            row_delta = jnp.einsum("qhd,qhd->hq", d_slab, out_slab)
            d_scores = jnp.einsum("qhd,khd->hqk", d_slab, values_split)
            d_half = rounded(probability * (d_scores - row_delta[:, :, None]) * score_scale)
            grad_slab = jnp.einsum("hqk,khd->qhd", d_half, keys_split).reshape(S_DEV, HW).astype(jnp.bfloat16)
            key_term = jnp.einsum("hqk,qhd->khd", d_half, query_slab).reshape(length, HW)
            value_term = jnp.einsum("hqk,qhd->khd", prob_half, d_slab).reshape(length, HW)
            return (key_accum + rounded(key_term), value_accum + rounded(value_term)), grad_slab

        zero_rows = jnp.zeros((length, HW), jnp.float32)
        sums, grad_slabs = lax.scan(backward_block, (zero_rows, zero_rows), blocks)
        outputs = (branch, grad_slabs.reshape(length, HW), sums[0].astype(jnp.bfloat16), sums[1].astype(jnp.bfloat16))
        return running + weight_term, outputs

    weight_sum, results = lax.scan(one_clip, jnp.zeros((HW, D), jnp.float32), (query, key_in, value, gate_rows, grad_out))
    return (results[0], results[1], results[2], results[3], weight_sum)
```

```python
import jax
import jax.numpy as jnp
from jax import lax
from jax.experimental import pallas as pl
from jax.experimental.pallas import tpu as pltpu
from jax.sharding import PartitionSpec as P

HEAD_DIM = 128
F32 = jnp.float32
BF16 = jnp.bfloat16
VMEM_LIMIT = 48 * 1024 * 1024


def dot(a, b, dims):
    return lax.dot_general(a, b, (dims, ((), ())), preferred_element_type=F32)


def params():
    return pltpu.CompilerParams(
        dimension_semantics=("arbitrary",), vmem_limit_bytes=VMEM_LIMIT
    )


def cost(flops, nbytes, exps=0):
    return pl.CostEstimate(flops=flops, bytes_accessed=nbytes, transcendentals=exps)


def add_rounded(a, b):
    return (a.astype(F32) + b.astype(F32)).astype(BF16)


def probabilities(q, k):
    scores = dot(q, k, ((1,), (1,))) * (HEAD_DIM ** (-0.5))
    shifted = jnp.exp(scores - jnp.max(scores, axis=1, keepdims=True))
    return shifted * (1.0 / jnp.sum(shifted, axis=1, keepdims=True))


def attention_call(me, pieces):
    n = len(pieces)
    _, rows, width = pieces[0].shape
    heads = width // HEAD_DIM

    def body(me_ref, *refs):
        piece_refs, out_ref = refs[:n], refs[n]
        q, k, v = (jnp.concatenate([r[t] for r in piece_refs], axis=0) for t in range(3))
        out = dot(probabilities(q, k).astype(BF16), v, ((1,), (0,))).astype(BF16)
        for s in range(n):
            slab = lax.rem(me_ref[0] + n - s, n)
            out_ref[pl.ds(pl.multiple_of(slab * rows, rows), rows), :] = out[
                s * rows : (s + 1) * rows
            ]

    length = n * rows
    return pl.pallas_call(
        body,
        grid_spec=pltpu.PrefetchScalarGridSpec(
            num_scalar_prefetch=1,
            grid=(heads,),
            in_specs=[pl.BlockSpec((3, rows, HEAD_DIM), lambda h, me: (0, 0, h))] * n,
            out_specs=pl.BlockSpec((length, HEAD_DIM), lambda h, me: (0, h)),
        ),
        out_shape=jax.ShapeDtypeStruct((length, width), BF16),
        compiler_params=params(),
        cost_estimate=cost(
            4 * length * length * width, 8 * length * width, heads * length * length
        ),
        name="attention_heads",
    )(me, *pieces)


def attention_grad_call(me, pieces, attention, d_terms):
    n = len(pieces)
    _, rows, width = pieces[0].shape
    heads = width // HEAD_DIM
    length = n * rows
    n_terms = len(d_terms)
    scale = HEAD_DIM ** (-0.5)

    def body(me_ref, *refs):
        piece_refs, attn_ref = refs[:n], refs[n]
        term_refs, out_refs = refs[n + 1 : n + 1 + n_terms], refs[n + 1 + n_terms :]
        q, k, v = (jnp.concatenate([r[t] for r in piece_refs], axis=0) for t in range(3))
        places = [
            pl.ds(pl.multiple_of(lax.rem(me_ref[0] + n - s, n) * rows, rows), rows)
            for s in range(n)
        ]
        attn = jnp.concatenate([attn_ref[p, :] for p in places], axis=0).astype(F32)
        d_attn = jnp.concatenate(
            [sum(t[p, :].astype(F32) for t in term_refs) for p in places], axis=0
        ).astype(BF16)
        prob = probabilities(q, k)
        delta = jnp.sum(d_attn.astype(F32) * attn, axis=1, keepdims=True)
        d_prob = dot(d_attn, v, ((1,), (1,)))
        d_half = (prob * (d_prob - delta) * scale).astype(BF16)
        grads = (
            dot(d_half, k, ((1,), (0,))),
            dot(d_half, q, ((0,), (0,))),
            dot(prob.astype(BF16), d_attn, ((0,), (0,))),
        )
        for t in range(3):
            g = grads[t].astype(BF16)
            for s in range(n):
                out_refs[s][t] = g[s * rows : (s + 1) * rows]

    piece = pl.BlockSpec((3, rows, HEAD_DIM), lambda h, me: (0, 0, h))
    whole = pl.BlockSpec((length, HEAD_DIM), lambda h, me: (0, h))
    return pl.pallas_call(
        body,
        grid_spec=pltpu.PrefetchScalarGridSpec(
            num_scalar_prefetch=1,
            grid=(heads,),
            in_specs=[piece] * n + [whole] * (1 + n_terms),
            out_specs=[piece] * n,
        ),
        out_shape=[jax.ShapeDtypeStruct((3, rows, width), BF16)] * n,
        compiler_params=params(),
        cost_estimate=cost(
            10 * length * length * width, 24 * length * width, heads * length * length
        ),
        name="attention_heads_grad",
    )(me, *pieces, attention, *d_terms)


def d_attn_parts_call(me, d_proj, weight, n):
    length, cols = d_proj.shape
    width = weight.shape[0] // n

    def body(me_ref, d_ref, w_ref, *out_refs):
        part = dot(d_ref[...], w_ref[...], ((1,), (1,))).astype(BF16)
        for s in range(n):

            @pl.when(pl.program_id(0) == s)
            def _():
                out_refs[s][...] = part

    return pl.pallas_call(
        body,
        grid_spec=pltpu.PrefetchScalarGridSpec(
            num_scalar_prefetch=1,
            grid=(n,),
            in_specs=[
                pl.BlockSpec((length, cols), lambda s, me: (0, 0)),
                pl.BlockSpec((width, cols), lambda s, me: (lax.rem(me[0] + s, n), 0)),
            ],
            out_specs=[pl.BlockSpec((length, width), lambda s, me: (0, 0))] * n,
        ),
        out_shape=[jax.ShapeDtypeStruct((length, width), BF16)] * n,
        compiler_params=params(),
        cost_estimate=cost(
            2 * length * cols * width * n, 2 * (length * cols + n * width * (cols + length))
        ),
        name="d_attn_parts",
    )(me, d_proj, weight)


def gathered_specs(n, length, width):
    return [pl.BlockSpec((length, width), lambda s, *_: (0, 0))] * (2 * n - 1)


def gathered_piece(refs, me, n, s):
    own, from_left, from_right = refs[0], refs[1:n], refs[n:]
    if s == 0:
        return own[...]
    return jnp.where(me + s < n, from_right[s - 1][...], from_left[n - s - 1][...])


def projection_call(me, gathered, weight, gate_row, n):
    length, width = gathered[0].shape
    cols = weight.shape[1]

    def body(me_ref, *refs):
        w_ref, gate_ref, out_ref, total = refs[2 * n - 1 :]
        for s in range(n):

            @pl.when(pl.program_id(0) == s)
            def _():
                piece = gathered_piece(refs[: 2 * n - 1], me_ref[0], n, s)
                term = dot(piece, w_ref[...], ((1,), (0,)))
                if s == 0:
                    total[...] = term
                elif s < n - 1:
                    total[...] += term
                else:
                    out_ref[...] = ((total[...] + term) * gate_ref[...]).astype(BF16)

    return pl.pallas_call(
        body,
        grid_spec=pltpu.PrefetchScalarGridSpec(
            num_scalar_prefetch=1,
            grid=(n,),
            in_specs=gathered_specs(n, length, width)
            + [
                pl.BlockSpec((width, cols), lambda s, me: (lax.rem(me[0] + s, n), 0)),
                pl.BlockSpec((1, cols), lambda s, me: (0, 0)),
            ],
            out_specs=pl.BlockSpec((length, cols), lambda s, me: (0, 0)),
            scratch_shapes=[pltpu.VMEM((length, cols), F32)],
        ),
        out_shape=jax.ShapeDtypeStruct((length, cols), BF16),
        compiler_params=params(),
        cost_estimate=cost(
            2 * length * cols * width * n, 2 * (length * cols + n * width * (cols + 2 * length))
        ),
        name="projection",
    )(me, *gathered, weight, gate_row)


def weight_grad_call(place, gathered, d_proj, n, dp):
    length, width = gathered[0].shape
    cols = d_proj.shape[1]
    rows = n * width // dp
    per_piece = width // (2 * rows)

    def body(place_ref, *refs):
        d_ref, keep_ref, send_ref = refs[2 * n - 1 :]
        for s in range(n):

            @pl.when(pl.program_id(0) == s)
            def _():
                piece = gathered_piece(refs[: 2 * n - 1], place_ref[0], n, s)
                term = dot(piece, d_ref[...], ((0,), (0,))).astype(BF16)
                term = term.reshape(per_piece, 2, rows, cols)
                first = place_ref[1] == 0
                keep_ref[...] = jnp.where(first, term[:, 0], term[:, 1])
                send_ref[...] = jnp.where(first, term[:, 1], term[:, 0])

    block = pl.BlockSpec(
        (per_piece, rows, cols), lambda s, place: (lax.rem(place[0] + s, n), 0, 0)
    )
    return pl.pallas_call(
        body,
        grid_spec=pltpu.PrefetchScalarGridSpec(
            num_scalar_prefetch=1,
            grid=(n,),
            in_specs=gathered_specs(n, length, width)
            + [pl.BlockSpec((length, cols), lambda s, place: (0, 0))],
            out_specs=[block, block],
        ),
        out_shape=[jax.ShapeDtypeStruct((dp // 2, rows, cols), BF16)] * 2,
        compiler_params=params(),
        cost_estimate=cost(
            2 * length * cols * width * n, 2 * (length * cols + n * width * (cols + 2 * length))
        ),
        name="weight_grad",
    )(place, *gathered, d_proj)


def assemble_call(me, pieces):
    n = len(pieces)
    _, rows, width = pieces[0].shape

    def body(me_ref, *refs):
        for t in range(3):
            for s in range(n):
                source = lax.rem(me_ref[0] + s, n)
                refs[n + t][:, pl.ds(pl.multiple_of(source * width, 128), width)] = refs[s][t]

    return pl.pallas_call(
        body,
        grid_spec=pltpu.PrefetchScalarGridSpec(
            num_scalar_prefetch=1,
            grid=(1,),
            in_specs=[pl.BlockSpec((3, rows, width), lambda i, me: (0, 0, 0))] * n,
            out_specs=[pl.BlockSpec((rows, n * width), lambda i, me: (0, 0))] * 3,
        ),
        out_shape=[jax.ShapeDtypeStruct((rows, n * width), BF16)] * 3,
        compiler_params=params(),
        cost_estimate=cost(0, 12 * n * rows * width),
        name="assemble_heads",
    )(me, *pieces)


def shift(x, axis, by):
    n = lax.axis_size(axis)
    return lax.ppermute(x, axis, [(i, (i + by) % n) for i in range(n)])


def line_gather(own, axis):
    n = lax.axis_size(axis)
    left, right = [], []
    to_right = to_left = own
    for i in range(1, n):
        to_right = lax.ppermute(to_right, axis, [(d, d + 1) for d in range(i - 1, n - 1)])
        to_left = lax.ppermute(to_left, axis, [(d, d - 1) for d in range(1, n - i + 1)])
        left.append(to_right)
        right.append(to_left)
    return left, right


def line_scatter(parts, axis):
    n = lax.axis_size(axis)
    to_right, to_left = parts[n - 1], parts[1]
    for i in range(1, n):
        if i > 1:
            to_right = add_rounded(parts[n - i], to_right)
            to_left = add_rounded(parts[i], to_left)
        to_right = lax.ppermute(to_right, axis, [(d, d + 1) for d in range(i)])
        to_left = lax.ppermute(to_left, axis, [(d, d - 1) for d in range(n - i, n)])
    return [parts[0], to_right, to_left]


def halving_scatter(keep, send, axis):
    n = lax.axis_size(axis)
    index = lax.axis_index(axis)

    def swap(x, bit):
        return lax.ppermute(x, axis, [(i, i ^ (1 << bit)) for i in range(n)])

    bits = list(range(1, n.bit_length() - 1))
    total = add_rounded(keep, swap(send, 0))
    rows, cols = keep.shape[1:]
    total = total.reshape((2,) * len(bits) + (2, rows // 2, cols))
    halves = [lax.index_in_dim(total, i, len(bits), False) for i in range(2)]
    orders = [bits, bits[::-1]]
    left = [list(bits[::-1]), list(bits[::-1])]
    for step in range(len(bits)):
        for h in range(2):
            bit = orders[h][step]
            dim = left[h].index(bit)
            left[h].remove(bit)
            mine = (index >> bit) & 1
            got = swap(lax.dynamic_index_in_dim(halves[h], 1 - mine, dim, False), bit)
            kept = lax.dynamic_index_in_dim(halves[h], mine, dim, False)
            halves[h] = kept.astype(F32) + got.astype(F32)
            if step < len(bits) - 1:
                halves[h] = halves[h].astype(BF16)
    return jnp.concatenate(halves, axis=0)


def by_heads(query, key_in, value, gate_table, timestep, out_weight, grad_out):
    n, dp = lax.axis_size("ctx"), lax.axis_size("dp")
    me = lax.axis_index("ctx").astype(jnp.int32)
    me_ref = me[None]
    width = query.shape[2] // n
    weight = lax.all_gather(out_weight, "dp", axis=0, tiled=True)

    def columns_for(device):
        return jnp.concatenate(
            [lax.dynamic_slice_in_dim(x, device * width, width, 2) for x in (query, key_in, value)],
            axis=0,
        )

    pieces = [columns_for(me)]
    pieces += [shift(columns_for((me + s) % n), "ctx", s) for s in range(1, n)]

    gate_row = lax.dynamic_slice_in_dim(gate_table, timestep[0], 1, 0)
    d_proj = (grad_out[0].astype(F32) * gate_row).astype(BF16)

    attention = attention_call(me_ref, pieces)
    parts = d_attn_parts_call(me_ref, d_proj, weight, n)
    left, right = line_gather(attention, "ctx")
    d_terms = line_scatter(parts, "ctx")
    gathered = [attention] + left + right
    place = jnp.stack([me, (lax.axis_index("dp") % 2).astype(jnp.int32)])
    keep, send = weight_grad_call(place, gathered, d_proj, n, dp)
    grad_weight = halving_scatter(keep, send, "dp")
    branch_out = projection_call(me_ref, gathered, weight, gate_row, n)[None]

    grads = attention_grad_call(me_ref, pieces, attention, d_terms)
    grads = [grads[0]] + [shift(grads[s], "ctx", -s) for s in range(1, n)]
    grad_query, grad_key, grad_value = assemble_call(me_ref, grads)
    return (branch_out, grad_query[None], grad_key[None], grad_value[None], grad_weight)


def by_tokens(query, key_in, value, gate_table, timestep, out_weight, grad_out):
    slab_rows = query.shape[1]
    attn_width = query.shape[2]
    head_count = attn_width // HEAD_DIM
    score_scale = HEAD_DIM ** (-0.5)
    query_heads = query[0].reshape(slab_rows, head_count, HEAD_DIM)
    keys_whole, values_whole = (
        lax.all_gather(key_in, "ctx", axis=1, tiled=True),
        lax.all_gather(value, "ctx", axis=1, tiled=True),
    )
    keys_all = keys_whole[0]
    values_all = values_whole[0]
    scores = (
        jnp.einsum(
            "qhd,khd->hqk",
            query_heads,
            keys_all.reshape(keys_all.shape[0], head_count, HEAD_DIM),
            preferred_element_type=jnp.float32,
        )
        * score_scale
    )
    length = keys_all.shape[0]
    key_heads = keys_all.reshape(length, head_count, HEAD_DIM)
    value_heads = values_all.reshape(length, head_count, HEAD_DIM)
    row_max = jnp.max(scores, axis=2, keepdims=True)
    exp_scores = jnp.exp(scores - row_max)
    probability = exp_scores / jnp.sum(exp_scores, axis=2, keepdims=True)
    prob_half = probability.astype(jnp.bfloat16)
    attention = jnp.einsum(
        "hqk,khd->qhd", prob_half, value_heads, preferred_element_type=jnp.float32
    )
    attention = attention.reshape(slab_rows, attn_width).astype(jnp.bfloat16)
    marker = (
        timestep[:, None] == jnp.arange(gate_table.shape[0], dtype=jnp.int32)[None, :]
    ).astype(jnp.float32)
    gate_row = jnp.dot(marker, gate_table, precision=lax.Precision.HIGHEST)
    attn_rows = lax.all_gather(attention, "ctx", axis=0, tiled=True)
    columns = attn_rows
    projected = jnp.dot(
        columns,
        lax.all_gather(out_weight, "dp", axis=0, tiled=True),
        preferred_element_type=jnp.float32,
    )
    branch_out = (projected * gate_row).astype(jnp.bfloat16)[None]
    d_proj = (grad_out[0].astype(jnp.float32) * gate_row).astype(jnp.bfloat16)
    partial_rows = jnp.einsum(
        "td,rd->tr",
        d_proj,
        lax.all_gather(out_weight, "dp", axis=0, tiled=True),
        preferred_element_type=jnp.float32,
    )
    d_attn = lax.psum_scatter(
        partial_rows.astype(jnp.bfloat16), "ctx", scatter_dimension=0, tiled=True
    ).astype(jnp.float32)
    d_attn = d_attn.astype(jnp.bfloat16)
    columns = attn_rows
    grad_weight = lax.psum_scatter(
        jnp.einsum("tr,td->rd", columns, d_proj, preferred_element_type=jnp.float32).astype(
            jnp.bfloat16
        ),
        "dp",
        scatter_dimension=0,
        tiled=True,
    ).astype(jnp.float32)
    d_heads = d_attn.reshape(slab_rows, head_count, HEAD_DIM)
    out_heads = attention.reshape(slab_rows, head_count, HEAD_DIM)
    row_delta = jnp.einsum("qhd,qhd->hq", d_heads, out_heads, preferred_element_type=jnp.float32)
    d_scores = jnp.einsum("qhd,khd->hqk", d_heads, value_heads, preferred_element_type=jnp.float32)
    d_half = (probability * (d_scores - row_delta[:, :, None]) * score_scale).astype(jnp.bfloat16)
    grad_query = jnp.einsum("hqk,khd->qhd", d_half, key_heads, preferred_element_type=jnp.float32)
    grad_query = grad_query.reshape(slab_rows, attn_width).astype(jnp.bfloat16)
    key_part = jnp.einsum(
        "hqk,qhd->khd", d_half, query_heads, preferred_element_type=jnp.float32
    ).reshape(slab_rows * lax.axis_size("ctx"), attn_width)
    value_part = jnp.einsum(
        "hqk,qhd->khd", prob_half, d_heads, preferred_element_type=jnp.float32
    ).reshape(slab_rows * lax.axis_size("ctx"), attn_width)
    key_sums = lax.psum_scatter(
        jnp.concatenate([key_part, value_part], axis=1).astype(jnp.bfloat16),
        "ctx",
        scatter_dimension=0,
        tiled=True,
    ).astype(jnp.float32)
    grad_key = key_sums[:, :attn_width].astype(jnp.bfloat16)
    grad_value = key_sums[:, attn_width:].astype(jnp.bfloat16)
    return (branch_out, grad_query[None], grad_key[None], grad_value[None], grad_weight)


def on_device(query, key_in, value, gate_table, timestep, out_weight, grad_out):
    n, dp = lax.axis_size("ctx"), lax.axis_size("dp")
    heads = query.shape[2] // HEAD_DIM
    rows = out_weight.shape[0]
    fits = heads % n == 0 and dp & (dp - 1) == 0 and dp >= 4
    fits = fits and (heads // n) * HEAD_DIM % (2 * rows) == 0 and rows % 32 == 0 and n > 1
    plan = by_heads if fits else by_tokens
    return plan(query, key_in, value, gate_table, timestep, out_weight, grad_out)


def solution(mesh):
    in_specs = (
        P("dp", "ctx", None),
        P("dp", "ctx", None),
        P("dp", "ctx", None),
        P(None, "ctx"),
        P("dp"),
        P("dp", "ctx"),
        P("dp", None, "ctx"),
    )
    out_specs = (
        P("dp", None, "ctx"),
        P("dp", "ctx", None),
        P("dp", "ctx", None),
        P("dp", "ctx", None),
        P("dp", "ctx"),
    )
    return jax.shard_map(
        on_device, mesh=mesh, in_specs=in_specs, out_specs=out_specs, check_vma=False
    )
```

```python
import math

import jax
import jax.numpy as jnp
from jax import lax
from jax.experimental import pallas as pl
from jax.experimental.pallas import tpu as pltpu
from jax.sharding import PartitionSpec as P

HEAD_DIM = 128
F32 = jnp.float32
BF16 = jnp.bfloat16
MIB = 1024 * 1024
PARTS = 2


def dot(a, b, dims):
    return lax.dot_general(a, b, (dims, ((), ())), preferred_element_type=F32)


def params(mib=32):
    return pltpu.CompilerParams(
        dimension_semantics=("arbitrary",), vmem_limit_bytes=mib * MIB
    )


def cost(flops, nbytes, exps=0):
    return pl.CostEstimate(flops=flops, bytes_accessed=nbytes, transcendentals=exps)


def any_specs(count):
    return [pl.BlockSpec(memory_space=pl.ANY)] * count


def add_rounded(a, b):
    return (a.astype(F32) + b.astype(F32)).astype(BF16)


def exponentials(q, k):
    scores = dot(k, q, ((1,), (1,)))
    top = jnp.max(scores, axis=0, keepdims=True)
    shifted = jnp.exp2((scores - top) * (HEAD_DIM ** (-0.5) * math.log2(math.e)))
    return shifted, 1.0 / jnp.sum(shifted, axis=0, keepdims=True)


def slab_rows(me, n, rows):
    return [pl.ds(pl.multiple_of(lax.rem(me + n - s, n) * rows, rows), rows) for s in range(n)]


def head_lanes(width):
    return [slice(i, i + HEAD_DIM) for i in range(0, width, HEAD_DIM)]


def pack_call(place, query, key_in, value, n, widths):
    rows, width = query.shape[1], sum(widths)

    def body(place_ref, *refs):
        for s in range(n):

            @pl.when(pl.program_id(0) == s)
            def _():
                start = 0
                for g in range(len(widths)):
                    for t in range(3):
                        refs[3 + g * n + s][t] = refs[t][0, :, start : start + widths[g]]
                    start += widths[g]

    block = pl.BlockSpec((1, rows, width), lambda s, p: (0, 0, lax.rem(p[0] + s, n)))
    outs = pl.pallas_call(
        body,
        grid_spec=pltpu.PrefetchScalarGridSpec(
            num_scalar_prefetch=1,
            grid=(n,),
            in_specs=[block] * 3,
            out_specs=[
                pl.BlockSpec((3, rows, w), lambda s, p: (0, 0, 0)) for w in widths for _ in range(n)
            ],
        ),
        out_shape=[jax.ShapeDtypeStruct((3, rows, w), BF16) for w in widths for _ in range(n)],
        compiler_params=params(),
        cost_estimate=cost(0, 12 * n * rows * width),
        name="pack_heads",
    )(place, query, key_in, value)
    return [list(outs[g * n : (g + 1) * n]) for g in range(len(widths))]


def attention_call(place, pieces):
    n = len(pieces)
    _, rows, width = pieces[0].shape
    length = n * rows
    block = length // PARTS

    def body(place_ref, *refs):
        piece_refs, out_refs, out_ref = refs[:n], refs[n:-1], refs[-1]
        places = slab_rows(place_ref[0], n, rows)
        for lanes in head_lanes(width):
            q, k, v = (
                jnp.concatenate([r[t, :, lanes] for r in piece_refs], axis=0) for t in range(3)
            )
            shifted, inverse = exponentials(q, k)
            out = dot(v, shifted.astype(BF16), ((0,), (0,))) * inverse
            out = out.T.astype(BF16)
            for s in range(n):
                out_ref[places[s], lanes] = out[s * rows : (s + 1) * rows]
        for i in range(PARTS):
            out_refs[i][...] = out_ref[i * block : (i + 1) * block]

    return pl.pallas_call(
        body,
        grid_spec=pltpu.PrefetchScalarGridSpec(
            num_scalar_prefetch=1,
            grid=(1,),
            in_specs=[pl.BlockSpec((3, rows, width), lambda i, p: (0, 0, 0))] * n,
            out_specs=[pl.BlockSpec((block, width), lambda i, p: (0, 0))] * PARTS,
            scratch_shapes=[pltpu.VMEM((length, width), BF16)],
        ),
        out_shape=[jax.ShapeDtypeStruct((block, width), BF16)] * PARTS,
        compiler_params=params(32),
        cost_estimate=cost(
            4 * length * length * width, 8 * length * width, length * length * width // HEAD_DIM
        ),
        name="attention_heads",
    )(place, *pieces)


def attention_grad_call(place, pieces, attention, d_terms):
    n = len(pieces)
    _, rows, width = pieces[0].shape
    length = n * rows
    block = length // PARTS
    n_terms = len(d_terms)
    scale = HEAD_DIM ** (-0.5)

    def body(place_ref, *refs):
        piece_refs, attn_refs = refs[:n], refs[n : n + PARTS]
        term_refs = refs[n + PARTS : n + PARTS * (1 + n_terms)]
        out_refs, (attn_held, d_held) = refs[n + PARTS * (1 + n_terms) : -2], refs[-2:]
        places = slab_rows(place_ref[0], n, rows)
        for i in range(PARTS):
            here = slice(i * block, (i + 1) * block)
            attn_held[here] = attn_refs[i][...]
            terms = [term_refs[t * PARTS + i][...].astype(F32) for t in range(n_terms)]
            d_held[here] = sum(terms).astype(BF16)
        for lanes in head_lanes(width):
            q, k, v = (
                jnp.concatenate([r[t, :, lanes] for r in piece_refs], axis=0) for t in range(3)
            )
            attn = jnp.concatenate([attn_held[p, lanes] for p in places], axis=0).astype(F32)
            d_attn = jnp.concatenate([d_held[p, lanes] for p in places], axis=0)
            shifted, inverse = exponentials(q, k)
            prob = shifted * inverse
            delta = jnp.sum(d_attn.astype(F32) * attn, axis=1, keepdims=True).T
            d_prob = dot(v, d_attn, ((1,), (1,)))
            d_half = (prob * (d_prob - delta) * scale).astype(BF16)
            grads = (
                dot(k, d_half, ((0,), (0,))).T,
                dot(d_half, q, ((1,), (0,))),
                dot(prob.astype(BF16), d_attn, ((1,), (0,))),
            )
            for t in range(3):
                g = grads[t].astype(BF16)
                for s in range(n):
                    out_refs[s][t, :, lanes] = g[s * rows : (s + 1) * rows]

    piece = pl.BlockSpec((3, rows, width), lambda i, p: (0, 0, 0))
    part = pl.BlockSpec((block, width), lambda i, p: (0, 0))
    return pl.pallas_call(
        body,
        grid_spec=pltpu.PrefetchScalarGridSpec(
            num_scalar_prefetch=1,
            grid=(1,),
            in_specs=[piece] * n + [part] * (PARTS * (1 + n_terms)),
            out_specs=[piece] * n,
            scratch_shapes=[pltpu.VMEM((length, width), BF16)] * 2,
        ),
        out_shape=[jax.ShapeDtypeStruct((3, rows, width), BF16)] * n,
        compiler_params=params(32),
        cost_estimate=cost(
            10 * length * length * width, 24 * length * width, length * length * width // HEAD_DIM
        ),
        name="attention_heads_grad",
    )(place, *pieces, *attention, *sum(d_terms, []))


def ahead(place_ref, s, n):
    me, core = place_ref[0], place_ref[1]
    return lax.rem(jnp.where(core == 0, me + s, me + n - s), n)


def position(place_ref, n):
    return jnp.where(place_ref[1] == 0, place_ref[0], n - 1 - place_ref[0])


def fetch_weight(shard_refs, held, sems, place_ref):
    core, index = place_ref[1], place_ref[2]
    own, one, two, own_o, one_o, two_o = shard_refs
    first, second = jnp.where(core == 0, 2, 4), jnp.where(core == 0, 4, 2)
    places = [
        (own, 0),
        (own_o, 1),
        (one, first),
        (one_o, second + 1),
        (two.at[0], second),
        (two_o.at[0], first + 1),
        (two.at[1], 6),
        (two_o.at[1], 7),
    ]
    for ref, step in places:
        owner = index ^ step
        pltpu.make_async_copy(ref, held.at[owner], sems.at[owner]).start()


def wait_weight(shard_refs, held, sems, first, count):
    for i in range(count):
        pltpu.make_async_copy(shard_refs[0], held.at[first + i], sems.at[first + i]).wait()


def fetch_heads(own, left, right, held, sems, pos, n):
    size = own[0].shape[0]
    for g in range(len(own)):
        rows = pl.ds(g * size, size)
        pltpu.make_async_copy(own[g], held.at[0, rows], sems.at[0, g]).start()
        for s in range(1, n):

            def copy(source, s=s, g=g, rows=rows):
                pltpu.make_async_copy(source, held.at[s, rows], sems.at[s, g]).start()

            @pl.when(pos + s < n)
            def _():
                copy(right[g][s - 1])

            @pl.when(pos + s >= n)
            def _():
                copy(left[g][n - s - 1])


def wait_heads(own, held, sems, s):
    size = own[0].shape[0]
    for g in range(len(own)):
        pltpu.make_async_copy(own[g], held.at[s, pl.ds(g * size, size)], sems.at[s, g]).wait()


def split_heads_refs(refs, groups, n):
    own = refs[:groups]
    rest = refs[groups : groups + 2 * groups * (n - 1)]
    lists = [rest[i * (n - 1) : (i + 1) * (n - 1)] for i in range(2 * groups)]
    return own, lists[:groups], lists[groups:]


def gated(d_ref, gate_ref):
    return (d_ref[...].astype(F32) * gate_ref[...]).astype(BF16)


def d_attn_parts_call(place, grad_out, gate_row, shards, n):
    length, cols = grad_out.shape
    rows, n_shards = shards[0].shape[0], len(shards)
    width = 2 * rows
    dp, per, block = 2 * n, 2, length // PARTS

    def body(place_ref, d_ref, gate_ref, *refs):
        shard_refs, out_refs, (held, sems) = refs[:n_shards], refs[n_shards:-2], refs[-2:]
        fetch_weight(shard_refs, held, sems, place_ref)
        d_proj = gated(d_ref, gate_ref)
        for s in (n - 1, *range(1, n - 1), 0):
            first = ahead(place_ref, s, n) * per
            wait_weight(shard_refs, held, sems, first, per)
            part = dot(d_proj, held[pl.ds(first, per)].reshape(width, cols), ((1,), (1,)))
            for g in range(PARTS):
                out_refs[g * n + s][...] = part[g * block : (g + 1) * block].astype(BF16)

    outs = pl.pallas_call(
        body,
        grid_spec=pltpu.PrefetchScalarGridSpec(
            num_scalar_prefetch=1,
            grid=(1,),
            in_specs=[
                pl.BlockSpec((length, cols), lambda i, p: (0, 0)),
                pl.BlockSpec((1, cols), lambda i, p: (0, 0)),
            ]
            + any_specs(n_shards),
            out_specs=[pl.BlockSpec((block, width), lambda i, p: (0, 0))] * (PARTS * n),
            scratch_shapes=[pltpu.VMEM((dp, rows, cols), BF16), pltpu.SemaphoreType.DMA((dp,))],
        ),
        out_shape=[jax.ShapeDtypeStruct((block, width), BF16)] * (PARTS * n),
        compiler_params=params(),
        cost_estimate=cost(
            2 * length * cols * width * n, 2 * (length * cols + n * width * (cols + length))
        ),
        name="d_attn_parts",
    )(place, grad_out, gate_row, *shards)
    return [outs[g * n : (g + 1) * n] for g in range(PARTS)]


def heads_scratch(n, length, width):
    return [pltpu.VMEM((n, length, width), BF16), pltpu.SemaphoreType.DMA((n, PARTS))]


def projection_call(place, own, behind, front, shards, gate_row, n):
    groups = len(own)
    length, width = groups * own[0].shape[0], own[0].shape[1]
    n_shards, (rows, cols) = len(shards), shards[0].shape
    dp, per, count = n * width // rows, width // rows, groups * (2 * n - 1)

    def body(place_ref, gate_ref, *refs):
        heads = split_heads_refs(refs[:count], groups, n)
        shard_refs = refs[count : count + n_shards]
        out_ref, w_held, w_sems, held, sems = refs[count + n_shards :]
        fetch_heads(*heads, held, sems, position(place_ref, n), n)
        fetch_weight(shard_refs, w_held, w_sems, place_ref)
        total = None
        for s in range(n):
            first = ahead(place_ref, s, n) * per
            wait_heads(heads[0], held, sems, s)
            wait_weight(shard_refs, w_held, w_sems, first, per)
            block = w_held[pl.ds(first, per)].reshape(width, cols)
            term = dot(held[s], block, ((1,), (0,)))
            total = term if s == 0 else total + term
        out_ref[...] = (total * gate_ref[...]).astype(BF16)

    return pl.pallas_call(
        body,
        grid_spec=pltpu.PrefetchScalarGridSpec(
            num_scalar_prefetch=1,
            grid=(1,),
            in_specs=[pl.BlockSpec((1, cols), lambda i, p: (0, 0))] + any_specs(count + n_shards),
            out_specs=pl.BlockSpec((length, cols), lambda i, p: (0, 0)),
            scratch_shapes=[
                pltpu.VMEM((dp, rows, cols), BF16),
                pltpu.SemaphoreType.DMA((dp,)),
                pltpu.VMEM((n, length, width), BF16),
                pltpu.SemaphoreType.DMA((n, groups)),
            ],
        ),
        out_shape=jax.ShapeDtypeStruct((length, cols), BF16),
        compiler_params=params(),
        cost_estimate=cost(
            2 * length * cols * width * n, 2 * (length * cols + n * width * (cols + length))
        ),
        name="projection",
    )(place, gate_row, *own, *sum(behind, []), *sum(front, []), *shards)


def weight_grad_call(place, steps, items, grad_out, gate_row, n, begun=None):
    block, width = items[0][0][0].shape
    length, cols = PARTS * block, grad_out.shape[1]
    rows, many = width // 2, len(steps)

    def body(place_ref, d_ref, gate_ref, *refs):
        keep_ref, send_ref, d_proj, held, sems = refs[-5:]
        i = pl.program_id(0)
        pos = position(place_ref, n)

        @pl.when(i == 0)
        def _():
            for j, s in enumerate(steps):
                for g in range(PARTS):
                    behind, front = refs[2 * (j * PARTS + g) : 2 * (j * PARTS + g) + 2]
                    there = held.at[j, pl.ds(g * block, block)]

                    @pl.when(pos + s < n)
                    def _():
                        pltpu.make_async_copy(front, there, sems.at[j, g]).start()

                    @pl.when(pos + s >= n)
                    def _():
                        pltpu.make_async_copy(behind, there, sems.at[j, g]).start()

            d_proj[...] = gated(d_ref, gate_ref)

        for g in range(PARTS):
            there = held.at[i, pl.ds(g * block, block)]
            pltpu.make_async_copy(refs[0], there, sems.at[i, g]).wait()
        term = dot(held[i], d_proj[...], ((0,), (0,))).astype(BF16)
        first = place_ref[1] == 0
        keep_ref[0] = jnp.where(first, term[:rows], term[rows:])
        send_ref[0] = jnp.where(first, term[rows:], term[:rows])

    def out_spec(other):
        def slot(i, place):
            s = sum(jnp.where(i == j, step, 0) for j, step in enumerate(steps))
            chip = ahead(place, s, n) ^ (place[2] // 2)
            x, y = chip % 2, chip // 2
            return jnp.where((place[1] ^ other) == 0, 2 * x + y, 2 * y + x), 0, 0

        return pl.BlockSpec((1, rows, cols), slot)

    flat = [x for item in items for pair in item for x in pair]
    begun = list(begun or ())
    return pl.pallas_call(
        body,
        grid_spec=pltpu.PrefetchScalarGridSpec(
            num_scalar_prefetch=1,
            grid=(many,),
            in_specs=[
                pl.BlockSpec((length, cols), lambda s, p: (0, 0)),
                pl.BlockSpec((1, cols), lambda s, p: (0, 0)),
            ]
            + any_specs(len(flat) + len(begun)),
            out_specs=[out_spec(0), out_spec(1)],
            scratch_shapes=[
                pltpu.VMEM((length, cols), BF16),
                pltpu.VMEM((many, length, width), BF16),
                pltpu.SemaphoreType.DMA((many, PARTS)),
            ],
        ),
        out_shape=[jax.ShapeDtypeStruct((n, rows, cols), BF16)] * 2,
        input_output_aliases={3 + len(flat) + i: i for i in range(len(begun))},
        compiler_params=params(),
        cost_estimate=cost(
            2 * length * cols * width * many,
            2 * (length * cols + many * width * (cols + 2 * length)),
        ),
        name="weight_grad",
    )(place, grad_out, gate_row, *flat, *begun)


def assemble_call(place, pieces):
    n = len(pieces)
    _, rows, width = pieces[0].shape

    def body(place_ref, *refs):
        for t in range(3):
            for s in range(n):
                start = lax.rem(place_ref[0] + s, n) * width
                lanes = pl.ds(pl.multiple_of(start, HEAD_DIM), width)
                refs[n + t][:, lanes] = refs[s][t]

    return pl.pallas_call(
        body,
        grid_spec=pltpu.PrefetchScalarGridSpec(
            num_scalar_prefetch=1,
            grid=(1,),
            in_specs=[pl.BlockSpec((3, rows, width), lambda i, p: (0, 0, 0))] * n,
            out_specs=[pl.BlockSpec((rows, n * width), lambda i, p: (0, 0))] * 3,
        ),
        out_shape=[jax.ShapeDtypeStruct((rows, n * width), BF16)] * 3,
        compiler_params=params(32),
        cost_estimate=cost(0, 12 * n * rows * width),
        name="assemble_heads",
    )(place, *pieces)


def shift(x, axis, by):
    n = lax.axis_size(axis)
    return lax.ppermute(x, axis, [(i, (i + by) % n) for i in range(n)])


def swap(x, axis, mask):
    n = lax.axis_size(axis)
    return lax.ppermute(x, axis, [(i, i ^ mask) for i in range(n)])


def chip_swap(x, axis, step):
    n = lax.axis_size(axis)
    return lax.ppermute(x, axis, [(i, i ^ (2 if (i + step) % 2 == 0 else 4)) for i in range(n)])


def line_move(x, dp_axis, axis, up):
    n, dp = lax.axis_size(axis), lax.axis_size(dp_axis)
    pairs = []
    for g in range(dp):
        for d in range(n - 1):
            low, high = g * n + d, g * n + d + 1
            pairs.append((low, high) if (g % 2 == 0) == up else (high, low))
    return lax.ppermute(x, (dp_axis, axis), pairs)


def line_payload(place, got, parts, t, n):
    shape = got[0].shape

    def body(place_ref, forward, back, part_f, part_b, out_f, out_b):
        pos = position(place_ref, n)
        for passes, x, part, out in (
            (pos >= t, forward, part_f, out_f),
            (n - 1 - pos >= t, back, part_b, out_b),
        ):

            @pl.when(passes)
            def _():
                out[...] = x[...]

            @pl.when(jnp.logical_not(passes))
            def _():
                out[...] = add_rounded(part[...], x[...])

    block = pl.BlockSpec(shape, lambda i, p: (0, 0))
    return pl.pallas_call(
        body,
        grid_spec=pltpu.PrefetchScalarGridSpec(
            num_scalar_prefetch=1, grid=(1,), in_specs=[block] * 4, out_specs=[block] * 2
        ),
        out_shape=[jax.ShapeDtypeStruct(shape, BF16)] * 2,
        compiler_params=params(8),
        cost_estimate=cost(0, 12 * got[0].size),
        name="line_payload",
    )(place, *got, parts[n - t], parts[t])


def after(x, done):
    return lax.optimization_barrier((x, done))[0]


def by_heads(query, key_in, value, gate_table, timestep, out_weight, grad_out):
    n, dp = lax.axis_size("ctx"), lax.axis_size("dp")
    me = lax.axis_index("ctx").astype(jnp.int32)
    index = lax.axis_index("dp").astype(jnp.int32)
    place = jnp.stack([me, index % 2, index])
    width = query.shape[2] // n
    heads = width // HEAD_DIM
    widths = [heads * HEAD_DIM]

    packed = pack_call(place, query, key_in, value, n, widths)
    pieces = [p[:1] + [shift(p[s], "ctx", s) for s in range(1, n)] for p in packed][0]
    gate_row = lax.dynamic_slice_in_dim(gate_table, timestep[0], 1, 0)

    one = after(chip_swap(after(out_weight, packed), "dp", 0), pieces[1])
    two = chip_swap(jnp.stack([out_weight, one]), "dp", 1)
    shards = after([out_weight, one, two], pieces)
    shards = shards + [swap(x, "dp", 1) for x in shards]
    parts = d_attn_parts_call(place, grad_out[0], gate_row, shards, n)
    attention = attention_call(place, pieces)

    def both_ways(forward, back):
        return line_move(forward, "dp", "ctx", True), line_move(back, "dp", "ctx", False)

    def items(s):
        if s == 0:
            return [(a, a) for a in attention]
        return [(got[g][n - s - 1][0], got[g][s - 1][1]) for g in range(PARTS)]

    got = [[both_ways(a, a)] for a in attention]
    begun = None
    for t in range(1, n):
        sent = [line_payload(place, got[g][-1], parts[g], t, n) for g in range(PARTS)]
        for g in range(PARTS):
            got[g].append(both_ways(*sent[g]))
        if t > 1:
            steps = [s for s in range(n) if max(s, n - s) <= t and max(s, n - s) > t - 1]
            steps = [0] * (t == 2) + steps
            begun = weight_grad_call(
                place, steps, [items(s) for s in steps], grad_out[0], gate_row, n, begun
            )
    keep, send = begun
    received = swap(send, "dp", 1)
    behind = [[got[g][i][0] for i in range(n - 1)] for g in range(PARTS)]
    front = [[got[g][i][1] for i in range(n - 1)] for g in range(PARTS)]
    d_terms = [[parts[g][0] for g in range(PARTS)]]
    d_terms += [[got[g][-1][i] for g in range(PARTS)] for i in range(2)]

    far = add_rounded(keep[2:], received[2:])
    grads = attention_grad_call(place, pieces, attention, after(d_terms, far))
    grads = [grads[0]] + [shift(grads[s], "ctx", -s) for s in range(1, n)]
    far = after(chip_swap(far, "dp", 0), grads[n // 2])
    near = keep[:2].astype(F32) + received[:2].astype(F32) + far.astype(F32)
    grad_weight = near[0] + chip_swap(near[1].astype(BF16), "dp", 1).astype(F32)

    gate_row = after(gate_row, near)
    branch_out = projection_call(place, attention, behind, front, shards, gate_row, n)[None]
    grad_query, grad_key, grad_value = assemble_call(place, after(grads, grad_weight))
    return (branch_out, grad_query[None], grad_key[None], grad_value[None], grad_weight)


def by_tokens(query, key_in, value, gate_table, timestep, out_weight, grad_out):
    slab_rows = query.shape[1]
    attn_width = query.shape[2]
    head_count = attn_width // HEAD_DIM
    score_scale = HEAD_DIM ** (-0.5)
    query_heads = query[0].reshape(slab_rows, head_count, HEAD_DIM)
    keys_whole, values_whole = (
        lax.all_gather(key_in, "ctx", axis=1, tiled=True),
        lax.all_gather(value, "ctx", axis=1, tiled=True),
    )
    keys_all = keys_whole[0]
    values_all = values_whole[0]
    scores = (
        jnp.einsum(
            "qhd,khd->hqk",
            query_heads,
            keys_all.reshape(keys_all.shape[0], head_count, HEAD_DIM),
            preferred_element_type=jnp.float32,
        )
        * score_scale
    )
    length = keys_all.shape[0]
    key_heads = keys_all.reshape(length, head_count, HEAD_DIM)
    value_heads = values_all.reshape(length, head_count, HEAD_DIM)
    row_max = jnp.max(scores, axis=2, keepdims=True)
    exp_scores = jnp.exp(scores - row_max)
    probability = exp_scores / jnp.sum(exp_scores, axis=2, keepdims=True)
    prob_half = probability.astype(jnp.bfloat16)
    attention = jnp.einsum(
        "hqk,khd->qhd", prob_half, value_heads, preferred_element_type=jnp.float32
    )
    attention = attention.reshape(slab_rows, attn_width).astype(jnp.bfloat16)
    marker = (
        timestep[:, None] == jnp.arange(gate_table.shape[0], dtype=jnp.int32)[None, :]
    ).astype(jnp.float32)
    gate_row = jnp.dot(marker, gate_table, precision=lax.Precision.HIGHEST)
    attn_rows = lax.all_gather(attention, "ctx", axis=0, tiled=True)
    columns = attn_rows
    projected = jnp.dot(
        columns,
        lax.all_gather(out_weight, "dp", axis=0, tiled=True),
        preferred_element_type=jnp.float32,
    )
    branch_out = (projected * gate_row).astype(jnp.bfloat16)[None]
    d_proj = (grad_out[0].astype(jnp.float32) * gate_row).astype(jnp.bfloat16)
    partial_rows = jnp.einsum(
        "td,rd->tr",
        d_proj,
        lax.all_gather(out_weight, "dp", axis=0, tiled=True),
        preferred_element_type=jnp.float32,
    )
    d_attn = lax.psum_scatter(
        partial_rows.astype(jnp.bfloat16), "ctx", scatter_dimension=0, tiled=True
    ).astype(jnp.float32)
    d_attn = d_attn.astype(jnp.bfloat16)
    columns = attn_rows
    grad_weight = lax.psum_scatter(
        jnp.einsum("tr,td->rd", columns, d_proj, preferred_element_type=jnp.float32).astype(
            jnp.bfloat16
        ),
        "dp",
        scatter_dimension=0,
        tiled=True,
    ).astype(jnp.float32)
    d_heads = d_attn.reshape(slab_rows, head_count, HEAD_DIM)
    out_heads = attention.reshape(slab_rows, head_count, HEAD_DIM)
    row_delta = jnp.einsum("qhd,qhd->hq", d_heads, out_heads, preferred_element_type=jnp.float32)
    d_scores = jnp.einsum("qhd,khd->hqk", d_heads, value_heads, preferred_element_type=jnp.float32)
    d_half = (probability * (d_scores - row_delta[:, :, None]) * score_scale).astype(jnp.bfloat16)
    grad_query = jnp.einsum("hqk,khd->qhd", d_half, key_heads, preferred_element_type=jnp.float32)
    grad_query = grad_query.reshape(slab_rows, attn_width).astype(jnp.bfloat16)
    key_part = jnp.einsum(
        "hqk,qhd->khd", d_half, query_heads, preferred_element_type=jnp.float32
    ).reshape(slab_rows * lax.axis_size("ctx"), attn_width)
    value_part = jnp.einsum(
        "hqk,qhd->khd", prob_half, d_heads, preferred_element_type=jnp.float32
    ).reshape(slab_rows * lax.axis_size("ctx"), attn_width)
    key_sums = lax.psum_scatter(
        jnp.concatenate([key_part, value_part], axis=1).astype(jnp.bfloat16),
        "ctx",
        scatter_dimension=0,
        tiled=True,
    ).astype(jnp.float32)
    grad_key = key_sums[:, :attn_width].astype(jnp.bfloat16)
    grad_value = key_sums[:, attn_width:].astype(jnp.bfloat16)
    return (branch_out, grad_query[None], grad_key[None], grad_value[None], grad_weight)


def on_device(query, key_in, value, gate_table, timestep, out_weight, grad_out):
    n, dp = lax.axis_size("ctx"), lax.axis_size("dp")
    heads = query.shape[2] // HEAD_DIM
    fits = heads % n == 0 and dp == 8 and dp == 2 * n
    fits = fits and out_weight.shape[0] * dp == query.shape[2]
    plan = by_heads if fits else by_tokens
    return plan(query, key_in, value, gate_table, timestep, out_weight, grad_out)


def solution(mesh):
    in_specs = (
        P("dp", "ctx", None),
        P("dp", "ctx", None),
        P("dp", "ctx", None),
        P(None, "ctx"),
        P("dp"),
        P("dp", "ctx"),
        P("dp", None, "ctx"),
    )
    out_specs = (
        P("dp", None, "ctx"),
        P("dp", "ctx", None),
        P("dp", "ctx", None),
        P("dp", "ctx", None),
        P("dp", "ctx"),
    )
    return jax.shard_map(
        on_device, mesh=mesh, in_specs=in_specs, out_specs=out_specs, check_vma=False
    )
```

```python
import math

import jax
import jax.numpy as jnp
from jax import lax
from jax.experimental import pallas as pl
from jax.experimental.pallas import tpu as pltpu
from jax.sharding import PartitionSpec as P

HEAD_DIM = 128
F32 = jnp.float32
BF16 = jnp.bfloat16
MIB = 1024 * 1024
PARTS = 2


def dot(a, b, dims):
    return lax.dot_general(a, b, (dims, ((), ())), preferred_element_type=F32)


def params(mib=32):
    return pltpu.CompilerParams(
        dimension_semantics=("arbitrary",), vmem_limit_bytes=mib * MIB
    )


def cost(flops, nbytes, exps=0):
    return pl.CostEstimate(flops=flops, bytes_accessed=nbytes, transcendentals=exps)


def any_specs(count):
    return [pl.BlockSpec(memory_space=pl.ANY)] * count


def add_rounded(a, b):
    return (a.astype(F32) + b.astype(F32)).astype(BF16)


def exponentials(q, k):
    scores = dot(k, q, ((1,), (1,)))
    top = jnp.max(scores, axis=0, keepdims=True)
    shifted = jnp.exp2((scores - top) * (HEAD_DIM ** (-0.5) * math.log2(math.e)))
    return shifted, 1.0 / jnp.sum(shifted, axis=0, keepdims=True)


def slab_rows(me, n, rows):
    return [pl.ds(pl.multiple_of(lax.rem(me + n - s, n) * rows, rows), rows) for s in range(n)]


def head_lanes(width):
    return [slice(i, i + HEAD_DIM) for i in range(0, width, HEAD_DIM)]


def pack_call(place, query, key_in, value, n):
    rows, width = query.shape[1], query.shape[2] // n

    def body(place_ref, *refs):
        inputs, outs, (held, sems, out_sems) = refs[:3], refs[3:-3], refs[-3:]
        order = [*range(1, n), 0]
        for s in order:
            first = lax.rem(place_ref[0] + s, n) * width
            lanes = pl.ds(pl.multiple_of(first, HEAD_DIM), width)
            for t in range(3):
                source = inputs[t].at[0, :, lanes]
                pltpu.make_async_copy(source, held.at[s, t], sems.at[s, t]).start()
        for s in order:
            for t in range(3):
                source = inputs[t].at[0, :, pl.ds(0, width)]
                pltpu.make_async_copy(source, held.at[s, t], sems.at[s, t]).wait()
                pltpu.make_async_copy(held.at[s, t], outs[s].at[t], out_sems.at[s, t]).start()
        for s in order:
            for t in range(3):
                pltpu.make_async_copy(held.at[s, t], outs[s].at[t], out_sems.at[s, t]).wait()

    return pl.pallas_call(
        body,
        grid_spec=pltpu.PrefetchScalarGridSpec(
            num_scalar_prefetch=1,
            grid=(1,),
            in_specs=any_specs(3),
            out_specs=any_specs(n),
            scratch_shapes=[
                pltpu.VMEM((n, 3, rows, width), BF16),
                pltpu.SemaphoreType.DMA((n, 3)),
                pltpu.SemaphoreType.DMA((n, 3)),
            ],
        ),
        out_shape=[jax.ShapeDtypeStruct((3, rows, width), BF16)] * n,
        compiler_params=params(60),
        cost_estimate=cost(0, 12 * n * rows * width),
        name="pack_heads",
    )(place, query, key_in, value)


def attention_call(place, pieces):
    n = len(pieces)
    _, rows, width = pieces[0].shape
    length = n * rows
    block = length // PARTS

    def body(place_ref, *refs):
        piece_refs, out_refs, kept_refs, out_ref = refs[:n], refs[n:-4], refs[-4:-1], refs[-1]
        places = slab_rows(place_ref[0], n, rows)
        for t in range(3):
            for s in range(n):
                kept_refs[t][s * rows : (s + 1) * rows] = piece_refs[s][t]
        for lanes in head_lanes(width):
            q, k, v = (r[:, lanes] for r in kept_refs)
            shifted, inverse = exponentials(q, k)
            out = dot(v, shifted.astype(BF16), ((0,), (0,))) * inverse
            out = out.T.astype(BF16)
            for s in range(n):
                out_ref[places[s], lanes] = out[s * rows : (s + 1) * rows]
        for i in range(PARTS):
            out_refs[i][...] = out_ref[i * block : (i + 1) * block]

    def spec(*shape):
        return pl.BlockSpec(shape, lambda i, p: (0,) * len(shape))

    outs = pl.pallas_call(
        body,
        grid_spec=pltpu.PrefetchScalarGridSpec(
            num_scalar_prefetch=1,
            grid=(1,),
            in_specs=[spec(3, rows, width)] * n,
            out_specs=[spec(block, width)] * PARTS + [spec(length, width)] * 3,
            scratch_shapes=[pltpu.VMEM((length, width), BF16)],
        ),
        out_shape=[jax.ShapeDtypeStruct((block, width), BF16)] * PARTS
        + [jax.ShapeDtypeStruct((length, width), BF16)] * 3,
        compiler_params=params(),
        cost_estimate=cost(
            4 * length * length * width, 14 * length * width, length * length * width // HEAD_DIM
        ),
        name="attention_heads",
    )(place, *pieces)
    return list(outs[:PARTS]), list(outs[PARTS:])


def attention_grad_call(place, kept, attention, d_terms, n):
    length, width = kept[0].shape
    rows, block = length // n, length // PARTS
    n_terms = len(d_terms)
    scale = HEAD_DIM ** (-0.5)

    def body(place_ref, *refs):
        kept_refs, attn_refs = refs[:3], refs[3 : 3 + PARTS]
        term_refs = refs[3 + PARTS : 3 + PARTS * (1 + n_terms)]
        out_refs, (attn_held, d_held) = refs[3 + PARTS * (1 + n_terms) : -2], refs[-2:]
        places = slab_rows(place_ref[0], n, rows)
        for i in range(PARTS):
            here = slice(i * block, (i + 1) * block)
            attn_held[here] = attn_refs[i][...]
            terms = [term_refs[t * PARTS + i][...].astype(F32) for t in range(n_terms)]
            d_held[here] = sum(terms).astype(BF16)
        for lanes in head_lanes(width):
            q, k, v = (r[:, lanes] for r in kept_refs)
            attn = jnp.concatenate([attn_held[p, lanes] for p in places], axis=0).astype(F32)
            d_attn = jnp.concatenate([d_held[p, lanes] for p in places], axis=0)
            shifted, inverse = exponentials(q, k)
            prob = shifted * inverse
            delta = jnp.sum(d_attn.astype(F32) * attn, axis=1, keepdims=True).T
            d_prob = dot(v, d_attn, ((1,), (1,)))
            d_half = (prob * (d_prob - delta) * scale).astype(BF16)
            grads = (
                dot(k, d_half, ((0,), (0,))).T,
                dot(d_half, q, ((1,), (0,))),
                dot(prob.astype(BF16), d_attn, ((1,), (0,))),
            )
            for t in range(3):
                g = grads[t].astype(BF16)
                for s in range(n):
                    out_refs[s][t, :, lanes] = g[s * rows : (s + 1) * rows]

    def spec(*shape):
        return pl.BlockSpec(shape, lambda i, p: (0,) * len(shape))

    return pl.pallas_call(
        body,
        grid_spec=pltpu.PrefetchScalarGridSpec(
            num_scalar_prefetch=1,
            grid=(1,),
            in_specs=[spec(length, width)] * 3 + [spec(block, width)] * (PARTS * (1 + n_terms)),
            out_specs=[spec(3, rows, width)] * n,
            scratch_shapes=[pltpu.VMEM((length, width), BF16)] * 2,
        ),
        out_shape=[jax.ShapeDtypeStruct((3, rows, width), BF16)] * n,
        compiler_params=params(),
        cost_estimate=cost(
            200 * length * length * width, 24 * length * width, length * length * width // HEAD_DIM
        ),
        name="attention_heads_grad",
    )(place, *kept, *attention, *sum(d_terms, []))


def ahead(place_ref, s, n):
    me, core = place_ref[0], place_ref[1]
    return lax.rem(jnp.where(core == 0, me + s, me + n - s), n)


def position(place_ref, n):
    return jnp.where(place_ref[1] == 0, place_ref[0], n - 1 - place_ref[0])


def fetch_weight(shard_refs, held, sems, place_ref):
    core, index = place_ref[1], place_ref[2]
    own, one, two, own_o, one_o, two_o = shard_refs
    first, second = jnp.where(core == 0, 2, 4), jnp.where(core == 0, 4, 2)
    places = [
        (own, 0),
        (own_o, 1),
        (one, first),
        (one_o, second + 1),
        (two.at[0], second),
        (two_o.at[0], first + 1),
        (two.at[1], 6),
        (two_o.at[1], 7),
    ]
    for ref, step in places:
        owner = index ^ step
        pltpu.make_async_copy(ref, held.at[owner], sems.at[owner]).start()


def wait_weight(shard_refs, held, sems, first, count):
    for i in range(count):
        pltpu.make_async_copy(shard_refs[0], held.at[first + i], sems.at[first + i]).wait()


def fetch_heads(own, left, right, held, sems, pos, n):
    size = own[0].shape[0]
    for g in range(len(own)):
        rows = pl.ds(g * size, size)
        pltpu.make_async_copy(own[g], held.at[0, rows], sems.at[0, g]).start()
        for s in range(1, n):

            def copy(source, s=s, g=g, rows=rows):
                pltpu.make_async_copy(source, held.at[s, rows], sems.at[s, g]).start()

            @pl.when(pos + s < n)
            def _():
                copy(right[g][s - 1])

            @pl.when(pos + s >= n)
            def _():
                copy(left[g][n - s - 1])


def wait_heads(own, held, sems, s):
    size = own[0].shape[0]
    for g in range(len(own)):
        pltpu.make_async_copy(own[g], held.at[s, pl.ds(g * size, size)], sems.at[s, g]).wait()


def split_heads_refs(refs, groups, n):
    own = refs[:groups]
    rest = refs[groups : groups + 2 * groups * (n - 1)]
    lists = [rest[i * (n - 1) : (i + 1) * (n - 1)] for i in range(2 * groups)]
    return own, lists[:groups], lists[groups:]


def gated(d_ref, gate_ref):
    return (d_ref[...].astype(F32) * gate_ref[...]).astype(BF16)


def d_attn_parts_call(place, grad_out, gate_row, shards, n):
    length, cols = grad_out.shape
    rows, n_shards = shards[0].shape[0], len(shards)
    width = 2 * rows
    dp, per, block = 2 * n, 2, length // PARTS

    def body(place_ref, d_ref, gate_ref, *refs):
        shard_refs, out_refs, (held, sems) = refs[:n_shards], refs[n_shards:-2], refs[-2:]
        fetch_weight(shard_refs, held, sems, place_ref)
        d_proj = gated(d_ref, gate_ref)
        for s in (n - 1, *range(1, n - 1), 0):
            first = ahead(place_ref, s, n) * per
            wait_weight(shard_refs, held, sems, first, per)
            part = dot(d_proj, held[pl.ds(first, per)].reshape(width, cols), ((1,), (1,)))
            for g in range(PARTS):
                out_refs[g * n + s][...] = part[g * block : (g + 1) * block].astype(BF16)

    outs = pl.pallas_call(
        body,
        grid_spec=pltpu.PrefetchScalarGridSpec(
            num_scalar_prefetch=1,
            grid=(1,),
            in_specs=[
                pl.BlockSpec((length, cols), lambda i, p: (0, 0)),
                pl.BlockSpec((1, cols), lambda i, p: (0, 0)),
            ]
            + any_specs(n_shards),
            out_specs=[pl.BlockSpec((block, width), lambda i, p: (0, 0))] * (PARTS * n),
            scratch_shapes=[pltpu.VMEM((dp, rows, cols), BF16), pltpu.SemaphoreType.DMA((dp,))],
        ),
        out_shape=[jax.ShapeDtypeStruct((block, width), BF16)] * (PARTS * n),
        compiler_params=params(),
        cost_estimate=cost(
            2 * length * cols * width * n, 2 * (length * cols + n * width * (cols + length))
        ),
        name="d_attn_parts",
    )(place, grad_out, gate_row, *shards)
    return [outs[g * n : (g + 1) * n] for g in range(PARTS)]


def heads_scratch(n, length, width):
    return [pltpu.VMEM((n, length, width), BF16), pltpu.SemaphoreType.DMA((n, PARTS))]


def projection_call(place, own, behind, front, shards, gate_row, n):
    groups = len(own)
    length, width = groups * own[0].shape[0], own[0].shape[1]
    n_shards, (rows, cols) = len(shards), shards[0].shape
    dp, per, count = n * width // rows, width // rows, groups * (2 * n - 1)

    def body(place_ref, gate_ref, *refs):
        heads = split_heads_refs(refs[:count], groups, n)
        shard_refs = refs[count : count + n_shards]
        out_ref, w_held, w_sems, held, sems = refs[count + n_shards :]
        fetch_heads(*heads, held, sems, position(place_ref, n), n)
        fetch_weight(shard_refs, w_held, w_sems, place_ref)
        total = None
        for s in range(n):
            first = ahead(place_ref, s, n) * per
            wait_heads(heads[0], held, sems, s)
            wait_weight(shard_refs, w_held, w_sems, first, per)
            block = w_held[pl.ds(first, per)].reshape(width, cols)
            term = dot(held[s], block, ((1,), (0,)))
            total = term if s == 0 else total + term
        out_ref[...] = (total * gate_ref[...]).astype(BF16)

    return pl.pallas_call(
        body,
        grid_spec=pltpu.PrefetchScalarGridSpec(
            num_scalar_prefetch=1,
            grid=(1,),
            in_specs=[pl.BlockSpec((1, cols), lambda i, p: (0, 0))] + any_specs(count + n_shards),
            out_specs=pl.BlockSpec((length, cols), lambda i, p: (0, 0)),
            scratch_shapes=[
                pltpu.VMEM((dp, rows, cols), BF16),
                pltpu.SemaphoreType.DMA((dp,)),
                pltpu.VMEM((n, length, width), BF16),
                pltpu.SemaphoreType.DMA((n, groups)),
            ],
        ),
        out_shape=jax.ShapeDtypeStruct((length, cols), BF16),
        compiler_params=params(),
        cost_estimate=cost(
            2 * length * cols * width * n, 2 * (length * cols + n * width * (cols + length))
        ),
        name="projection",
    )(place, gate_row, *own, *sum(behind, []), *sum(front, []), *shards)


def weight_grad_call(place, steps, items, grad_out, gate_row, n, begun=None):
    block, width = items[0][0][0].shape
    length, cols = PARTS * block, grad_out.shape[1]
    rows, many = width // 2, len(steps)

    def body(place_ref, d_ref, gate_ref, *refs):
        keep_ref, send_ref, d_proj, held, sems = refs[-5:]
        i = pl.program_id(0)
        pos = position(place_ref, n)

        @pl.when(i == 0)
        def _():
            for j, s in enumerate(steps):
                for g in range(PARTS):
                    behind, front = refs[2 * (j * PARTS + g) : 2 * (j * PARTS + g) + 2]
                    there = held.at[j, pl.ds(g * block, block)]

                    @pl.when(pos + s < n)
                    def _():
                        pltpu.make_async_copy(front, there, sems.at[j, g]).start()

                    @pl.when(pos + s >= n)
                    def _():
                        pltpu.make_async_copy(behind, there, sems.at[j, g]).start()

            d_proj[...] = gated(d_ref, gate_ref)

        for g in range(PARTS):
            there = held.at[i, pl.ds(g * block, block)]
            pltpu.make_async_copy(refs[0], there, sems.at[i, g]).wait()
        term = dot(held[i], d_proj[...], ((0,), (0,))).astype(BF16)
        first = place_ref[1] == 0
        keep_ref[0] = jnp.where(first, term[:rows], term[rows:])
        send_ref[0] = jnp.where(first, term[rows:], term[:rows])

    def out_spec(other):
        def slot(i, place):
            s = sum(jnp.where(i == j, step, 0) for j, step in enumerate(steps))
            chip = ahead(place, s, n) ^ (place[2] // 2)
            x, y = chip % 2, chip // 2
            return jnp.where((place[1] ^ other) == 0, 2 * x + y, 2 * y + x), 0, 0

        return pl.BlockSpec((1, rows, cols), slot)

    flat = [x for item in items for pair in item for x in pair]
    begun = list(begun or ())
    return pl.pallas_call(
        body,
        grid_spec=pltpu.PrefetchScalarGridSpec(
            num_scalar_prefetch=1,
            grid=(many,),
            in_specs=[
                pl.BlockSpec((length, cols), lambda s, p: (0, 0)),
                pl.BlockSpec((1, cols), lambda s, p: (0, 0)),
            ]
            + any_specs(len(flat) + len(begun)),
            out_specs=[out_spec(0), out_spec(1)],
            scratch_shapes=[
                pltpu.VMEM((length, cols), BF16),
                pltpu.VMEM((many, length, width), BF16),
                pltpu.SemaphoreType.DMA((many, PARTS)),
            ],
        ),
        out_shape=[jax.ShapeDtypeStruct((n, rows, cols), BF16)] * 2,
        input_output_aliases={3 + len(flat) + i: i for i in range(len(begun))},
        compiler_params=params(),
        cost_estimate=cost(
            2 * length * cols * width * many,
            2 * (length * cols + many * width * (cols + 2 * length)),
        ),
        name="weight_grad",
    )(place, grad_out, gate_row, *flat, *begun)


def assemble_call(place, pieces):
    n = len(pieces)
    _, rows, width = pieces[0].shape

    def body(place_ref, *refs):
        for t in range(3):
            for s in range(n):
                start = lax.rem(place_ref[0] + s, n) * width
                lanes = pl.ds(pl.multiple_of(start, HEAD_DIM), width)
                refs[n + t][:, lanes] = refs[s][t]

    return pl.pallas_call(
        body,
        grid_spec=pltpu.PrefetchScalarGridSpec(
            num_scalar_prefetch=1,
            grid=(1,),
            in_specs=[pl.BlockSpec((3, rows, width), lambda i, p: (0, 0, 0))] * n,
            out_specs=[pl.BlockSpec((rows, n * width), lambda i, p: (0, 0))] * 3,
        ),
        out_shape=[jax.ShapeDtypeStruct((rows, n * width), BF16)] * 3,
        compiler_params=params(32),
        cost_estimate=cost(0, 12 * n * rows * width),
        name="assemble_heads",
    )(place, *pieces)


def shift(x, axis, by):
    n = lax.axis_size(axis)
    return lax.ppermute(x, axis, [(i, (i + by) % n) for i in range(n)])


def swap(x, axis, mask):
    n = lax.axis_size(axis)
    return lax.ppermute(x, axis, [(i, i ^ mask) for i in range(n)])


def chip_swap(x, axis, step):
    n = lax.axis_size(axis)
    return lax.ppermute(x, axis, [(i, i ^ (2 if (i + step) % 2 == 0 else 4)) for i in range(n)])


def line_move(x, dp_axis, axis, up):
    n, dp = lax.axis_size(axis), lax.axis_size(dp_axis)
    pairs = []
    for g in range(dp):
        for d in range(n - 1):
            low, high = g * n + d, g * n + d + 1
            pairs.append((low, high) if (g % 2 == 0) == up else (high, low))
    return lax.ppermute(x, (dp_axis, axis), pairs)


def line_payload(place, got, parts, t, n):
    shape = got[0].shape

    def body(place_ref, forward, back, part_f, part_b, out_f, out_b):
        pos = position(place_ref, n)
        for passes, x, part, out in (
            (pos >= t, forward, part_f, out_f),
            (n - 1 - pos >= t, back, part_b, out_b),
        ):

            @pl.when(passes)
            def _():
                out[...] = x[...]

            @pl.when(jnp.logical_not(passes))
            def _():
                out[...] = add_rounded(part[...], x[...])

    block = pl.BlockSpec(shape, lambda i, p: (0, 0))
    return pl.pallas_call(
        body,
        grid_spec=pltpu.PrefetchScalarGridSpec(
            num_scalar_prefetch=1, grid=(1,), in_specs=[block] * 4, out_specs=[block] * 2
        ),
        out_shape=[jax.ShapeDtypeStruct(shape, BF16)] * 2,
        compiler_params=params(8),
        cost_estimate=cost(0, 12 * got[0].size),
        name="line_payload",
    )(place, *got, parts[n - t], parts[t])


def after(x, done):
    return lax.optimization_barrier((x, done))[0]


def by_heads(query, key_in, value, gate_table, timestep, out_weight, grad_out):
    n, dp = lax.axis_size("ctx"), lax.axis_size("dp")
    me = lax.axis_index("ctx").astype(jnp.int32)
    index = lax.axis_index("dp").astype(jnp.int32)
    place = jnp.stack([me, index % 2, index])

    packed = pack_call(place, query, key_in, value, n)
    pieces = [packed[0]] + [shift(packed[s], "ctx", s) for s in range(1, n)]
    gate_row = lax.dynamic_slice_in_dim(gate_table, timestep[0], 1, 0)

    one = chip_swap(after(out_weight, packed), "dp", 0)
    two = chip_swap(after(jnp.stack([out_weight, one]), pieces[1]), "dp", 1)
    shards = [out_weight, one, after(two, pieces[2])]
    shards = shards + [swap(x, "dp", 1) for x in shards]
    parts = d_attn_parts_call(place, grad_out[0], gate_row, shards, n)
    attention, kept = attention_call(place, after(pieces, parts))

    def both_ways(forward, back):
        return line_move(forward, "dp", "ctx", True), line_move(back, "dp", "ctx", False)

    def items(s):
        if s == 0:
            return [(a, a) for a in attention]
        return [(got[g][n - s - 1][0], got[g][s - 1][1]) for g in range(PARTS)]

    got = [[both_ways(a, a)] for a in attention]
    begun = None
    for t in range(1, n):
        sent = [line_payload(place, got[g][-1], parts[g], t, n) for g in range(PARTS)]
        for g in range(PARTS):
            got[g].append(both_ways(*sent[g]))
        if t > 1:
            steps = [s for s in range(n) if max(s, n - s) <= t and max(s, n - s) > t - 1]
            steps = [0] * (t == 2) + steps
            begun = weight_grad_call(
                place, steps, [items(s) for s in steps], grad_out[0], gate_row, n, begun
            )
    keep, send = begun
    received = swap(send, "dp", 1)
    behind = [[got[g][i][0] for i in range(n - 1)] for g in range(PARTS)]
    front = [[got[g][i][1] for i in range(n - 1)] for g in range(PARTS)]
    d_terms = [[parts[g][0] for g in range(PARTS)]]
    d_terms += [[got[g][-1][i] for g in range(PARTS)] for i in range(2)]

    grads = attention_grad_call(place, kept, attention, d_terms, n)
    received = after(received, grads)
    far = add_rounded(keep[2:], received[2:])
    grads = [grads[0]] + [shift(grads[s], "ctx", -s) for s in range(1, n)]
    far = after(chip_swap(far, "dp", 0), grads[n // 2])
    near = keep[:2].astype(F32) + received[:2].astype(F32) + far.astype(F32)
    grad_weight = near[0] + chip_swap(near[1].astype(BF16), "dp", 1).astype(F32)

    gate_row = after(gate_row, near)
    branch_out = projection_call(place, attention, behind, front, shards, gate_row, n)[None]
    grad_query, grad_key, grad_value = assemble_call(place, after(grads, grad_weight))
    return (branch_out, grad_query[None], grad_key[None], grad_value[None], grad_weight)


def by_tokens(query, key_in, value, gate_table, timestep, out_weight, grad_out):
    slab_rows = query.shape[1]
    attn_width = query.shape[2]
    head_count = attn_width // HEAD_DIM
    score_scale = HEAD_DIM ** (-0.5)
    query_heads = query[0].reshape(slab_rows, head_count, HEAD_DIM)
    keys_whole, values_whole = (
        lax.all_gather(key_in, "ctx", axis=1, tiled=True),
        lax.all_gather(value, "ctx", axis=1, tiled=True),
    )
    keys_all = keys_whole[0]
    values_all = values_whole[0]
    scores = (
        jnp.einsum(
            "qhd,khd->hqk",
            query_heads,
            keys_all.reshape(keys_all.shape[0], head_count, HEAD_DIM),
            preferred_element_type=jnp.float32,
        )
        * score_scale
    )
    length = keys_all.shape[0]
    key_heads = keys_all.reshape(length, head_count, HEAD_DIM)
    value_heads = values_all.reshape(length, head_count, HEAD_DIM)
    row_max = jnp.max(scores, axis=2, keepdims=True)
    exp_scores = jnp.exp(scores - row_max)
    probability = exp_scores / jnp.sum(exp_scores, axis=2, keepdims=True)
    prob_half = probability.astype(jnp.bfloat16)
    attention = jnp.einsum(
        "hqk,khd->qhd", prob_half, value_heads, preferred_element_type=jnp.float32
    )
    attention = attention.reshape(slab_rows, attn_width).astype(jnp.bfloat16)
    marker = (
        timestep[:, None] == jnp.arange(gate_table.shape[0], dtype=jnp.int32)[None, :]
    ).astype(jnp.float32)
    gate_row = jnp.dot(marker, gate_table, precision=lax.Precision.HIGHEST)
    attn_rows = lax.all_gather(attention, "ctx", axis=0, tiled=True)
    columns = attn_rows
    projected = jnp.dot(
        columns,
        lax.all_gather(out_weight, "dp", axis=0, tiled=True),
        preferred_element_type=jnp.float32,
    )
    branch_out = (projected * gate_row).astype(jnp.bfloat16)[None]
    d_proj = (grad_out[0].astype(jnp.float32) * gate_row).astype(jnp.bfloat16)
    partial_rows = jnp.einsum(
        "td,rd->tr",
        d_proj,
        lax.all_gather(out_weight, "dp", axis=0, tiled=True),
        preferred_element_type=jnp.float32,
    )
    d_attn = lax.psum_scatter(
        partial_rows.astype(jnp.bfloat16), "ctx", scatter_dimension=0, tiled=True
    ).astype(jnp.float32)
    d_attn = d_attn.astype(jnp.bfloat16)
    columns = attn_rows
    grad_weight = lax.psum_scatter(
        jnp.einsum("tr,td->rd", columns, d_proj, preferred_element_type=jnp.float32).astype(
            jnp.bfloat16
        ),
        "dp",
        scatter_dimension=0,
        tiled=True,
    ).astype(jnp.float32)
    d_heads = d_attn.reshape(slab_rows, head_count, HEAD_DIM)
    out_heads = attention.reshape(slab_rows, head_count, HEAD_DIM)
    row_delta = jnp.einsum("qhd,qhd->hq", d_heads, out_heads, preferred_element_type=jnp.float32)
    d_scores = jnp.einsum("qhd,khd->hqk", d_heads, value_heads, preferred_element_type=jnp.float32)
    d_half = (probability * (d_scores - row_delta[:, :, None]) * score_scale).astype(jnp.bfloat16)
    grad_query = jnp.einsum("hqk,khd->qhd", d_half, key_heads, preferred_element_type=jnp.float32)
    grad_query = grad_query.reshape(slab_rows, attn_width).astype(jnp.bfloat16)
    key_part = jnp.einsum(
        "hqk,qhd->khd", d_half, query_heads, preferred_element_type=jnp.float32
    ).reshape(slab_rows * lax.axis_size("ctx"), attn_width)
    value_part = jnp.einsum(
        "hqk,qhd->khd", prob_half, d_heads, preferred_element_type=jnp.float32
    ).reshape(slab_rows * lax.axis_size("ctx"), attn_width)
    key_sums = lax.psum_scatter(
        jnp.concatenate([key_part, value_part], axis=1).astype(jnp.bfloat16),
        "ctx",
        scatter_dimension=0,
        tiled=True,
    ).astype(jnp.float32)
    grad_key = key_sums[:, :attn_width].astype(jnp.bfloat16)
    grad_value = key_sums[:, attn_width:].astype(jnp.bfloat16)
    return (branch_out, grad_query[None], grad_key[None], grad_value[None], grad_weight)


def on_device(query, key_in, value, gate_table, timestep, out_weight, grad_out):
    n, dp = lax.axis_size("ctx"), lax.axis_size("dp")
    heads = query.shape[2] // HEAD_DIM
    fits = heads % n == 0 and dp == 8 and dp == 2 * n
    fits = fits and out_weight.shape[0] * dp == query.shape[2]
    plan = by_heads if fits else by_tokens
    return plan(query, key_in, value, gate_table, timestep, out_weight, grad_out)


def solution(mesh):
    in_specs = (
        P("dp", "ctx", None),
        P("dp", "ctx", None),
        P("dp", "ctx", None),
        P(None, "ctx"),
        P("dp"),
        P("dp", "ctx"),
        P("dp", None, "ctx"),
    )
    out_specs = (
        P("dp", None, "ctx"),
        P("dp", "ctx", None),
        P("dp", "ctx", None),
        P("dp", "ctx", None),
        P("dp", "ctx"),
    )
    return jax.shard_map(
        on_device, mesh=mesh, in_specs=in_specs, out_specs=out_specs, check_vma=False
    )
```

```python
import math

import jax
import jax.numpy as jnp
from jax import lax
from jax.experimental import pallas as pl
from jax.experimental.pallas import tpu as pltpu
from jax.sharding import PartitionSpec as P

HEAD_DIM = 128
F32 = jnp.float32
BF16 = jnp.bfloat16
MIB = 1024 * 1024
PARTS = 2


def dot(a, b, dims):
    return lax.dot_general(a, b, (dims, ((), ())), preferred_element_type=F32)


def params(mib=32):
    return pltpu.CompilerParams(
        dimension_semantics=("arbitrary",), vmem_limit_bytes=mib * MIB
    )


def cost(flops, nbytes, exps=0):
    return pl.CostEstimate(flops=flops, bytes_accessed=nbytes, transcendentals=exps)


def any_specs(count):
    return [pl.BlockSpec(memory_space=pl.ANY)] * count


def add_rounded(a, b):
    return (a.astype(F32) + b.astype(F32)).astype(BF16)


def exponentials(q, k):
    scores = dot(k, q, ((1,), (1,)))
    top = jnp.max(scores, axis=0, keepdims=True)
    shifted = jnp.exp2((scores - top) * (HEAD_DIM ** (-0.5) * math.log2(math.e)))
    return shifted, 1.0 / jnp.sum(shifted, axis=0, keepdims=True)


def slab_rows(me, n, rows):
    return [pl.ds(pl.multiple_of(lax.rem(me + n - s, n) * rows, rows), rows) for s in range(n)]


def head_lanes(width):
    return [slice(i, i + HEAD_DIM) for i in range(0, width, HEAD_DIM)]


def pack_call(query, key_in, value, axis):
    n = lax.axis_size(axis)
    rows, width = query.shape[1], query.shape[2] // n

    def body(*refs):
        me = lax.axis_index(axis)
        inputs, outs, (held, sems, out_sems) = refs[:3], refs[3:-3], refs[-3:]
        order = [*range(1, n), 0]
        for s in order:
            first = lax.rem(me + s, n) * width
            lanes = pl.ds(pl.multiple_of(first, HEAD_DIM), width)
            for t in range(3):
                source = inputs[t].at[0, :, lanes]
                pltpu.make_async_copy(source, held.at[s, t], sems.at[s, t]).start()
        for s in order:
            for t in range(3):
                source = inputs[t].at[0, :, pl.ds(0, width)]
                pltpu.make_async_copy(source, held.at[s, t], sems.at[s, t]).wait()
                pltpu.make_async_copy(held.at[s, t], outs[s].at[t], out_sems.at[s, t]).start()
        for s in order:
            for t in range(3):
                pltpu.make_async_copy(held.at[s, t], outs[s].at[t], out_sems.at[s, t]).wait()

    return pl.pallas_call(
        body,
        in_specs=any_specs(3),
        out_specs=any_specs(n),
        scratch_shapes=[
            pltpu.VMEM((n, 3, rows, width), BF16),
            pltpu.SemaphoreType.DMA((n, 3)),
            pltpu.SemaphoreType.DMA((n, 3)),
        ],
        out_shape=[jax.ShapeDtypeStruct((3, rows, width), BF16)] * n,
        compiler_params=pltpu.CompilerParams(vmem_limit_bytes=60 * MIB),
        cost_estimate=cost(0, 12 * n * rows * width),
        name="pack_heads",
    )(query, key_in, value)


def attention_call(place, inputs, block, n):
    first = len(inputs) == n
    rows, width = inputs[0].shape[-2:] if first else (inputs[0].shape[0] // n, inputs[0].shape[1])
    length = n * rows
    slabs = n // PARTS

    def body(place_ref, *refs):
        in_refs, out_ref = refs[: len(inputs)], refs[len(inputs)]
        kept_refs = refs[len(inputs) + 1 :] if first else in_refs
        if first:
            for t in range(3):
                for s in range(n):
                    kept_refs[t][s * rows : (s + 1) * rows] = in_refs[s][t]
        wanted = [
            pl.ds(pl.multiple_of(lax.rem(place_ref[0] + n - slab, n) * rows, rows), rows)
            for slab in range(block * slabs, (block + 1) * slabs)
        ]
        for lanes in head_lanes(width):
            q = jnp.concatenate([kept_refs[0][w, lanes] for w in wanted], axis=0)
            shifted, inverse = exponentials(q, kept_refs[1][:, lanes])
            out = dot(kept_refs[2][:, lanes], shifted.astype(BF16), ((0,), (0,))) * inverse
            out_ref[:, lanes] = out.T.astype(BF16)

    def spec(*shape):
        return pl.BlockSpec(shape, lambda i, p: (0,) * len(shape))

    def out_of(*shape):
        return jax.ShapeDtypeStruct(shape, BF16)

    kept = [(length, width)] * (3 * first)
    outs = pl.pallas_call(
        body,
        grid_spec=pltpu.PrefetchScalarGridSpec(
            num_scalar_prefetch=1,
            grid=(1,),
            in_specs=[spec(*x.shape) for x in inputs],
            out_specs=[spec(length // PARTS, width)] + [spec(*k) for k in kept],
        ),
        out_shape=[out_of(length // PARTS, width)] + [out_of(*k) for k in kept],
        compiler_params=params(),
        cost_estimate=cost(
            4 * length * length * width // PARTS,
            10 * length * width,
            length * length * width // HEAD_DIM // PARTS,
        ),
        name="attention_heads",
    )(place, *inputs)
    return outs[0], list(outs[1:])


def attention_grad_call(place, kept, attention, parts, d_terms, n):
    length, width = kept[0].shape
    rows, block = length // n, length // PARTS
    n_terms = len(d_terms)
    scale = HEAD_DIM ** (-0.5)

    def body(place_ref, *refs):
        kept_refs, attn_refs = refs[:3], refs[3 : 3 + PARTS]
        part_ref, term_refs = refs[3 + PARTS], refs[4 + PARTS : 4 + PARTS * (1 + n_terms)]
        out_refs, (attn_held, d_held) = refs[4 + PARTS * (1 + n_terms) : -2], refs[-2:]
        places = slab_rows(place_ref[0], n, rows)
        for i in range(PARTS):
            here = slice(i * block, (i + 1) * block)
            attn_held[here] = attn_refs[i][...]
            terms = [term_refs[t * PARTS + i][...].astype(F32) for t in range(n_terms)]
            d_held[here] = sum(terms, part_ref[i, 0].astype(F32)).astype(BF16)
        for lanes in head_lanes(width):
            q, k, v = (r[:, lanes] for r in kept_refs)
            attn = jnp.concatenate([attn_held[p, lanes] for p in places], axis=0).astype(F32)
            d_attn = jnp.concatenate([d_held[p, lanes] for p in places], axis=0)
            shifted, inverse = exponentials(q, k)
            prob = shifted * inverse
            delta = jnp.sum(d_attn.astype(F32) * attn, axis=1, keepdims=True).T
            d_prob = dot(v, d_attn, ((1,), (1,)))
            d_half = (prob * (d_prob - delta) * scale).astype(BF16)
            grads = (
                dot(k, d_half, ((0,), (0,))).T,
                dot(d_half, q, ((1,), (0,))),
                dot(prob.astype(BF16), d_attn, ((1,), (0,))),
            )
            for t in range(3):
                g = grads[t].astype(BF16)
                for s in range(n):
                    out_refs[s][t, :, lanes] = g[s * rows : (s + 1) * rows]

    def spec(*shape):
        return pl.BlockSpec(shape, lambda i, p: (0,) * len(shape))

    return pl.pallas_call(
        body,
        grid_spec=pltpu.PrefetchScalarGridSpec(
            num_scalar_prefetch=1,
            grid=(1,),
            in_specs=[spec(length, width)] * 3
            + [spec(block, width)] * PARTS
            + [spec(PARTS, 1, block, width)]
            + [spec(block, width)] * (PARTS * n_terms),
            out_specs=[spec(3, rows, width)] * n,
            scratch_shapes=[pltpu.VMEM((length, width), BF16)] * 2,
        ),
        out_shape=[jax.ShapeDtypeStruct((3, rows, width), BF16)] * n,
        compiler_params=params(),
        cost_estimate=cost(
            200 * length * length * width, 24 * length * width, length * length * width // HEAD_DIM
        ),
        name="attention_heads_grad",
    )(place, *kept, *attention, parts, *sum(d_terms, []))


def ahead(place_ref, s, n):
    me, core = place_ref[0], place_ref[1]
    return lax.rem(jnp.where(core == 0, me + s, me + n - s), n)


def position(place_ref, n):
    return jnp.where(place_ref[1] == 0, place_ref[0], n - 1 - place_ref[0])


def weight_steps(place_ref, shard_refs, held, sems, n):
    core, index = place_ref[1], place_ref[2]
    own, one, two, own_o, one_o, two_o = shard_refs
    first, second = jnp.where(core == 0, 1, 2), jnp.where(core == 0, 2, 1)
    pairs = [
        (own, own_o, 0),
        (one, two_o.at[0], first),
        (two.at[0], one_o, second),
        (two.at[1], two_o.at[1], 3),
    ]

    def copies(i):
        mine, other, _ = pairs[i]
        return [
            pltpu.make_async_copy(mine, held.at[i, core], sems.at[i, 0]),
            pltpu.make_async_copy(other, held.at[i, 1 - core], sems.at[i, 1]),
        ]

    for i in range(2):
        for c in copies(i):
            c.start()
    for i in range(n):
        for c in copies(i):
            c.wait()
        if i + 2 < n:
            for c in copies(i + 2):
                c.start()
        chip = (index // 2) ^ pairs[i][2]
        me = place_ref[0]
        yield i, lax.rem(jnp.where(core == 0, chip + n - me, me + n - chip), n)


def weight_scratch(n, rows, cols):
    return [pltpu.VMEM((n, 2, rows, cols), BF16), pltpu.SemaphoreType.DMA((n, 2))]


def fetch_heads(own, left, right, held, sems, pos, n):
    size = own[0].shape[0]
    for g in range(len(own)):
        rows = pl.ds(g * size, size)
        pltpu.make_async_copy(own[g], held.at[0, rows], sems.at[0, g]).start()
        for s in range(1, n):

            def copy(source, s=s, g=g, rows=rows):
                pltpu.make_async_copy(source, held.at[s, rows], sems.at[s, g]).start()

            @pl.when(pos + s < n)
            def _():
                copy(right[g][s - 1])

            @pl.when(pos + s >= n)
            def _():
                copy(left[g][n - s - 1])


def wait_heads(own, held, sems, s):
    size = own[0].shape[0]
    for g in range(len(own)):
        pltpu.make_async_copy(own[g], held.at[s, pl.ds(g * size, size)], sems.at[s, g]).wait()


def split_heads_refs(refs, groups, n):
    own = refs[:groups]
    rest = refs[groups : groups + 2 * groups * (n - 1)]
    lists = [rest[i * (n - 1) : (i + 1) * (n - 1)] for i in range(2 * groups)]
    return own, lists[:groups], lists[groups:]


def d_attn_parts_call(place, d_proj, shards, n):
    length, cols = d_proj.shape
    rows, n_shards = shards[0].shape[0], len(shards)
    width, block = 2 * rows, length // PARTS

    def body(place_ref, d_ref, *refs):
        shard_refs, (out_ref, held, sems, ready, out_sems) = refs[:n_shards], refs[n_shards:]
        copies = []
        for i, s in weight_steps(place_ref, shard_refs, held, sems, n):
            rows_here = held[i].reshape(width, cols)
            for j in range(0, width, 256):
                part = dot(d_ref[...], rows_here[j : j + 256], ((1,), (1,)))
                ready[i, :, j : min(j + 256, width)] = part.astype(BF16)
            for g in range(PARTS):
                source = ready.at[i, pl.ds(g * block, block)]
                copies.append(pltpu.make_async_copy(source, out_ref.at[g, s], out_sems.at[i, g]))
                copies[-1].start()
        for c in copies:
            c.wait()

    return pl.pallas_call(
        body,
        grid_spec=pltpu.PrefetchScalarGridSpec(
            num_scalar_prefetch=1,
            grid=(1,),
            in_specs=[pl.BlockSpec((length, cols), lambda i, p: (0, 0))] + any_specs(n_shards),
            out_specs=pl.BlockSpec(memory_space=pl.ANY),
            scratch_shapes=weight_scratch(n, rows, cols)
            + [
                pltpu.VMEM((n, length, width), BF16),
                pltpu.SemaphoreType.DMA((n, PARTS)),
            ],
        ),
        out_shape=jax.ShapeDtypeStruct((PARTS, n, block, width), BF16),
        compiler_params=params(),
        cost_estimate=cost(
            2 * length * cols * width * n, 2 * (length * cols + n * width * (cols + length))
        ),
        name="d_attn_parts",
    )(place, d_proj, *shards)


def projection_call(place, own, behind, front, shards, gate_row, n):
    length, width = PARTS * own[0].shape[0], own[0].shape[1]
    n_shards, (rows, cols) = len(shards), shards[0].shape
    count = PARTS * (2 * n - 1)

    def body(place_ref, gate_ref, *refs):
        heads = split_heads_refs(refs[:count], PARTS, n)
        shard_refs = refs[count : count + n_shards]
        out_ref, w_held, w_sems, held, sems = refs[count + n_shards :]
        fetch_heads(*heads, held, sems, position(place_ref, n), n)
        total = None
        for i, s in weight_steps(place_ref, shard_refs, w_held, w_sems, n):
            if i == 0:
                for j in range(n):
                    wait_heads(heads[0], held, sems, j)
            term = dot(held[s], w_held[i].reshape(width, cols), ((1,), (0,)))
            total = term if i == 0 else total + term
        out_ref[...] = (total * gate_ref[...]).astype(BF16)

    return pl.pallas_call(
        body,
        grid_spec=pltpu.PrefetchScalarGridSpec(
            num_scalar_prefetch=1,
            grid=(1,),
            in_specs=[pl.BlockSpec((1, cols), lambda i, p: (0, 0))] + any_specs(count + n_shards),
            out_specs=pl.BlockSpec((length, cols), lambda i, p: (0, 0)),
            scratch_shapes=weight_scratch(n, rows, cols)
            + [
                pltpu.VMEM((n, length, width), BF16),
                pltpu.SemaphoreType.DMA((n, PARTS)),
            ],
        ),
        out_shape=jax.ShapeDtypeStruct((length, cols), BF16),
        compiler_params=params(),
        cost_estimate=cost(
            2 * length * cols * width * n, 2 * (length * cols + n * width * (cols + length))
        ),
        name="projection",
    )(place, gate_row, *own, *sum(behind, []), *sum(front, []), *shards)


def weight_grad_call(place, steps, items, d_proj, n):
    block, width = items[0][0][0].shape
    length, cols = PARTS * block, d_proj.shape[1]
    rows, many = width // 2, len(steps)

    def body(place_ref, d_ref, *refs):
        keep_ref, send_ref, held, sems = refs[-4:]
        i = pl.program_id(0)
        pos = position(place_ref, n)

        @pl.when(i == 0)
        def _():
            for j, s in enumerate(steps):
                for g in range(PARTS):
                    behind, front = refs[2 * (j * PARTS + g) : 2 * (j * PARTS + g) + 2]
                    there = held.at[j, pl.ds(g * block, block)]

                    @pl.when(pos + s < n)
                    def _():
                        pltpu.make_async_copy(front, there, sems.at[j, g]).start()

                    @pl.when(pos + s >= n)
                    def _():
                        pltpu.make_async_copy(behind, there, sems.at[j, g]).start()

        for g in range(PARTS):
            there = held.at[i, pl.ds(g * block, block)]
            pltpu.make_async_copy(refs[0], there, sems.at[i, g]).wait()
        term = dot(held[i], d_ref[...], ((0,), (0,))).astype(BF16)
        first = place_ref[1] == 0
        keep_ref[0] = jnp.where(first, term[:rows], term[rows:])
        send_ref[0] = jnp.where(first, term[rows:], term[:rows])

    def out_spec(other):
        def slot(i, place):
            s = sum(jnp.where(i == j, step, 0) for j, step in enumerate(steps))
            chip = ahead(place, s, n) ^ (place[2] // 2)
            x, y = chip % 2, chip // 2
            return jnp.where((place[1] ^ other) == 0, 2 * x + y, 2 * y + x), 0, 0

        return pl.BlockSpec((1, rows, cols), slot)

    flat = [x for item in items for pair in item for x in pair]
    return pl.pallas_call(
        body,
        grid_spec=pltpu.PrefetchScalarGridSpec(
            num_scalar_prefetch=1,
            grid=(many,),
            in_specs=[pl.BlockSpec((length, cols), lambda s, p: (0, 0))]
            + any_specs(len(flat)),
            out_specs=[out_spec(0), out_spec(1)],
            scratch_shapes=[
                pltpu.VMEM((many, length, width), BF16),
                pltpu.SemaphoreType.DMA((many, PARTS)),
            ],
        ),
        out_shape=[jax.ShapeDtypeStruct((n, rows, cols), BF16)] * 2,
        compiler_params=params(),
        cost_estimate=cost(
            2 * length * cols * width * many,
            2 * (length * cols + many * width * (cols + 2 * length)),
        ),
        name="weight_grad",
    )(place, d_proj, *flat)


def assemble_call(place, pieces):
    n = len(pieces)
    _, rows, width = pieces[0].shape

    def body(place_ref, *refs):
        outs, sems = refs[n : n + 3], refs[n + 3]
        copies = []
        for s in range(n):
            start = lax.rem(place_ref[0] + s, n) * width
            lanes = pl.ds(pl.multiple_of(start, HEAD_DIM), width)
            for t in range(3):
                copies.append(
                    pltpu.make_async_copy(refs[s].at[t], outs[t].at[:, lanes], sems.at[s, t])
                )
                copies[-1].start()
        for c in copies:
            c.wait()

    return pl.pallas_call(
        body,
        grid_spec=pltpu.PrefetchScalarGridSpec(
            num_scalar_prefetch=1,
            grid=(1,),
            in_specs=[pl.BlockSpec((3, rows, width), lambda i, me: (0, 0, 0))] * n,
            out_specs=any_specs(3),
            scratch_shapes=[pltpu.SemaphoreType.DMA((n, 3))],
        ),
        out_shape=[jax.ShapeDtypeStruct((rows, n * width), BF16)] * 3,
        compiler_params=params(),
        cost_estimate=cost(0, 12 * n * rows * width),
        name="assemble_heads",
    )(place, *pieces)


def shift(x, axis, by):
    n = lax.axis_size(axis)
    return lax.ppermute(x, axis, [(i, (i + by) % n) for i in range(n)])


def swap(x, axis, mask):
    n = lax.axis_size(axis)
    return lax.ppermute(x, axis, [(i, i ^ mask) for i in range(n)])


def chip_swap(x, axis, step):
    n = lax.axis_size(axis)
    return lax.ppermute(x, axis, [(i, i ^ (2 if (i + step) % 2 == 0 else 4)) for i in range(n)])


def line_move(x, dp_axis, axis, up):
    n, dp = lax.axis_size(axis), lax.axis_size(dp_axis)
    pairs = []
    for g in range(dp):
        for d in range(n - 1):
            low, high = g * n + d, g * n + d + 1
            pairs.append((low, high) if (g % 2 == 0) == up else (high, low))
    return lax.ppermute(x, (dp_axis, axis), pairs)


def line_payload(place, got, parts, g, t, n):
    shape = got[0].shape

    def body(place_ref, forward, back, part_f, part_b, out_f, out_b):
        pos = position(place_ref, n)
        for passes, x, part, out in (
            (pos >= t, forward, part_f, out_f),
            (n - 1 - pos >= t, back, part_b, out_b),
        ):

            @pl.when(passes)
            def _():
                out[...] = x[...]

            @pl.when(jnp.logical_not(passes))
            def _():
                out[...] = add_rounded(part[0, 0], x[...])

    block = pl.BlockSpec(shape, lambda i, p: (0, 0))

    def term(s):
        return pl.BlockSpec((1, 1, *shape), lambda i, p: (g, s, 0, 0))

    return pl.pallas_call(
        body,
        grid_spec=pltpu.PrefetchScalarGridSpec(
            num_scalar_prefetch=1,
            grid=(1,),
            in_specs=[block, block, term(n - t), term(t)],
            out_specs=[block] * 2,
        ),
        out_shape=[jax.ShapeDtypeStruct(shape, BF16)] * 2,
        compiler_params=params(8),
        cost_estimate=cost(0, 12 * got[0].size),
        name="line_payload",
    )(place, *got, parts, parts)


def after(x, done):
    return lax.optimization_barrier((x, done))[0]


def by_heads(query, key_in, value, gate_table, timestep, out_weight, grad_out):
    n, dp = lax.axis_size("ctx"), lax.axis_size("dp")
    me = lax.axis_index("ctx").astype(jnp.int32)
    index = lax.axis_index("dp").astype(jnp.int32)
    place = jnp.stack([me, index % 2, index])

    packed = pack_call(query, key_in, value, "ctx")
    pieces = [packed[0]] + [shift(packed[s], "ctx", s) for s in range(1, n)]
    gate_row = lax.dynamic_slice_in_dim(gate_table, timestep[0], 1, 0)

    one = chip_swap(after(out_weight, packed), "dp", 0)
    two = chip_swap(after(jnp.stack([out_weight, one]), pieces[1]), "dp", 1)
    d_proj = (grad_out[0].astype(F32) * gate_row).astype(BF16)
    shards = [out_weight, one, after(two, (pieces[2], d_proj))]
    shards = shards + [swap(x, "dp", 1) for x in shards]
    parts = d_attn_parts_call(place, d_proj, shards, n)
    attended, kept = attention_call(place, after(pieces, parts), 0, n)
    attention = [attended] + [attention_call(place, kept, g, n)[0] for g in range(1, PARTS)]

    def both_ways(forward, back):
        return line_move(forward, "dp", "ctx", True), line_move(back, "dp", "ctx", False)

    def items(s):
        if s == 0:
            return [(a, a) for a in attention]
        return [(got[g][n - s - 1][0], got[g][s - 1][1]) for g in range(PARTS)]

    got = [[both_ways(a, a)] for a in attention]
    for t in range(1, n):
        sent = [line_payload(place, got[g][-1], parts, g, t, n) for g in range(PARTS)]
        for g in range(PARTS):
            got[g].append(both_ways(*sent[g]))
    steps = sorted(range(n), key=lambda s: max(s, n - s) if s else 0)
    keep, send = weight_grad_call(place, steps, [items(s) for s in steps], d_proj, n)
    received = swap(send, "dp", 1)
    behind = [[got[g][i][0] for i in range(n - 1)] for g in range(PARTS)]
    front = [[got[g][i][1] for i in range(n - 1)] for g in range(PARTS)]
    d_terms = [[got[g][-1][i] for g in range(PARTS)] for i in range(2)]

    grads = attention_grad_call(place, kept, attention, parts, d_terms, n)
    received = after(received, grads)
    far = add_rounded(keep[2:], received[2:])
    grads = [grads[0]] + [shift(grads[s], "ctx", -s) for s in range(1, n)]
    far = after(chip_swap(far, "dp", 0), grads[n // 2])
    near = keep[:2].astype(F32) + received[:2].astype(F32) + far.astype(F32)
    grad_weight = near[0] + chip_swap(near[1].astype(BF16), "dp", 1).astype(F32)

    gate_row = after(gate_row, near)
    branch_out = projection_call(place, attention, behind, front, shards, gate_row, n)[None]
    grad_query, grad_key, grad_value = assemble_call(place, after(grads, grad_weight))
    return (branch_out, grad_query[None], grad_key[None], grad_value[None], grad_weight)


def by_tokens(query, key_in, value, gate_table, timestep, out_weight, grad_out):
    slab_rows = query.shape[1]
    attn_width = query.shape[2]
    head_count = attn_width // HEAD_DIM
    score_scale = HEAD_DIM ** (-0.5)
    query_heads = query[0].reshape(slab_rows, head_count, HEAD_DIM)
    keys_whole, values_whole = (
        lax.all_gather(key_in, "ctx", axis=1, tiled=True),
        lax.all_gather(value, "ctx", axis=1, tiled=True),
    )
    keys_all = keys_whole[0]
    values_all = values_whole[0]
    scores = (
        jnp.einsum(
            "qhd,khd->hqk",
            query_heads,
            keys_all.reshape(keys_all.shape[0], head_count, HEAD_DIM),
            preferred_element_type=jnp.float32,
        )
        * score_scale
    )
    length = keys_all.shape[0]
    key_heads = keys_all.reshape(length, head_count, HEAD_DIM)
    value_heads = values_all.reshape(length, head_count, HEAD_DIM)
    row_max = jnp.max(scores, axis=2, keepdims=True)
    exp_scores = jnp.exp(scores - row_max)
    probability = exp_scores / jnp.sum(exp_scores, axis=2, keepdims=True)
    prob_half = probability.astype(jnp.bfloat16)
    attention = jnp.einsum(
        "hqk,khd->qhd", prob_half, value_heads, preferred_element_type=jnp.float32
    )
    attention = attention.reshape(slab_rows, attn_width).astype(jnp.bfloat16)
    marker = (
        timestep[:, None] == jnp.arange(gate_table.shape[0], dtype=jnp.int32)[None, :]
    ).astype(jnp.float32)
    gate_row = jnp.dot(marker, gate_table, precision=lax.Precision.HIGHEST)
    attn_rows = lax.all_gather(attention, "ctx", axis=0, tiled=True)
    columns = attn_rows
    projected = jnp.dot(
        columns,
        lax.all_gather(out_weight, "dp", axis=0, tiled=True),
        preferred_element_type=jnp.float32,
    )
    branch_out = (projected * gate_row).astype(jnp.bfloat16)[None]
    d_proj = (grad_out[0].astype(jnp.float32) * gate_row).astype(jnp.bfloat16)
    partial_rows = jnp.einsum(
        "td,rd->tr",
        d_proj,
        lax.all_gather(out_weight, "dp", axis=0, tiled=True),
        preferred_element_type=jnp.float32,
    )
    d_attn = lax.psum_scatter(
        partial_rows.astype(jnp.bfloat16), "ctx", scatter_dimension=0, tiled=True
    ).astype(jnp.float32)
    d_attn = d_attn.astype(jnp.bfloat16)
    columns = attn_rows
    grad_weight = lax.psum_scatter(
        jnp.einsum("tr,td->rd", columns, d_proj, preferred_element_type=jnp.float32).astype(
            jnp.bfloat16
        ),
        "dp",
        scatter_dimension=0,
        tiled=True,
    ).astype(jnp.float32)
    d_heads = d_attn.reshape(slab_rows, head_count, HEAD_DIM)
    out_heads = attention.reshape(slab_rows, head_count, HEAD_DIM)
    row_delta = jnp.einsum("qhd,qhd->hq", d_heads, out_heads, preferred_element_type=jnp.float32)
    d_scores = jnp.einsum("qhd,khd->hqk", d_heads, value_heads, preferred_element_type=jnp.float32)
    d_half = (probability * (d_scores - row_delta[:, :, None]) * score_scale).astype(jnp.bfloat16)
    grad_query = jnp.einsum("hqk,khd->qhd", d_half, key_heads, preferred_element_type=jnp.float32)
    grad_query = grad_query.reshape(slab_rows, attn_width).astype(jnp.bfloat16)
    key_part = jnp.einsum(
        "hqk,qhd->khd", d_half, query_heads, preferred_element_type=jnp.float32
    ).reshape(slab_rows * lax.axis_size("ctx"), attn_width)
    value_part = jnp.einsum(
        "hqk,qhd->khd", prob_half, d_heads, preferred_element_type=jnp.float32
    ).reshape(slab_rows * lax.axis_size("ctx"), attn_width)
    key_sums = lax.psum_scatter(
        jnp.concatenate([key_part, value_part], axis=1).astype(jnp.bfloat16),
        "ctx",
        scatter_dimension=0,
        tiled=True,
    ).astype(jnp.float32)
    grad_key = key_sums[:, :attn_width].astype(jnp.bfloat16)
    grad_value = key_sums[:, attn_width:].astype(jnp.bfloat16)
    return (branch_out, grad_query[None], grad_key[None], grad_value[None], grad_weight)


def on_device(query, key_in, value, gate_table, timestep, out_weight, grad_out):
    n, dp = lax.axis_size("ctx"), lax.axis_size("dp")
    heads = query.shape[2] // HEAD_DIM
    fits = heads % n == 0 and dp == 8 and dp == 2 * n
    fits = fits and out_weight.shape[0] * dp == query.shape[2]
    plan = by_heads if fits else by_tokens
    return plan(query, key_in, value, gate_table, timestep, out_weight, grad_out)


def solution(mesh):
    in_specs = (
        P("dp", "ctx", None),
        P("dp", "ctx", None),
        P("dp", "ctx", None),
        P(None, "ctx"),
        P("dp"),
        P("dp", "ctx"),
        P("dp", None, "ctx"),
    )
    out_specs = (
        P("dp", None, "ctx"),
        P("dp", "ctx", None),
        P("dp", "ctx", None),
        P("dp", "ctx", None),
        P("dp", "ctx"),
    )
    return jax.shard_map(
        on_device, mesh=mesh, in_specs=in_specs, out_specs=out_specs, check_vma=False
    )
```

```python
import math

import jax
import jax.numpy as jnp
from jax import lax
from jax.experimental import pallas as pl
from jax.experimental.pallas import tpu as pltpu
from jax.sharding import PartitionSpec as P

HEAD_DIM = 128
F32 = jnp.float32
BF16 = jnp.bfloat16
MIB = 1024 * 1024
PARTS = 2
FAR_PARTS = 2


def dot(a, b, dims):
    return lax.dot_general(a, b, (dims, ((), ())), preferred_element_type=F32)


def params(mib=20):
    return pltpu.CompilerParams(
        dimension_semantics=("arbitrary",), vmem_limit_bytes=mib * MIB
    )


def cost(flops, nbytes, exps=0):
    return pl.CostEstimate(flops=flops, bytes_accessed=nbytes, transcendentals=exps)


def any_specs(count):
    return [pl.BlockSpec(memory_space=pl.ANY)] * count


def add_rounded(a, b):
    return (a.astype(F32) + b.astype(F32)).astype(BF16)


def exponentials(q, k):
    scores = dot(k, q, ((1,), (1,)))
    top = jnp.max(scores, axis=0, keepdims=True)
    shifted = jnp.exp2((scores - top) * (HEAD_DIM ** (-0.5) * math.log2(math.e)))
    return shifted, 1.0 / jnp.sum(shifted, axis=0, keepdims=True)


def slab_rows(me, n, rows):
    return [pl.ds(pl.multiple_of(lax.rem(me + n - s, n) * rows, rows), rows) for s in range(n)]


def head_lanes(width):
    return [slice(i, i + HEAD_DIM) for i in range(0, width, HEAD_DIM)]


def pack_call(query, key_in, value, axis):
    n = lax.axis_size(axis)
    rows, width = query.shape[1], query.shape[2] // n

    def body(*refs):
        me = lax.axis_index(axis)
        inputs, outs, (held, sems, out_sems) = refs[:3], refs[3:-3], refs[-3:]
        order = [*range(1, n), 0]
        for s in order:
            first = lax.rem(me + s, n) * width
            lanes = pl.ds(pl.multiple_of(first, HEAD_DIM), width)
            for t in range(3):
                source = inputs[t].at[0, :, lanes]
                pltpu.make_async_copy(source, held.at[s, t], sems.at[s, t]).start()
        for s in order:
            for t in range(3):
                source = inputs[t].at[0, :, pl.ds(0, width)]
                pltpu.make_async_copy(source, held.at[s, t], sems.at[s, t]).wait()
                pltpu.make_async_copy(held.at[s, t], outs[s].at[t], out_sems.at[s, t]).start()
        for s in order:
            for t in range(3):
                pltpu.make_async_copy(held.at[s, t], outs[s].at[t], out_sems.at[s, t]).wait()

    return pl.pallas_call(
        body,
        in_specs=any_specs(3),
        out_specs=any_specs(n),
        scratch_shapes=[
            pltpu.VMEM((n, 3, rows, width), BF16),
            pltpu.SemaphoreType.DMA((n, 3)),
            pltpu.SemaphoreType.DMA((n, 3)),
        ],
        out_shape=[jax.ShapeDtypeStruct((3, rows, width), BF16)] * n,
        compiler_params=pltpu.CompilerParams(vmem_limit_bytes=60 * MIB),
        cost_estimate=cost(0, 12 * n * rows * width),
        name="pack_heads",
    )(query, key_in, value)


def attention_call(place, inputs, block, n):
    first = len(inputs) == n
    rows, width = inputs[0].shape[-2:] if first else (inputs[0].shape[0] // n, inputs[0].shape[1])
    length = n * rows
    slabs = n // PARTS

    def body(place_ref, *refs):
        in_refs, out_ref = refs[: len(inputs)], refs[len(inputs)]
        kept_refs = refs[len(inputs) + 1 :] if first else in_refs
        if first:
            for t in range(3):
                for s in range(n):
                    kept_refs[t][s * rows : (s + 1) * rows] = in_refs[s][t]
        wanted = [
            pl.ds(pl.multiple_of(lax.rem(place_ref[0] + n - slab, n) * rows, rows), rows)
            for slab in range(block * slabs, (block + 1) * slabs)
        ]
        for lanes in head_lanes(width):
            q = jnp.concatenate([kept_refs[0][w, lanes] for w in wanted], axis=0)
            shifted, inverse = exponentials(q, kept_refs[1][:, lanes])
            out = dot(kept_refs[2][:, lanes], shifted.astype(BF16), ((0,), (0,))) * inverse
            out_ref[:, lanes] = out.T.astype(BF16)

    def spec(*shape):
        return pl.BlockSpec(shape, lambda i, p: (0,) * len(shape))

    def out_of(*shape):
        return jax.ShapeDtypeStruct(shape, BF16)

    kept = [(length, width)] * (3 * first)
    outs = pl.pallas_call(
        body,
        grid_spec=pltpu.PrefetchScalarGridSpec(
            num_scalar_prefetch=1,
            grid=(1,),
            in_specs=[spec(*x.shape) for x in inputs],
            out_specs=[spec(length // PARTS, width)] + [spec(*k) for k in kept],
        ),
        out_shape=[out_of(length // PARTS, width)] + [out_of(*k) for k in kept],
        compiler_params=params(),
        cost_estimate=cost(
            4 * length * length * width // PARTS,
            10 * length * width,
            length * length * width // HEAD_DIM // PARTS,
        ),
        name="attention_heads",
    )(place, *inputs)
    return outs[0], list(outs[1:])


def attention_grad_call(place, kept, attention, parts, d_terms, n):
    length, width = kept[0].shape
    rows, block = length // n, length // PARTS
    n_terms = len(d_terms)
    scale = HEAD_DIM ** (-0.5)

    def body(place_ref, *refs):
        kept_refs, attn_refs = refs[:3], refs[3 : 3 + PARTS]
        part_ref, term_refs = refs[3 + PARTS], refs[4 + PARTS : 4 + PARTS * (1 + n_terms)]
        out_refs, (attn_held, d_held) = refs[4 + PARTS * (1 + n_terms) : -2], refs[-2:]
        places = slab_rows(place_ref[0], n, rows)
        for i in range(PARTS):
            here = slice(i * block, (i + 1) * block)
            attn_held[here] = attn_refs[i][...]
            terms = [term_refs[t * PARTS + i][...].astype(F32) for t in range(n_terms)]
            d_held[here] = sum(terms, part_ref[i, 0].astype(F32)).astype(BF16)
        for lanes in head_lanes(width):
            q, k, v = (r[:, lanes] for r in kept_refs)
            attn = jnp.concatenate([attn_held[p, lanes] for p in places], axis=0).astype(F32)
            d_attn = jnp.concatenate([d_held[p, lanes] for p in places], axis=0)
            shifted, inverse = exponentials(q, k)
            prob = shifted * inverse
            delta = jnp.sum(d_attn.astype(F32) * attn, axis=1, keepdims=True).T
            d_prob = dot(v, d_attn, ((1,), (1,)))
            d_half = (prob * (d_prob - delta) * scale).astype(BF16)
            grads = (
                dot(k, d_half, ((0,), (0,))).T,
                dot(d_half, q, ((1,), (0,))),
                dot(prob.astype(BF16), d_attn, ((1,), (0,))),
            )
            for t in range(3):
                g = grads[t].astype(BF16)
                for s in range(n):
                    out_refs[s][t, :, lanes] = g[s * rows : (s + 1) * rows]

    def spec(*shape):
        return pl.BlockSpec(shape, lambda i, p: (0,) * len(shape))

    return pl.pallas_call(
        body,
        grid_spec=pltpu.PrefetchScalarGridSpec(
            num_scalar_prefetch=1,
            grid=(1,),
            in_specs=[spec(length, width)] * 3
            + [spec(block, width)] * PARTS
            + [spec(PARTS, 1, block, width)]
            + [spec(block, width)] * (PARTS * n_terms),
            out_specs=[spec(3, rows, width)] * n,
            scratch_shapes=[pltpu.VMEM((length, width), BF16)] * 2,
        ),
        out_shape=[jax.ShapeDtypeStruct((3, rows, width), BF16)] * n,
        compiler_params=params(),
        cost_estimate=cost(
            200 * length * length * width, 24 * length * width, length * length * width // HEAD_DIM
        ),
        name="attention_heads_grad",
    )(place, *kept, *attention, parts, *sum(d_terms, []))


def ahead(place_ref, s, n):
    me, core = place_ref[0], place_ref[1]
    return lax.rem(jnp.where(core == 0, me + s, me + n - s), n)


def position(place_ref, n):
    return jnp.where(place_ref[1] == 0, place_ref[0], n - 1 - place_ref[0])


def weight_steps(place_ref, shard_refs, held, sems, n):
    core, index = place_ref[1], place_ref[2]
    first, second = jnp.where(core == 0, 1, 2), jnp.where(core == 0, 2, 1)
    mine, (own, one, two), far = shard_refs[:4], shard_refs[4:7], shard_refs[7:]
    chips = [(mine[0], [own]), (mine[1], [two]), (mine[2], [one]), (mine[3], far)]
    steps = (0, first, second, 3)

    def copies(i):
        found = [pltpu.make_async_copy(chips[i][0], held.at[i, core], sems.at[i, 0])]
        start = 0
        for j, ref in enumerate(chips[i][1]):
            there = held.at[i, 1 - core, pl.ds(start, ref.shape[0])]
            start += ref.shape[0]
            found.append(pltpu.make_async_copy(ref, there, sems.at[i, 1 + j]))
        return found

    for i in range(2):
        for c in copies(i):
            c.start()
    for i in range(n):
        for c in copies(i):
            c.wait()
        if i + 2 < n:
            for c in copies(i + 2):
                c.start()
        chip = (index // 2) ^ steps[i]
        me = place_ref[0]
        yield i, lax.rem(jnp.where(core == 0, chip + n - me, me + n - chip), n)


def weight_scratch(n, rows, cols):
    return [pltpu.VMEM((n, 2, rows, cols), BF16), pltpu.SemaphoreType.DMA((n, 1 + FAR_PARTS))]


def fetch_heads(own, left, right, held, sems, pos, n):
    size = own[0].shape[0]
    for g in range(len(own)):
        rows = pl.ds(g * size, size)
        pltpu.make_async_copy(own[g], held.at[0, rows], sems.at[0, g]).start()
        for s in range(1, n):

            def copy(source, s=s, g=g, rows=rows):
                pltpu.make_async_copy(source, held.at[s, rows], sems.at[s, g]).start()

            @pl.when(pos + s < n)
            def _():
                copy(right[g][s - 1])

            @pl.when(pos + s >= n)
            def _():
                copy(left[g][n - s - 1])


def wait_heads(own, held, sems, s):
    size = own[0].shape[0]
    for g in range(len(own)):
        pltpu.make_async_copy(own[g], held.at[s, pl.ds(g * size, size)], sems.at[s, g]).wait()


def split_heads_refs(refs, groups, n):
    own = refs[:groups]
    rest = refs[groups : groups + 2 * groups * (n - 1)]
    lists = [rest[i * (n - 1) : (i + 1) * (n - 1)] for i in range(2 * groups)]
    return own, lists[:groups], lists[groups:]


def d_attn_parts_call(place, d_proj, shards, n):
    length, cols = d_proj.shape
    rows, n_shards = shards[0].shape[0], len(shards)
    width, block = 2 * rows, length // PARTS

    def body(place_ref, d_ref, *refs):
        shard_refs, (out_ref, held, sems, ready, out_sems) = refs[:n_shards], refs[n_shards:]
        copies = []
        for i, s in weight_steps(place_ref, shard_refs, held, sems, n):
            rows_here = held[i].reshape(width, cols)
            for j in range(0, width, 256):
                part = dot(d_ref[...], rows_here[j : j + 256], ((1,), (1,)))
                ready[i, :, j : min(j + 256, width)] = part.astype(BF16)
            for g in range(PARTS):
                source = ready.at[i, pl.ds(g * block, block)]
                copies.append(pltpu.make_async_copy(source, out_ref.at[g, s], out_sems.at[i, g]))
                copies[-1].start()
        for c in copies:
            c.wait()

    return pl.pallas_call(
        body,
        grid_spec=pltpu.PrefetchScalarGridSpec(
            num_scalar_prefetch=1,
            grid=(1,),
            in_specs=[pl.BlockSpec((length, cols), lambda i, p: (0, 0))] + any_specs(n_shards),
            out_specs=pl.BlockSpec(memory_space=pl.ANY),
            scratch_shapes=weight_scratch(n, rows, cols)
            + [
                pltpu.VMEM((n, length, width), BF16),
                pltpu.SemaphoreType.DMA((n, PARTS)),
            ],
        ),
        out_shape=jax.ShapeDtypeStruct((PARTS, n, block, width), BF16),
        compiler_params=params(),
        cost_estimate=cost(0, 0),
        name="d_attn_parts",
    )(place, d_proj, *shards)


def projection_call(place, own, behind, front, shards, gate_row, n):
    length, width = PARTS * own[0].shape[0], own[0].shape[1]
    n_shards, (rows, cols) = len(shards), shards[0].shape
    count = PARTS * (2 * n - 1)

    def body(place_ref, gate_ref, *refs):
        heads = split_heads_refs(refs[:count], PARTS, n)
        shard_refs = refs[count : count + n_shards]
        out_ref, w_held, w_sems, held, sems = refs[count + n_shards :]
        fetch_heads(*heads, held, sems, position(place_ref, n), n)
        total = None
        for i, s in weight_steps(place_ref, shard_refs, w_held, w_sems, n):
            if i == 0:
                for j in range(n):
                    wait_heads(heads[0], held, sems, j)
            term = dot(held[s], w_held[i].reshape(width, cols), ((1,), (0,)))
            total = term if i == 0 else total + term
        out_ref[...] = (total * gate_ref[...]).astype(BF16)

    return pl.pallas_call(
        body,
        grid_spec=pltpu.PrefetchScalarGridSpec(
            num_scalar_prefetch=1,
            grid=(1,),
            in_specs=[pl.BlockSpec((1, cols), lambda i, p: (0, 0))] + any_specs(count + n_shards),
            out_specs=pl.BlockSpec((length, cols), lambda i, p: (0, 0)),
            scratch_shapes=weight_scratch(n, rows, cols)
            + [
                pltpu.VMEM((n, length, width), BF16),
                pltpu.SemaphoreType.DMA((n, PARTS)),
            ],
        ),
        out_shape=jax.ShapeDtypeStruct((length, cols), BF16),
        compiler_params=params(),
        cost_estimate=cost(0, 0),
        name="projection",
    )(place, gate_row, *own, *sum(behind, []), *sum(front, []), *shards)


def weight_grad_call(place, steps, items, d_proj, n):
    block, width = items[0][0][0].shape
    length, cols = PARTS * block, d_proj.shape[1]
    rows, many = width // 2, len(steps)

    def body(place_ref, d_ref, *refs):
        keep_ref, send_ref, held, sems = refs[-4:]
        i = pl.program_id(0)
        pos = position(place_ref, n)

        @pl.when(i == 0)
        def _():
            for j, s in enumerate(steps):
                for g in range(PARTS):
                    behind, front = refs[2 * (j * PARTS + g) : 2 * (j * PARTS + g) + 2]
                    there = held.at[j, pl.ds(g * block, block)]

                    @pl.when(pos + s < n)
                    def _():
                        pltpu.make_async_copy(front, there, sems.at[j, g]).start()

                    @pl.when(pos + s >= n)
                    def _():
                        pltpu.make_async_copy(behind, there, sems.at[j, g]).start()

        for g in range(PARTS):
            there = held.at[i, pl.ds(g * block, block)]
            pltpu.make_async_copy(refs[0], there, sems.at[i, g]).wait()
        term = dot(held[i], d_ref[...], ((0,), (0,))).astype(BF16)
        first = place_ref[1] == 0
        keep_ref[0] = jnp.where(first, term[:rows], term[rows:])
        send_ref[0] = jnp.where(first, term[rows:], term[:rows])

    def out_spec(other):
        def slot(i, place):
            s = sum(jnp.where(i == j, step, 0) for j, step in enumerate(steps))
            chip = ahead(place, s, n) ^ (place[2] // 2)
            x, y = chip % 2, chip // 2
            return jnp.where((place[1] ^ other) == 0, 2 * x + y, 2 * y + x), 0, 0

        return pl.BlockSpec((1, rows, cols), slot)

    flat = [x for item in items for pair in item for x in pair]
    return pl.pallas_call(
        body,
        grid_spec=pltpu.PrefetchScalarGridSpec(
            num_scalar_prefetch=1,
            grid=(many,),
            in_specs=[pl.BlockSpec((length, cols), lambda s, p: (0, 0))]
            + any_specs(len(flat)),
            out_specs=[out_spec(0), out_spec(1)],
            scratch_shapes=[
                pltpu.VMEM((many, length, width), BF16),
                pltpu.SemaphoreType.DMA((many, PARTS)),
            ],
        ),
        out_shape=[jax.ShapeDtypeStruct((n, rows, cols), BF16)] * 2,
        compiler_params=params(),
        cost_estimate=cost(
            2 * length * cols * width * many,
            2 * (length * cols + many * width * (cols + 2 * length)),
        ),
        name="weight_grad",
    )(place, d_proj, *flat)


def assemble_call(place, pieces):
    n = len(pieces)
    _, rows, width = pieces[0].shape

    def body(place_ref, *refs):
        outs, sems = refs[n : n + 3], refs[n + 3]
        copies = []
        for s in range(n):
            start = lax.rem(place_ref[0] + s, n) * width
            lanes = pl.ds(pl.multiple_of(start, HEAD_DIM), width)
            for t in range(3):
                copies.append(
                    pltpu.make_async_copy(refs[s].at[t], outs[t].at[:, lanes], sems.at[s, t])
                )
                copies[-1].start()
        for c in copies:
            c.wait()

    return pl.pallas_call(
        body,
        grid_spec=pltpu.PrefetchScalarGridSpec(
            num_scalar_prefetch=1,
            grid=(1,),
            in_specs=[pl.BlockSpec((3, rows, width), lambda i, me: (0, 0, 0))] * n,
            out_specs=any_specs(3),
            scratch_shapes=[pltpu.SemaphoreType.DMA((n, 3))],
        ),
        out_shape=[jax.ShapeDtypeStruct((rows, n * width), BF16)] * 3,
        compiler_params=params(),
        cost_estimate=cost(0, 48 * n * rows * width),
        name="assemble_heads",
    )(place, *pieces)


def shift(x, axis, by):
    n = lax.axis_size(axis)
    return lax.ppermute(x, axis, [(i, (i + by) % n) for i in range(n)])


def swap(x, axis, mask):
    n = lax.axis_size(axis)
    return lax.ppermute(x, axis, [(i, i ^ mask) for i in range(n)])


def chip_swap(x, axis, step):
    n = lax.axis_size(axis)
    return lax.ppermute(x, axis, [(i, i ^ (2 if (i + step) % 2 == 0 else 4)) for i in range(n)])


def line_move(x, dp_axis, axis, up):
    n, dp = lax.axis_size(axis), lax.axis_size(dp_axis)
    pairs = []
    for g in range(dp):
        for d in range(n - 1):
            low, high = g * n + d, g * n + d + 1
            pairs.append((low, high) if (g % 2 == 0) == up else (high, low))
    return lax.ppermute(x, (dp_axis, axis), pairs)


def line_payload(place, got, parts, g, t, n):
    shape = got[0].shape

    def body(place_ref, forward, back, part_f, part_b, out_f, out_b):
        pos = position(place_ref, n)
        for passes, x, part, out in (
            (pos >= t, forward, part_f, out_f),
            (n - 1 - pos >= t, back, part_b, out_b),
        ):

            @pl.when(passes)
            def _():
                out[...] = x[...]

            @pl.when(jnp.logical_not(passes))
            def _():
                out[...] = add_rounded(part[0, 0], x[...])

    block = pl.BlockSpec(shape, lambda i, p: (0, 0))

    def term(s):
        return pl.BlockSpec((1, 1, *shape), lambda i, p: (g, s, 0, 0))

    return pl.pallas_call(
        body,
        grid_spec=pltpu.PrefetchScalarGridSpec(
            num_scalar_prefetch=1,
            grid=(1,),
            in_specs=[block, block, term(n - t), term(t)],
            out_specs=[block] * 2,
        ),
        out_shape=[jax.ShapeDtypeStruct(shape, BF16)] * 2,
        compiler_params=params(8),
        cost_estimate=cost(0, 12 * got[0].size),
        name="line_payload",
    )(place, *got, parts, parts)


def after(x, done):
    return lax.optimization_barrier((x, done))[0]


def by_heads(query, key_in, value, gate_table, timestep, out_weight, grad_out):
    n, dp = lax.axis_size("ctx"), lax.axis_size("dp")
    me = lax.axis_index("ctx").astype(jnp.int32)
    index = lax.axis_index("dp").astype(jnp.int32)
    place = jnp.stack([me, index % 2, index])

    packed = pack_call(query, key_in, value, "ctx")
    pieces = [packed[0]] + [shift(packed[s], "ctx", s) for s in range(1, n)]
    gate_row = lax.dynamic_slice_in_dim(gate_table, timestep[0], 1, 0)

    mine = after(out_weight, packed)
    own = swap(mine, "dp", 1)
    one = chip_swap(mine, "dp", 0)
    two = chip_swap(after(mine, (one, pieces[1])), "dp", 1)
    far = chip_swap(after(one, pieces[1]), "dp", 1)
    d_proj = (after(grad_out[0], own).astype(F32) * gate_row).astype(BF16)
    shards = [out_weight, one, two, far, own, swap(one, "dp", 1), swap(two, "dp", 1)]
    shards += [swap(x, "dp", 1) for x in jnp.split(after(far, d_proj), FAR_PARTS)]
    parts = d_attn_parts_call(place, d_proj, shards, n)
    attended, kept = attention_call(place, after(pieces, parts), 0, n)
    attention = [attended] + [attention_call(place, kept, g, n)[0] for g in range(1, PARTS)]

    def both_ways(forward, back):
        return line_move(forward, "dp", "ctx", True), line_move(back, "dp", "ctx", False)

    def items(s):
        if s == 0:
            return [(a, a) for a in attention]
        return [(got[g][n - s - 1][0], got[g][s - 1][1]) for g in range(PARTS)]

    got = [[both_ways(a, a)] for a in attention]
    for t in range(1, n):
        sent = [line_payload(place, got[g][-1], parts, g, t, n) for g in range(PARTS)]
        for g in range(PARTS):
            got[g].append(both_ways(*sent[g]))
    steps = sorted(range(n), key=lambda s: max(s, n - s) if s else 0)
    keep, send = weight_grad_call(place, steps, [items(s) for s in steps], d_proj, n)
    received = swap(send, "dp", 1)
    behind = [[got[g][i][0] for i in range(n - 1)] for g in range(PARTS)]
    front = [[got[g][i][1] for i in range(n - 1)] for g in range(PARTS)]
    d_terms = [[got[g][-1][i] for g in range(PARTS)] for i in range(2)]

    grads = attention_grad_call(place, kept, attention, parts, d_terms, n)
    received = after(received, grads)
    far = add_rounded(keep[2:], received[2:])
    grads = [grads[0]] + [shift(grads[s], "ctx", -s) for s in range(1, n)]
    far = chip_swap(far, "dp", 0)
    near = keep[:2].astype(F32) + received[:2].astype(F32) + far.astype(F32)
    halves = jnp.split(near[1].astype(BF16), 2, axis=0)
    last = jnp.concatenate([chip_swap(x, "dp", 1) for x in halves], axis=0)
    grad_weight = near[0] + last.astype(F32)

    gate_row = after(gate_row, near)
    branch_out = projection_call(place, attention, behind, front, shards, gate_row, n)[None]
    grad_query, grad_key, grad_value = assemble_call(place, after(grads, branch_out))
    return (branch_out, grad_query[None], grad_key[None], grad_value[None], grad_weight)


def by_tokens(query, key_in, value, gate_table, timestep, out_weight, grad_out):
    slab_rows = query.shape[1]
    attn_width = query.shape[2]
    head_count = attn_width // HEAD_DIM
    score_scale = HEAD_DIM ** (-0.5)
    query_heads = query[0].reshape(slab_rows, head_count, HEAD_DIM)
    keys_whole, values_whole = (
        lax.all_gather(key_in, "ctx", axis=1, tiled=True),
        lax.all_gather(value, "ctx", axis=1, tiled=True),
    )
    keys_all = keys_whole[0]
    values_all = values_whole[0]
    scores = (
        jnp.einsum(
            "qhd,khd->hqk",
            query_heads,
            keys_all.reshape(keys_all.shape[0], head_count, HEAD_DIM),
            preferred_element_type=jnp.float32,
        )
        * score_scale
    )
    length = keys_all.shape[0]
    key_heads = keys_all.reshape(length, head_count, HEAD_DIM)
    value_heads = values_all.reshape(length, head_count, HEAD_DIM)
    row_max = jnp.max(scores, axis=2, keepdims=True)
    exp_scores = jnp.exp(scores - row_max)
    probability = exp_scores / jnp.sum(exp_scores, axis=2, keepdims=True)
    prob_half = probability.astype(jnp.bfloat16)
    attention = jnp.einsum(
        "hqk,khd->qhd", prob_half, value_heads, preferred_element_type=jnp.float32
    )
    attention = attention.reshape(slab_rows, attn_width).astype(jnp.bfloat16)
    marker = (
        timestep[:, None] == jnp.arange(gate_table.shape[0], dtype=jnp.int32)[None, :]
    ).astype(jnp.float32)
    gate_row = jnp.dot(marker, gate_table, precision=lax.Precision.HIGHEST)
    attn_rows = lax.all_gather(attention, "ctx", axis=0, tiled=True)
    columns = attn_rows
    projected = jnp.dot(
        columns,
        lax.all_gather(out_weight, "dp", axis=0, tiled=True),
        preferred_element_type=jnp.float32,
    )
    branch_out = (projected * gate_row).astype(jnp.bfloat16)[None]
    d_proj = (grad_out[0].astype(jnp.float32) * gate_row).astype(jnp.bfloat16)
    partial_rows = jnp.einsum(
        "td,rd->tr",
        d_proj,
        lax.all_gather(out_weight, "dp", axis=0, tiled=True),
        preferred_element_type=jnp.float32,
    )
    d_attn = lax.psum_scatter(
        partial_rows.astype(jnp.bfloat16), "ctx", scatter_dimension=0, tiled=True
    ).astype(jnp.float32)
    d_attn = d_attn.astype(jnp.bfloat16)
    columns = attn_rows
    grad_weight = lax.psum_scatter(
        jnp.einsum("tr,td->rd", columns, d_proj, preferred_element_type=jnp.float32).astype(
            jnp.bfloat16
        ),
        "dp",
        scatter_dimension=0,
        tiled=True,
    ).astype(jnp.float32)
    d_heads = d_attn.reshape(slab_rows, head_count, HEAD_DIM)
    out_heads = attention.reshape(slab_rows, head_count, HEAD_DIM)
    row_delta = jnp.einsum("qhd,qhd->hq", d_heads, out_heads, preferred_element_type=jnp.float32)
    d_scores = jnp.einsum("qhd,khd->hqk", d_heads, value_heads, preferred_element_type=jnp.float32)
    d_half = (probability * (d_scores - row_delta[:, :, None]) * score_scale).astype(jnp.bfloat16)
    grad_query = jnp.einsum("hqk,khd->qhd", d_half, key_heads, preferred_element_type=jnp.float32)
    grad_query = grad_query.reshape(slab_rows, attn_width).astype(jnp.bfloat16)
    key_part = jnp.einsum(
        "hqk,qhd->khd", d_half, query_heads, preferred_element_type=jnp.float32
    ).reshape(slab_rows * lax.axis_size("ctx"), attn_width)
    value_part = jnp.einsum(
        "hqk,qhd->khd", prob_half, d_heads, preferred_element_type=jnp.float32
    ).reshape(slab_rows * lax.axis_size("ctx"), attn_width)
    key_sums = lax.psum_scatter(
        jnp.concatenate([key_part, value_part], axis=1).astype(jnp.bfloat16),
        "ctx",
        scatter_dimension=0,
        tiled=True,
    ).astype(jnp.float32)
    grad_key = key_sums[:, :attn_width].astype(jnp.bfloat16)
    grad_value = key_sums[:, attn_width:].astype(jnp.bfloat16)
    return (branch_out, grad_query[None], grad_key[None], grad_value[None], grad_weight)


def on_device(query, key_in, value, gate_table, timestep, out_weight, grad_out):
    n, dp = lax.axis_size("ctx"), lax.axis_size("dp")
    heads = query.shape[2] // HEAD_DIM
    fits = heads % n == 0 and dp == 8 and dp == 2 * n
    fits = fits and out_weight.shape[0] * dp == query.shape[2]
    plan = by_heads if fits else by_tokens
    return plan(query, key_in, value, gate_table, timestep, out_weight, grad_out)


def solution(mesh):
    in_specs = (
        P("dp", "ctx", None),
        P("dp", "ctx", None),
        P("dp", "ctx", None),
        P(None, "ctx"),
        P("dp"),
        P("dp", "ctx"),
        P("dp", None, "ctx"),
    )
    out_specs = (
        P("dp", None, "ctx"),
        P("dp", "ctx", None),
        P("dp", "ctx", None),
        P("dp", "ctx", None),
        P("dp", "ctx"),
    )
    return jax.shard_map(
        on_device, mesh=mesh, in_specs=in_specs, out_specs=out_specs, check_vma=False
    )
```

```python
import math

import jax
import jax.numpy as jnp
from jax import lax
from jax.experimental import pallas as pl
from jax.experimental.pallas import tpu as pltpu
from jax.sharding import PartitionSpec as P

HEAD_DIM = 128
F32 = jnp.float32
BF16 = jnp.bfloat16
MIB = 1024 * 1024
PARTS = 2
FAR_PARTS = 2


def dot(a, b, dims):
    return lax.dot_general(a, b, (dims, ((), ())), preferred_element_type=F32)


def params(mib=20):
    return pltpu.CompilerParams(
        dimension_semantics=("arbitrary",), vmem_limit_bytes=mib * MIB
    )


def cost(flops, nbytes, exps=0):
    return pl.CostEstimate(flops=flops, bytes_accessed=nbytes, transcendentals=exps)


def any_specs(count):
    return [pl.BlockSpec(memory_space=pl.ANY)] * count


def add_rounded(a, b):
    return (a.astype(F32) + b.astype(F32)).astype(BF16)


def exponentials(scores):
    top = jnp.max(scores, axis=0, keepdims=True)
    shifted = jnp.exp2((scores - top) * (HEAD_DIM ** (-0.5) * math.log2(math.e)))
    return shifted, 1.0 / jnp.sum(shifted, axis=0, keepdims=True)


def slab_rows(me, n, rows):
    return [pl.ds(pl.multiple_of(lax.rem(me + n - s, n) * rows, rows), rows) for s in range(n)]


def head_lanes(width):
    return [slice(i, i + HEAD_DIM) for i in range(0, width, HEAD_DIM)]


def pack_call(query, key_in, value, axis):
    n = lax.axis_size(axis)
    rows, width = query.shape[1], query.shape[2] // n

    def body(*refs):
        me = lax.axis_index(axis)
        inputs, outs, (held, sems, out_sems) = refs[:3], refs[3:-3], refs[-3:]
        order = [*range(1, n), 0]
        for s in order:
            first = lax.rem(me + s, n) * width
            lanes = pl.ds(pl.multiple_of(first, HEAD_DIM), width)
            for t in range(3):
                source = inputs[t].at[0, :, lanes]
                pltpu.make_async_copy(source, held.at[s, t], sems.at[s, t]).start()
        for s in order:
            for t in range(3):
                source = inputs[t].at[0, :, pl.ds(0, width)]
                pltpu.make_async_copy(source, held.at[s, t], sems.at[s, t]).wait()
                pltpu.make_async_copy(held.at[s, t], outs[s].at[t], out_sems.at[s, t]).start()
        for s in order:
            for t in range(3):
                pltpu.make_async_copy(held.at[s, t], outs[s].at[t], out_sems.at[s, t]).wait()

    return pl.pallas_call(
        body,
        in_specs=any_specs(3),
        out_specs=any_specs(n),
        scratch_shapes=[
            pltpu.VMEM((n, 3, rows, width), BF16),
            pltpu.SemaphoreType.DMA((n, 3)),
            pltpu.SemaphoreType.DMA((n, 3)),
        ],
        out_shape=[jax.ShapeDtypeStruct((3, rows, width), BF16)] * n,
        compiler_params=pltpu.CompilerParams(vmem_limit_bytes=60 * MIB),
        cost_estimate=cost(0, 12 * n * rows * width),
        name="pack_heads",
    )(query, key_in, value)


def attention_call(place, inputs, block, n):
    first = len(inputs) == n
    rows, width = inputs[0].shape[-2:] if first else (inputs[0].shape[0] // n, inputs[0].shape[1])
    length = n * rows
    slabs = n // PARTS

    def body(place_ref, *refs):
        in_refs, out_ref = refs[: len(inputs)], refs[len(inputs)]
        kept_refs = refs[len(inputs) + 1 :] if first else in_refs
        if first:
            for t in range(3):
                for s in range(n):
                    kept_refs[t][s * rows : (s + 1) * rows] = in_refs[s][t]
        wanted = [
            pl.ds(pl.multiple_of(lax.rem(place_ref[0] + n - slab, n) * rows, rows), rows)
            for slab in range(block * slabs, (block + 1) * slabs)
        ]
        def scores_of(lanes):
            q = jnp.concatenate([kept_refs[0][w, lanes] for w in wanted], axis=0)
            return dot(kept_refs[1][:, lanes], q, ((1,), (1,)))

        every = head_lanes(width)
        ready = scores_of(every[0])
        for h, lanes in enumerate(every):
            scores = ready
            if h + 1 < len(every):
                ready = scores_of(every[h + 1])
            shifted, inverse = exponentials(scores)
            out = dot(kept_refs[2][:, lanes], shifted.astype(BF16), ((0,), (0,))) * inverse
            out_ref[:, lanes] = out.T.astype(BF16)

    def spec(*shape):
        return pl.BlockSpec(shape, lambda i, p: (0,) * len(shape))

    def out_of(*shape):
        return jax.ShapeDtypeStruct(shape, BF16)

    kept = [(length, width)] * (3 * first)
    outs = pl.pallas_call(
        body,
        grid_spec=pltpu.PrefetchScalarGridSpec(
            num_scalar_prefetch=1,
            grid=(1,),
            in_specs=[spec(*x.shape) for x in inputs],
            out_specs=[spec(length // PARTS, width)] + [spec(*k) for k in kept],
        ),
        out_shape=[out_of(length // PARTS, width)] + [out_of(*k) for k in kept],
        compiler_params=params(),
        cost_estimate=cost(
            4 * length * length * width // PARTS,
            10 * length * width,
            length * length * width // HEAD_DIM // PARTS,
        ),
        name="attention_heads",
    )(place, *inputs)
    return outs[0], list(outs[1:])


def attention_grad_call(place, kept, attention, parts, d_terms, n):
    length, width = kept[0].shape
    rows, block = length // n, length // PARTS
    n_terms = len(d_terms)
    scale = HEAD_DIM ** (-0.5)

    def body(place_ref, *refs):
        kept_refs, attn_refs = refs[:3], refs[3 : 3 + PARTS]
        part_ref, term_refs = refs[3 + PARTS], refs[4 + PARTS : 4 + PARTS * (1 + n_terms)]
        out_refs, (attn_held, d_held) = refs[4 + PARTS * (1 + n_terms) : -2], refs[-2:]
        places = slab_rows(place_ref[0], n, rows)
        for i in range(PARTS):
            here = slice(i * block, (i + 1) * block)
            attn_held[here] = attn_refs[i][...]
            terms = [term_refs[t * PARTS + i][...].astype(F32) for t in range(n_terms)]
            d_held[here] = sum(terms, part_ref[i, 0].astype(F32)).astype(BF16)
        def scores_of(lanes):
            k = kept_refs[1][:, lanes]
            return dot(k, kept_refs[0][:, lanes], ((1,), (1,)))

        def d_of(lanes):
            d_attn = jnp.concatenate([d_held[p, lanes] for p in places], axis=0)
            return d_attn, dot(kept_refs[2][:, lanes], d_attn, ((1,), (1,)))

        every = head_lanes(width)
        ready = (scores_of(every[0]), d_of(every[0]))
        for h, lanes in enumerate(every):
            scores, (d_attn, d_prob) = ready
            if h + 1 < len(every):
                ready = (scores_of(every[h + 1]), d_of(every[h + 1]))
            q, k, v = (r[:, lanes] for r in kept_refs)
            attn = jnp.concatenate([attn_held[p, lanes] for p in places], axis=0).astype(F32)
            shifted, inverse = exponentials(scores)
            prob = shifted * inverse
            delta = jnp.sum(d_attn.astype(F32) * attn, axis=1, keepdims=True).T
            d_half = (prob * (d_prob - delta) * scale).astype(BF16)
            grads = (
                dot(k, d_half, ((0,), (0,))).T,
                dot(d_half, q, ((1,), (0,))),
                dot(prob.astype(BF16), d_attn, ((1,), (0,))),
            )
            for t in range(3):
                g = grads[t].astype(BF16)
                for s in range(n):
                    out_refs[s][t, :, lanes] = g[s * rows : (s + 1) * rows]

    def spec(*shape):
        return pl.BlockSpec(shape, lambda i, p: (0,) * len(shape))

    return pl.pallas_call(
        body,
        grid_spec=pltpu.PrefetchScalarGridSpec(
            num_scalar_prefetch=1,
            grid=(1,),
            in_specs=[spec(length, width)] * 3
            + [spec(block, width)] * PARTS
            + [spec(PARTS, 1, block, width)]
            + [spec(block, width)] * (PARTS * n_terms),
            out_specs=[spec(3, rows, width)] * n,
            scratch_shapes=[pltpu.VMEM((length, width), BF16)] * 2,
        ),
        out_shape=[jax.ShapeDtypeStruct((3, rows, width), BF16)] * n,
        compiler_params=params(),
        cost_estimate=cost(
            200 * length * length * width, 24 * length * width, length * length * width // HEAD_DIM
        ),
        name="attention_heads_grad",
    )(place, *kept, *attention, parts, *sum(d_terms, []))


def ahead(place_ref, s, n):
    me, core = place_ref[0], place_ref[1]
    return lax.rem(jnp.where(core == 0, me + s, me + n - s), n)


def position(place_ref, n):
    return jnp.where(place_ref[1] == 0, place_ref[0], n - 1 - place_ref[0])


def weight_steps(place_ref, shard_refs, held, sems, n):
    core, index = place_ref[1], place_ref[2]
    first, second = jnp.where(core == 0, 1, 2), jnp.where(core == 0, 2, 1)
    mine, (own, one, two), far = shard_refs[:4], shard_refs[4:7], shard_refs[7:]
    chips = [(mine[0], [own]), (mine[1], [two]), (mine[2], [one]), (mine[3], far)]
    steps = (0, first, second, 3)

    def copies(i):
        found = [pltpu.make_async_copy(chips[i][0], held.at[i, core], sems.at[i, 0])]
        start = 0
        for j, ref in enumerate(chips[i][1]):
            there = held.at[i, 1 - core, pl.ds(start, ref.shape[0])]
            start += ref.shape[0]
            found.append(pltpu.make_async_copy(ref, there, sems.at[i, 1 + j]))
        return found

    for i in range(2):
        for c in copies(i):
            c.start()
    for i in range(n):
        for c in copies(i):
            c.wait()
        if i + 2 < n:
            for c in copies(i + 2):
                c.start()
        chip = (index // 2) ^ steps[i]
        me = place_ref[0]
        yield i, lax.rem(jnp.where(core == 0, chip + n - me, me + n - chip), n)


def weight_scratch(n, rows, cols):
    return [pltpu.VMEM((n, 2, rows, cols), BF16), pltpu.SemaphoreType.DMA((n, 1 + FAR_PARTS))]


def fetch_heads(own, left, right, held, sems, pos, n):
    size = own[0].shape[0]
    for g in range(len(own)):
        rows = pl.ds(g * size, size)
        pltpu.make_async_copy(own[g], held.at[0, rows], sems.at[0, g]).start()
        for s in range(1, n):

            def copy(source, s=s, g=g, rows=rows):
                pltpu.make_async_copy(source, held.at[s, rows], sems.at[s, g]).start()

            @pl.when(pos + s < n)
            def _():
                copy(right[g][s - 1])

            @pl.when(pos + s >= n)
            def _():
                copy(left[g][n - s - 1])


def wait_heads(own, held, sems, s):
    size = own[0].shape[0]
    for g in range(len(own)):
        pltpu.make_async_copy(own[g], held.at[s, pl.ds(g * size, size)], sems.at[s, g]).wait()


def split_heads_refs(refs, groups, n):
    own = refs[:groups]
    rest = refs[groups : groups + 2 * groups * (n - 1)]
    lists = [rest[i * (n - 1) : (i + 1) * (n - 1)] for i in range(2 * groups)]
    return own, lists[:groups], lists[groups:]


def d_attn_parts_call(place, d_proj, shards, n):
    length, cols = d_proj.shape
    rows, n_shards = shards[0].shape[0], len(shards)
    width, block = 2 * rows, length // PARTS

    def body(place_ref, d_ref, *refs):
        shard_refs, (out_ref, held, sems, ready, out_sems) = refs[:n_shards], refs[n_shards:]
        copies = []
        for i, s in weight_steps(place_ref, shard_refs, held, sems, n):
            rows_here = held[i].reshape(width, cols)
            for j in range(0, width, 256):
                part = dot(d_ref[...], rows_here[j : j + 256], ((1,), (1,)))
                ready[i, :, j : min(j + 256, width)] = part.astype(BF16)
            for g in range(PARTS):
                source = ready.at[i, pl.ds(g * block, block)]
                copies.append(pltpu.make_async_copy(source, out_ref.at[g, s], out_sems.at[i, g]))
                copies[-1].start()
        for c in copies:
            c.wait()

    return pl.pallas_call(
        body,
        grid_spec=pltpu.PrefetchScalarGridSpec(
            num_scalar_prefetch=1,
            grid=(1,),
            in_specs=[pl.BlockSpec((length, cols), lambda i, p: (0, 0))] + any_specs(n_shards),
            out_specs=pl.BlockSpec(memory_space=pl.ANY),
            scratch_shapes=weight_scratch(n, rows, cols)
            + [
                pltpu.VMEM((n, length, width), BF16),
                pltpu.SemaphoreType.DMA((n, PARTS)),
            ],
        ),
        out_shape=jax.ShapeDtypeStruct((PARTS, n, block, width), BF16),
        compiler_params=params(),
        cost_estimate=cost(0, 0),
        name="d_attn_parts",
    )(place, d_proj, *shards)


def projection_call(place, own, behind, front, shards, gate_row, n):
    length, width = PARTS * own[0].shape[0], own[0].shape[1]
    n_shards, (rows, cols) = len(shards), shards[0].shape
    count = PARTS * (2 * n - 1)

    def body(place_ref, gate_ref, *refs):
        heads = split_heads_refs(refs[:count], PARTS, n)
        shard_refs = refs[count : count + n_shards]
        out_ref, w_held, w_sems, held, sems = refs[count + n_shards :]
        fetch_heads(*heads, held, sems, position(place_ref, n), n)
        total = None
        for i, s in weight_steps(place_ref, shard_refs, w_held, w_sems, n):
            if i == 0:
                for j in range(n):
                    wait_heads(heads[0], held, sems, j)
            term = dot(held[s], w_held[i].reshape(width, cols), ((1,), (0,)))
            total = term if i == 0 else total + term
        out_ref[...] = (total * gate_ref[...]).astype(BF16)

    return pl.pallas_call(
        body,
        grid_spec=pltpu.PrefetchScalarGridSpec(
            num_scalar_prefetch=1,
            grid=(1,),
            in_specs=[pl.BlockSpec((1, cols), lambda i, p: (0, 0))] + any_specs(count + n_shards),
            out_specs=pl.BlockSpec((length, cols), lambda i, p: (0, 0)),
            scratch_shapes=weight_scratch(n, rows, cols)
            + [
                pltpu.VMEM((n, length, width), BF16),
                pltpu.SemaphoreType.DMA((n, PARTS)),
            ],
        ),
        out_shape=jax.ShapeDtypeStruct((length, cols), BF16),
        compiler_params=params(),
        cost_estimate=cost(0, 0),
        name="projection",
    )(place, gate_row, *own, *sum(behind, []), *sum(front, []), *shards)


def weight_grad_call(place, steps, items, d_proj, n):
    block, width = items[0][0][0].shape
    length, cols = PARTS * block, d_proj.shape[1]
    rows, many = width // 2, len(steps)

    def body(place_ref, d_ref, *refs):
        keep_ref, send_ref, held, sems = refs[-4:]
        i = pl.program_id(0)
        pos = position(place_ref, n)

        @pl.when(i == 0)
        def _():
            for j, s in enumerate(steps):
                for g in range(PARTS):
                    behind, front = refs[2 * (j * PARTS + g) : 2 * (j * PARTS + g) + 2]
                    there = held.at[j, pl.ds(g * block, block)]

                    @pl.when(pos + s < n)
                    def _():
                        pltpu.make_async_copy(front, there, sems.at[j, g]).start()

                    @pl.when(pos + s >= n)
                    def _():
                        pltpu.make_async_copy(behind, there, sems.at[j, g]).start()

        for g in range(PARTS):
            there = held.at[i, pl.ds(g * block, block)]
            pltpu.make_async_copy(refs[0], there, sems.at[i, g]).wait()
        term = dot(held[i], d_ref[...], ((0,), (0,))).astype(BF16)
        first = place_ref[1] == 0
        keep_ref[0] = jnp.where(first, term[:rows], term[rows:])
        send_ref[0] = jnp.where(first, term[rows:], term[:rows])

    def out_spec(other):
        def slot(i, place):
            s = sum(jnp.where(i == j, step, 0) for j, step in enumerate(steps))
            chip = ahead(place, s, n) ^ (place[2] // 2)
            x, y = chip % 2, chip // 2
            return jnp.where((place[1] ^ other) == 0, 2 * x + y, 2 * y + x), 0, 0

        return pl.BlockSpec((1, rows, cols), slot)

    flat = [x for item in items for pair in item for x in pair]
    return pl.pallas_call(
        body,
        grid_spec=pltpu.PrefetchScalarGridSpec(
            num_scalar_prefetch=1,
            grid=(many,),
            in_specs=[pl.BlockSpec((length, cols), lambda s, p: (0, 0))]
            + any_specs(len(flat)),
            out_specs=[out_spec(0), out_spec(1)],
            scratch_shapes=[
                pltpu.VMEM((many, length, width), BF16),
                pltpu.SemaphoreType.DMA((many, PARTS)),
            ],
        ),
        out_shape=[jax.ShapeDtypeStruct((n, rows, cols), BF16)] * 2,
        compiler_params=params(),
        cost_estimate=cost(
            2 * length * cols * width * many,
            2 * (length * cols + many * width * (cols + 2 * length)),
        ),
        name="weight_grad",
    )(place, d_proj, *flat)


def assemble_call(place, pieces):
    n = len(pieces)
    _, rows, width = pieces[0].shape

    def body(place_ref, *refs):
        outs, sems = refs[n : n + 3], refs[n + 3]
        copies = []
        for s in range(n):
            start = lax.rem(place_ref[0] + s, n) * width
            lanes = pl.ds(pl.multiple_of(start, HEAD_DIM), width)
            for t in range(3):
                copies.append(
                    pltpu.make_async_copy(refs[s].at[t], outs[t].at[:, lanes], sems.at[s, t])
                )
                copies[-1].start()
        for c in copies:
            c.wait()

    return pl.pallas_call(
        body,
        grid_spec=pltpu.PrefetchScalarGridSpec(
            num_scalar_prefetch=1,
            grid=(1,),
            in_specs=[pl.BlockSpec((3, rows, width), lambda i, me: (0, 0, 0))] * n,
            out_specs=any_specs(3),
            scratch_shapes=[pltpu.SemaphoreType.DMA((n, 3))],
        ),
        out_shape=[jax.ShapeDtypeStruct((rows, n * width), BF16)] * 3,
        compiler_params=params(),
        cost_estimate=cost(0, 48 * n * rows * width),
        name="assemble_heads",
    )(place, *pieces)


def shift(x, axis, by):
    n = lax.axis_size(axis)
    return lax.ppermute(x, axis, [(i, (i + by) % n) for i in range(n)])


def swap(x, axis, mask):
    n = lax.axis_size(axis)
    return lax.ppermute(x, axis, [(i, i ^ mask) for i in range(n)])


def chip_swap(x, axis, step):
    n = lax.axis_size(axis)
    return lax.ppermute(x, axis, [(i, i ^ (2 if (i + step) % 2 == 0 else 4)) for i in range(n)])


def line_move(x, dp_axis, axis, up):
    n, dp = lax.axis_size(axis), lax.axis_size(dp_axis)
    pairs = []
    for g in range(dp):
        for d in range(n - 1):
            low, high = g * n + d, g * n + d + 1
            pairs.append((low, high) if (g % 2 == 0) == up else (high, low))
    return lax.ppermute(x, (dp_axis, axis), pairs)


def line_payload(place, got, parts, g, t, n):
    shape = got[0].shape

    def body(place_ref, forward, back, part_f, part_b, out_f, out_b):
        pos = position(place_ref, n)
        for passes, x, part, out in (
            (pos >= t, forward, part_f, out_f),
            (n - 1 - pos >= t, back, part_b, out_b),
        ):

            @pl.when(passes)
            def _():
                out[...] = x[...]

            @pl.when(jnp.logical_not(passes))
            def _():
                out[...] = add_rounded(part[0, 0], x[...])

    block = pl.BlockSpec(shape, lambda i, p: (0, 0))

    def term(s):
        return pl.BlockSpec((1, 1, *shape), lambda i, p: (g, s, 0, 0))

    return pl.pallas_call(
        body,
        grid_spec=pltpu.PrefetchScalarGridSpec(
            num_scalar_prefetch=1,
            grid=(1,),
            in_specs=[block, block, term(n - t), term(t)],
            out_specs=[block] * 2,
        ),
        out_shape=[jax.ShapeDtypeStruct(shape, BF16)] * 2,
        compiler_params=params(8),
        cost_estimate=cost(0, 12 * got[0].size),
        name="line_payload",
    )(place, *got, parts, parts)


def after(x, done):
    return lax.optimization_barrier((x, done))[0]


def by_heads(query, key_in, value, gate_table, timestep, out_weight, grad_out):
    n, dp = lax.axis_size("ctx"), lax.axis_size("dp")
    me = lax.axis_index("ctx").astype(jnp.int32)
    index = lax.axis_index("dp").astype(jnp.int32)
    place = jnp.stack([me, index % 2, index])

    packed = pack_call(query, key_in, value, "ctx")
    pieces = [packed[0]] + [shift(packed[s], "ctx", s) for s in range(1, n)]
    gate_row = lax.dynamic_slice_in_dim(gate_table, timestep[0], 1, 0)

    mine = after(out_weight, packed)
    own = swap(mine, "dp", 1)
    one = chip_swap(mine, "dp", 0)
    two = chip_swap(after(mine, (one, pieces[1])), "dp", 1)
    far = chip_swap(after(one, pieces[1]), "dp", 1)
    d_proj = (grad_out[0].astype(F32) * gate_row).astype(BF16)
    shards = [out_weight, one, two, far, own, swap(one, "dp", 1), swap(two, "dp", 1)]
    shards += [swap(x, "dp", 1) for x in jnp.split(after(far, d_proj), FAR_PARTS)]
    parts = d_attn_parts_call(place, d_proj, shards, n)
    attended, kept = attention_call(place, after(pieces, parts), 0, n)
    attention = [attended] + [attention_call(place, kept, g, n)[0] for g in range(1, PARTS)]

    def both_ways(forward, back):
        return line_move(forward, "dp", "ctx", True), line_move(back, "dp", "ctx", False)

    def items(s):
        if s == 0:
            return [(a, a) for a in attention]
        return [(got[g][n - s - 1][0], got[g][s - 1][1]) for g in range(PARTS)]

    got = [[both_ways(a, a)] for a in attention]
    for t in range(1, n):
        sent = [line_payload(place, got[g][-1], parts, g, t, n) for g in range(PARTS)]
        for g in range(PARTS):
            got[g].append(both_ways(*sent[g]))
    steps = sorted(range(n), key=lambda s: max(s, n - s) if s else 0)
    keep, send = weight_grad_call(place, steps, [items(s) for s in steps], d_proj, n)
    received = swap(send, "dp", 1)
    behind = [[got[g][i][0] for i in range(n - 1)] for g in range(PARTS)]
    front = [[got[g][i][1] for i in range(n - 1)] for g in range(PARTS)]
    d_terms = [[got[g][-1][i] for g in range(PARTS)] for i in range(2)]

    grads = attention_grad_call(place, kept, attention, parts, d_terms, n)
    received = after(received, grads)
    far = add_rounded(keep[2:], received[2:])
    grads = [grads[0]] + [shift(grads[s], "ctx", -s) for s in range(1, n)]
    far = chip_swap(far, "dp", 0)
    near = keep[:2].astype(F32) + received[:2].astype(F32) + far.astype(F32)
    halves = jnp.split(near[1].astype(BF16), 2, axis=0)
    last = jnp.concatenate([chip_swap(x, "dp", 1) for x in halves], axis=0)
    grad_weight = near[0] + last.astype(F32)

    gate_row = after(gate_row, near)
    branch_out = projection_call(place, attention, behind, front, shards, gate_row, n)[None]
    grad_query, grad_key, grad_value = assemble_call(place, after(grads, branch_out))
    return (branch_out, grad_query[None], grad_key[None], grad_value[None], grad_weight)


def by_tokens(query, key_in, value, gate_table, timestep, out_weight, grad_out):
    slab_rows = query.shape[1]
    attn_width = query.shape[2]
    head_count = attn_width // HEAD_DIM
    score_scale = HEAD_DIM ** (-0.5)
    query_heads = query[0].reshape(slab_rows, head_count, HEAD_DIM)
    keys_whole, values_whole = (
        lax.all_gather(key_in, "ctx", axis=1, tiled=True),
        lax.all_gather(value, "ctx", axis=1, tiled=True),
    )
    keys_all = keys_whole[0]
    values_all = values_whole[0]
    scores = (
        jnp.einsum(
            "qhd,khd->hqk",
            query_heads,
            keys_all.reshape(keys_all.shape[0], head_count, HEAD_DIM),
            preferred_element_type=jnp.float32,
        )
        * score_scale
    )
    length = keys_all.shape[0]
    key_heads = keys_all.reshape(length, head_count, HEAD_DIM)
    value_heads = values_all.reshape(length, head_count, HEAD_DIM)
    row_max = jnp.max(scores, axis=2, keepdims=True)
    exp_scores = jnp.exp(scores - row_max)
    probability = exp_scores / jnp.sum(exp_scores, axis=2, keepdims=True)
    prob_half = probability.astype(jnp.bfloat16)
    attention = jnp.einsum(
        "hqk,khd->qhd", prob_half, value_heads, preferred_element_type=jnp.float32
    )
    attention = attention.reshape(slab_rows, attn_width).astype(jnp.bfloat16)
    marker = (
        timestep[:, None] == jnp.arange(gate_table.shape[0], dtype=jnp.int32)[None, :]
    ).astype(jnp.float32)
    gate_row = jnp.dot(marker, gate_table, precision=lax.Precision.HIGHEST)
    attn_rows = lax.all_gather(attention, "ctx", axis=0, tiled=True)
    columns = attn_rows
    projected = jnp.dot(
        columns,
        lax.all_gather(out_weight, "dp", axis=0, tiled=True),
        preferred_element_type=jnp.float32,
    )
    branch_out = (projected * gate_row).astype(jnp.bfloat16)[None]
    d_proj = (grad_out[0].astype(jnp.float32) * gate_row).astype(jnp.bfloat16)
    partial_rows = jnp.einsum(
        "td,rd->tr",
        d_proj,
        lax.all_gather(out_weight, "dp", axis=0, tiled=True),
        preferred_element_type=jnp.float32,
    )
    d_attn = lax.psum_scatter(
        partial_rows.astype(jnp.bfloat16), "ctx", scatter_dimension=0, tiled=True
    ).astype(jnp.float32)
    d_attn = d_attn.astype(jnp.bfloat16)
    columns = attn_rows
    grad_weight = lax.psum_scatter(
        jnp.einsum("tr,td->rd", columns, d_proj, preferred_element_type=jnp.float32).astype(
            jnp.bfloat16
        ),
        "dp",
        scatter_dimension=0,
        tiled=True,
    ).astype(jnp.float32)
    d_heads = d_attn.reshape(slab_rows, head_count, HEAD_DIM)
    out_heads = attention.reshape(slab_rows, head_count, HEAD_DIM)
    row_delta = jnp.einsum("qhd,qhd->hq", d_heads, out_heads, preferred_element_type=jnp.float32)
    d_scores = jnp.einsum("qhd,khd->hqk", d_heads, value_heads, preferred_element_type=jnp.float32)
    d_half = (probability * (d_scores - row_delta[:, :, None]) * score_scale).astype(jnp.bfloat16)
    grad_query = jnp.einsum("hqk,khd->qhd", d_half, key_heads, preferred_element_type=jnp.float32)
    grad_query = grad_query.reshape(slab_rows, attn_width).astype(jnp.bfloat16)
    key_part = jnp.einsum(
        "hqk,qhd->khd", d_half, query_heads, preferred_element_type=jnp.float32
    ).reshape(slab_rows * lax.axis_size("ctx"), attn_width)
    value_part = jnp.einsum(
        "hqk,qhd->khd", prob_half, d_heads, preferred_element_type=jnp.float32
    ).reshape(slab_rows * lax.axis_size("ctx"), attn_width)
    key_sums = lax.psum_scatter(
        jnp.concatenate([key_part, value_part], axis=1).astype(jnp.bfloat16),
        "ctx",
        scatter_dimension=0,
        tiled=True,
    ).astype(jnp.float32)
    grad_key = key_sums[:, :attn_width].astype(jnp.bfloat16)
    grad_value = key_sums[:, attn_width:].astype(jnp.bfloat16)
    return (branch_out, grad_query[None], grad_key[None], grad_value[None], grad_weight)


def on_device(query, key_in, value, gate_table, timestep, out_weight, grad_out):
    n, dp = lax.axis_size("ctx"), lax.axis_size("dp")
    heads = query.shape[2] // HEAD_DIM
    fits = heads % n == 0 and dp == 8 and dp == 2 * n
    fits = fits and out_weight.shape[0] * dp == query.shape[2]
    plan = by_heads if fits else by_tokens
    return plan(query, key_in, value, gate_table, timestep, out_weight, grad_out)


def solution(mesh):
    in_specs = (
        P("dp", "ctx", None),
        P("dp", "ctx", None),
        P("dp", "ctx", None),
        P(None, "ctx"),
        P("dp"),
        P("dp", "ctx"),
        P("dp", None, "ctx"),
    )
    out_specs = (
        P("dp", None, "ctx"),
        P("dp", "ctx", None),
        P("dp", "ctx", None),
        P("dp", "ctx", None),
        P("dp", "ctx"),
    )
    return jax.shard_map(
        on_device, mesh=mesh, in_specs=in_specs, out_specs=out_specs, check_vma=False
    )
```

```python
import math

import jax
import jax.numpy as jnp
from jax import lax
from jax.experimental import pallas as pl
from jax.experimental.pallas import tpu as pltpu
from jax.sharding import PartitionSpec as P

HEAD_DIM = 128
F32 = jnp.float32
BF16 = jnp.bfloat16
MIB = 1024 * 1024
PARTS = 2
FAR_PARTS = 2


def dot(a, b, dims):
    return lax.dot_general(a, b, (dims, ((), ())), preferred_element_type=F32)


def params(mib=20):
    return pltpu.CompilerParams(
        dimension_semantics=("arbitrary",), vmem_limit_bytes=mib * MIB
    )


def cost(flops, nbytes, exps=0):
    return pl.CostEstimate(flops=flops, bytes_accessed=nbytes, transcendentals=exps)


def any_specs(count):
    return [pl.BlockSpec(memory_space=pl.ANY)] * count


def add_rounded(a, b):
    return (a.astype(F32) + b.astype(F32)).astype(BF16)


def exponentials(scores):
    top = jnp.max(scores, axis=0, keepdims=True)
    shifted = jnp.exp2((scores - top) * (HEAD_DIM ** (-0.5) * math.log2(math.e)))
    return shifted, 1.0 / jnp.sum(shifted, axis=0, keepdims=True)


def slab_rows(me, n, rows):
    return [pl.ds(pl.multiple_of(lax.rem(me + n - s, n) * rows, rows), rows) for s in range(n)]


def head_lanes(width):
    return [slice(i, i + HEAD_DIM) for i in range(0, width, HEAD_DIM)]


def pack_call(query, key_in, value, axis):
    n = lax.axis_size(axis)
    rows, width = query.shape[1], query.shape[2] // n

    def body(*refs):
        me = lax.axis_index(axis)
        inputs, outs, (held, sems, out_sems) = refs[:3], refs[3:-3], refs[-3:]
        order = [*range(1, n), 0]
        for s in order:
            first = lax.rem(me + s, n) * width
            lanes = pl.ds(pl.multiple_of(first, HEAD_DIM), width)
            for t in range(3):
                source = inputs[t].at[0, :, lanes]
                pltpu.make_async_copy(source, held.at[s, t], sems.at[s, t]).start()
        for s in order:
            for t in range(3):
                source = inputs[t].at[0, :, pl.ds(0, width)]
                pltpu.make_async_copy(source, held.at[s, t], sems.at[s, t]).wait()
                pltpu.make_async_copy(held.at[s, t], outs[s].at[t], out_sems.at[s, t]).start()
        for s in order:
            for t in range(3):
                pltpu.make_async_copy(held.at[s, t], outs[s].at[t], out_sems.at[s, t]).wait()

    return pl.pallas_call(
        body,
        in_specs=any_specs(3),
        out_specs=any_specs(n),
        scratch_shapes=[
            pltpu.VMEM((n, 3, rows, width), BF16),
            pltpu.SemaphoreType.DMA((n, 3)),
            pltpu.SemaphoreType.DMA((n, 3)),
        ],
        out_shape=[jax.ShapeDtypeStruct((3, rows, width), BF16)] * n,
        compiler_params=pltpu.CompilerParams(vmem_limit_bytes=60 * MIB),
        cost_estimate=cost(0, 12 * n * rows * width),
        name="pack_heads",
    )(query, key_in, value)


def attention_call(place, inputs, block, n):
    first = len(inputs) == n
    rows, width = inputs[0].shape[-2:] if first else (inputs[0].shape[0] // n, inputs[0].shape[1])
    length = n * rows
    slabs = n // PARTS

    def body(place_ref, *refs):
        in_refs, (out_ref, exp_ref, inverse_ref) = refs[: len(inputs)], refs[len(inputs) :][:3]
        kept_refs = refs[len(inputs) + 3 :] if first else in_refs
        if first:
            for t in range(3):
                for s in range(n):
                    kept_refs[t][s * rows : (s + 1) * rows] = in_refs[s][t]
        wanted = [
            pl.ds(pl.multiple_of(lax.rem(place_ref[0] + n - slab, n) * rows, rows), rows)
            for slab in range(block * slabs, (block + 1) * slabs)
        ]
        def scores_of(lanes):
            q = jnp.concatenate([kept_refs[0][w, lanes] for w in wanted], axis=0)
            return dot(kept_refs[1][:, lanes], q, ((1,), (1,)))

        every = head_lanes(width)
        ready = scores_of(every[0])
        for h, lanes in enumerate(every):
            scores = ready
            if h + 1 < len(every):
                ready = scores_of(every[h + 1])
            shifted, inverse = exponentials(scores)
            shifted = shifted.astype(BF16)
            exp_ref[h], inverse_ref[h] = shifted, inverse
            out = dot(kept_refs[2][:, lanes], shifted, ((0,), (0,))) * inverse
            out_ref[:, lanes] = out.T.astype(BF16)

    def spec(*shape):
        return pl.BlockSpec(shape, lambda i, p: (0,) * len(shape))

    def out_of(*shape):
        return jax.ShapeDtypeStruct(shape, BF16)

    kept = [(length, width)] * (3 * first)
    heads, cols = width // HEAD_DIM, length // PARTS
    outs = pl.pallas_call(
        body,
        grid_spec=pltpu.PrefetchScalarGridSpec(
            num_scalar_prefetch=1,
            grid=(1,),
            in_specs=[spec(*x.shape) for x in inputs],
            out_specs=[spec(cols, width), spec(heads, length, cols), spec(heads, 1, cols)]
            + [spec(*k) for k in kept],
        ),
        out_shape=[
            out_of(cols, width),
            out_of(heads, length, cols),
            jax.ShapeDtypeStruct((heads, 1, cols), F32),
        ]
        + [out_of(*k) for k in kept],
        compiler_params=params(),
        cost_estimate=cost(
            4 * length * length * width // PARTS,
            10 * length * width,
            length * length * width // HEAD_DIM // PARTS,
        ),
        name="attention_heads",
    )(place, *inputs)
    return outs[0], outs[1:3], list(outs[3:])


def attention_grad_call(place, kept, weights, attention, parts, d_terms, n):
    length, width = kept[0].shape
    rows, block, heads = length // n, length // PARTS, width // HEAD_DIM
    n_terms = len(d_terms)
    scale = HEAD_DIM ** (-0.5)

    def body(place_ref, *refs):
        kept_refs, refs = refs[:3], refs[3:]
        weight_refs, refs = refs[: 2 * PARTS], refs[2 * PARTS :]
        attn_refs, part_ref, refs = refs[:PARTS], refs[PARTS], refs[PARTS + 1 :]
        term_refs, refs = refs[: PARTS * n_terms], refs[PARTS * n_terms :]
        out_refs, (attn_held, d_held, query_grad) = refs[:n], refs[n:]
        me = place_ref[0]
        wanted = slab_rows(me, n, rows)
        for i in range(PARTS):
            here = slice(i * block, (i + 1) * block)
            attn_held[here] = attn_refs[i][...]
            terms = [term_refs[t * PARTS + i][...].astype(F32) for t in range(n_terms)]
            d_held[here] = sum(terms, part_ref[i, 0].astype(F32)).astype(BF16)

        def d_of(lanes):
            return dot(kept_refs[2][:, lanes], d_held[:, lanes], ((1,), (1,)))

        every = head_lanes(width)
        ready = d_of(every[0])
        for h, lanes in enumerate(every):
            d_prob = ready
            if h + 1 < len(every):
                ready = d_of(every[h + 1])
            q = jnp.concatenate([kept_refs[0][w, lanes] for w in wanted], axis=0)
            shifted = jnp.concatenate([r[h] for r in weight_refs[::2]], axis=1).astype(F32)
            inverse = jnp.concatenate([r[h] for r in weight_refs[1::2]], axis=1)
            prob, d_attn = shifted * inverse, d_held[:, lanes]
            attn = attn_held[:, lanes].astype(F32)
            delta = jnp.sum(d_attn.astype(F32) * attn, axis=1, keepdims=True).T
            d_half = (prob * (d_prob - delta) * scale).astype(BF16)
            query_grad[:, lanes] = dot(kept_refs[1][:, lanes], d_half, ((0,), (0,))).T.astype(BF16)
            grads = dot(d_half, q, ((1,), (0,))), dot(prob.astype(BF16), d_attn, ((1,), (0,)))
            for t in range(2):
                g = grads[t].astype(BF16)
                for s in range(n):
                    out_refs[s][1 + t, :, lanes] = g[s * rows : (s + 1) * rows]
        for s in range(n):
            out_refs[s][0] = query_grad[wanted[s], :]

    def spec(*shape):
        return pl.BlockSpec(shape, lambda i, p: (0,) * len(shape))

    return pl.pallas_call(
        body,
        grid_spec=pltpu.PrefetchScalarGridSpec(
            num_scalar_prefetch=1,
            grid=(1,),
            in_specs=[spec(length, width)] * 3
            + [spec(heads, length, block), spec(heads, 1, block)] * PARTS
            + [spec(block, width)] * PARTS
            + [spec(PARTS, 1, block, width)]
            + [spec(block, width)] * (PARTS * n_terms),
            out_specs=[spec(3, rows, width)] * n,
            scratch_shapes=[pltpu.VMEM((length, width), BF16)] * 3,
        ),
        out_shape=[jax.ShapeDtypeStruct((3, rows, width), BF16)] * n,
        compiler_params=params(),
        cost_estimate=cost(
            200 * length * length * width, 24 * length * width, length * length * width // HEAD_DIM
        ),
        name="attention_heads_grad",
    )(place, *kept, *sum(weights, []), *attention, parts, *sum(d_terms, []))


def ahead(place_ref, s, n):
    me, core = place_ref[0], place_ref[1]
    return lax.rem(jnp.where(core == 0, me + s, me + n - s), n)


def position(place_ref, n):
    return jnp.where(place_ref[1] == 0, place_ref[0], n - 1 - place_ref[0])


def weight_steps(place_ref, shard_refs, held, sems, n):
    core, index = place_ref[1], place_ref[2]
    first, second = jnp.where(core == 0, 1, 2), jnp.where(core == 0, 2, 1)
    mine, (own, one, two), far = shard_refs[:4], shard_refs[4:7], shard_refs[7:]
    chips = [(mine[0], [own]), (mine[1], [two]), (mine[2], [one]), (mine[3], far)]
    steps = (0, first, second, 3)

    def copies(i):
        found = [pltpu.make_async_copy(chips[i][0], held.at[i, core], sems.at[i, 0])]
        start = 0
        for j, ref in enumerate(chips[i][1]):
            there = held.at[i, 1 - core, pl.ds(start, ref.shape[0])]
            start += ref.shape[0]
            found.append(pltpu.make_async_copy(ref, there, sems.at[i, 1 + j]))
        return found

    for i in range(2):
        for c in copies(i):
            c.start()
    for i in range(n):
        for c in copies(i):
            c.wait()
        if i + 2 < n:
            for c in copies(i + 2):
                c.start()
        chip = (index // 2) ^ steps[i]
        me = place_ref[0]
        yield i, lax.rem(jnp.where(core == 0, chip + n - me, me + n - chip), n)


def weight_scratch(n, rows, cols):
    return [pltpu.VMEM((n, 2, rows, cols), BF16), pltpu.SemaphoreType.DMA((n, 1 + FAR_PARTS))]


def fetch_heads(own, left, right, held, sems, pos, n):
    size = own[0].shape[0]
    for g in range(len(own)):
        rows = pl.ds(g * size, size)
        pltpu.make_async_copy(own[g], held.at[0, rows], sems.at[0, g]).start()
        for s in range(1, n):

            def copy(source, s=s, g=g, rows=rows):
                pltpu.make_async_copy(source, held.at[s, rows], sems.at[s, g]).start()

            @pl.when(pos + s < n)
            def _():
                copy(right[g][s - 1])

            @pl.when(pos + s >= n)
            def _():
                copy(left[g][n - s - 1])


def wait_heads(own, held, sems, s):
    size = own[0].shape[0]
    for g in range(len(own)):
        pltpu.make_async_copy(own[g], held.at[s, pl.ds(g * size, size)], sems.at[s, g]).wait()


def split_heads_refs(refs, groups, n):
    own = refs[:groups]
    rest = refs[groups : groups + 2 * groups * (n - 1)]
    lists = [rest[i * (n - 1) : (i + 1) * (n - 1)] for i in range(2 * groups)]
    return own, lists[:groups], lists[groups:]


def d_attn_parts_call(place, d_proj, shards, n):
    length, cols = d_proj.shape
    rows, n_shards = shards[0].shape[0], len(shards)
    width, block = 2 * rows, length // PARTS

    def body(place_ref, d_ref, *refs):
        shard_refs, (out_ref, held, sems, ready, out_sems) = refs[:n_shards], refs[n_shards:]
        copies = []
        for i, s in weight_steps(place_ref, shard_refs, held, sems, n):
            rows_here = held[i].reshape(width, cols)
            for j in range(0, width, 256):
                part = dot(d_ref[...], rows_here[j : j + 256], ((1,), (1,)))
                ready[i, :, j : min(j + 256, width)] = part.astype(BF16)
            for g in range(PARTS):
                source = ready.at[i, pl.ds(g * block, block)]
                copies.append(pltpu.make_async_copy(source, out_ref.at[g, s], out_sems.at[i, g]))
                copies[-1].start()
        for c in copies:
            c.wait()

    return pl.pallas_call(
        body,
        grid_spec=pltpu.PrefetchScalarGridSpec(
            num_scalar_prefetch=1,
            grid=(1,),
            in_specs=[pl.BlockSpec((length, cols), lambda i, p: (0, 0))] + any_specs(n_shards),
            out_specs=pl.BlockSpec(memory_space=pl.ANY),
            scratch_shapes=weight_scratch(n, rows, cols)
            + [
                pltpu.VMEM((n, length, width), BF16),
                pltpu.SemaphoreType.DMA((n, PARTS)),
            ],
        ),
        out_shape=jax.ShapeDtypeStruct((PARTS, n, block, width), BF16),
        compiler_params=params(),
        cost_estimate=cost(0, 0),
        name="d_attn_parts",
    )(place, d_proj, *shards)


def projection_call(place, own, behind, front, shards, gate_row, n):
    length, width = PARTS * own[0].shape[0], own[0].shape[1]
    n_shards, (rows, cols) = len(shards), shards[0].shape
    count = PARTS * (2 * n - 1)

    def body(place_ref, gate_ref, *refs):
        heads = split_heads_refs(refs[:count], PARTS, n)
        shard_refs = refs[count : count + n_shards]
        out_ref, w_held, w_sems, held, sems = refs[count + n_shards :]
        fetch_heads(*heads, held, sems, position(place_ref, n), n)
        total = None
        for i, s in weight_steps(place_ref, shard_refs, w_held, w_sems, n):
            if i == 0:
                for j in range(n):
                    wait_heads(heads[0], held, sems, j)
            term = dot(held[s], w_held[i].reshape(width, cols), ((1,), (0,)))
            total = term if i == 0 else total + term
        out_ref[...] = (total * gate_ref[...]).astype(BF16)

    return pl.pallas_call(
        body,
        grid_spec=pltpu.PrefetchScalarGridSpec(
            num_scalar_prefetch=1,
            grid=(1,),
            in_specs=[pl.BlockSpec((1, cols), lambda i, p: (0, 0))] + any_specs(count + n_shards),
            out_specs=pl.BlockSpec((length, cols), lambda i, p: (0, 0)),
            scratch_shapes=weight_scratch(n, rows, cols)
            + [
                pltpu.VMEM((n, length, width), BF16),
                pltpu.SemaphoreType.DMA((n, PARTS)),
            ],
        ),
        out_shape=jax.ShapeDtypeStruct((length, cols), BF16),
        compiler_params=params(),
        cost_estimate=cost(0, 0),
        name="projection",
    )(place, gate_row, *own, *sum(behind, []), *sum(front, []), *shards)


def weight_grad_call(place, steps, items, d_proj, n):
    block, width = items[0][0][0].shape
    length, cols = PARTS * block, d_proj.shape[1]
    rows, many = width // 2, len(steps)

    def body(place_ref, d_ref, *refs):
        keep_ref, send_ref, held, sems = refs[-4:]
        i = pl.program_id(0)
        pos = position(place_ref, n)

        @pl.when(i == 0)
        def _():
            for j, s in enumerate(steps):
                for g in range(PARTS):
                    behind, front = refs[2 * (j * PARTS + g) : 2 * (j * PARTS + g) + 2]
                    there = held.at[j, pl.ds(g * block, block)]

                    @pl.when(pos + s < n)
                    def _():
                        pltpu.make_async_copy(front, there, sems.at[j, g]).start()

                    @pl.when(pos + s >= n)
                    def _():
                        pltpu.make_async_copy(behind, there, sems.at[j, g]).start()

        for g in range(PARTS):
            there = held.at[i, pl.ds(g * block, block)]
            pltpu.make_async_copy(refs[0], there, sems.at[i, g]).wait()
        term = dot(held[i], d_ref[...], ((0,), (0,))).astype(BF16)
        first = place_ref[1] == 0
        keep_ref[0] = jnp.where(first, term[:rows], term[rows:])
        send_ref[0] = jnp.where(first, term[rows:], term[:rows])

    def out_spec(other):
        def slot(i, place):
            s = sum(jnp.where(i == j, step, 0) for j, step in enumerate(steps))
            chip = ahead(place, s, n) ^ (place[2] // 2)
            x, y = chip % 2, chip // 2
            return jnp.where((place[1] ^ other) == 0, 2 * x + y, 2 * y + x), 0, 0

        return pl.BlockSpec((1, rows, cols), slot)

    flat = [x for item in items for pair in item for x in pair]
    return pl.pallas_call(
        body,
        grid_spec=pltpu.PrefetchScalarGridSpec(
            num_scalar_prefetch=1,
            grid=(many,),
            in_specs=[pl.BlockSpec((length, cols), lambda s, p: (0, 0))]
            + any_specs(len(flat)),
            out_specs=[out_spec(0), out_spec(1)],
            scratch_shapes=[
                pltpu.VMEM((many, length, width), BF16),
                pltpu.SemaphoreType.DMA((many, PARTS)),
            ],
        ),
        out_shape=[jax.ShapeDtypeStruct((n, rows, cols), BF16)] * 2,
        compiler_params=params(),
        cost_estimate=cost(
            2 * length * cols * width * many,
            2 * (length * cols + many * width * (cols + 2 * length)),
        ),
        name="weight_grad",
    )(place, d_proj, *flat)


def assemble_call(place, pieces):
    n = len(pieces)
    _, rows, width = pieces[0].shape

    def body(place_ref, *refs):
        outs, sems = refs[n : n + 3], refs[n + 3]
        copies = []
        for s in range(n):
            start = lax.rem(place_ref[0] + s, n) * width
            lanes = pl.ds(pl.multiple_of(start, HEAD_DIM), width)
            for t in range(3):
                copies.append(
                    pltpu.make_async_copy(refs[s].at[t], outs[t].at[:, lanes], sems.at[s, t])
                )
                copies[-1].start()
        for c in copies:
            c.wait()

    return pl.pallas_call(
        body,
        grid_spec=pltpu.PrefetchScalarGridSpec(
            num_scalar_prefetch=1,
            grid=(1,),
            in_specs=[pl.BlockSpec((3, rows, width), lambda i, me: (0, 0, 0))] * n,
            out_specs=any_specs(3),
            scratch_shapes=[pltpu.SemaphoreType.DMA((n, 3))],
        ),
        out_shape=[jax.ShapeDtypeStruct((rows, n * width), BF16)] * 3,
        compiler_params=params(),
        cost_estimate=cost(0, 48 * n * rows * width),
        name="assemble_heads",
    )(place, *pieces)


def shift(x, axis, by):
    n = lax.axis_size(axis)
    return lax.ppermute(x, axis, [(i, (i + by) % n) for i in range(n)])


def swap(x, axis, mask):
    n = lax.axis_size(axis)
    return lax.ppermute(x, axis, [(i, i ^ mask) for i in range(n)])


def chip_swap(x, axis, step):
    n = lax.axis_size(axis)
    return lax.ppermute(x, axis, [(i, i ^ (2 if (i + step) % 2 == 0 else 4)) for i in range(n)])


def line_move(x, dp_axis, axis, up):
    n, dp = lax.axis_size(axis), lax.axis_size(dp_axis)
    pairs = []
    for g in range(dp):
        for d in range(n - 1):
            low, high = g * n + d, g * n + d + 1
            pairs.append((low, high) if (g % 2 == 0) == up else (high, low))
    return lax.ppermute(x, (dp_axis, axis), pairs)


def line_payload(place, got, parts, g, t, n):
    shape = got[0].shape

    def body(place_ref, forward, back, part_f, part_b, out_f, out_b):
        pos = position(place_ref, n)
        for passes, x, part, out in (
            (pos >= t, forward, part_f, out_f),
            (n - 1 - pos >= t, back, part_b, out_b),
        ):

            @pl.when(passes)
            def _():
                out[...] = x[...]

            @pl.when(jnp.logical_not(passes))
            def _():
                out[...] = add_rounded(part[0, 0], x[...])

    block = pl.BlockSpec(shape, lambda i, p: (0, 0))

    def term(s):
        return pl.BlockSpec((1, 1, *shape), lambda i, p: (g, s, 0, 0))

    return pl.pallas_call(
        body,
        grid_spec=pltpu.PrefetchScalarGridSpec(
            num_scalar_prefetch=1,
            grid=(1,),
            in_specs=[block, block, term(n - t), term(t)],
            out_specs=[block] * 2,
        ),
        out_shape=[jax.ShapeDtypeStruct(shape, BF16)] * 2,
        compiler_params=params(8),
        cost_estimate=cost(0, 12 * got[0].size),
        name="line_payload",
    )(place, *got, parts, parts)


def after(x, done):
    return lax.optimization_barrier((x, done))[0]


def by_heads(query, key_in, value, gate_table, timestep, out_weight, grad_out):
    n, dp = lax.axis_size("ctx"), lax.axis_size("dp")
    me = lax.axis_index("ctx").astype(jnp.int32)
    index = lax.axis_index("dp").astype(jnp.int32)
    place = jnp.stack([me, index % 2, index])

    packed = pack_call(query, key_in, value, "ctx")
    pieces = [packed[0]] + [shift(packed[s], "ctx", s) for s in range(1, n)]
    gate_row = lax.dynamic_slice_in_dim(gate_table, timestep[0], 1, 0)

    mine = after(out_weight, packed)
    own = swap(mine, "dp", 1)
    one = chip_swap(mine, "dp", 0)
    two = chip_swap(after(mine, (one, pieces[1])), "dp", 1)
    far = chip_swap(after(one, pieces[1]), "dp", 1)
    d_proj = (grad_out[0].astype(F32) * gate_row).astype(BF16)
    shards = [out_weight, one, two, far, own, swap(one, "dp", 1), swap(two, "dp", 1)]
    shards += [swap(x, "dp", 1) for x in jnp.split(after(far, d_proj), FAR_PARTS)]
    parts = d_attn_parts_call(place, d_proj, shards, n)
    attended, exps, kept = attention_call(place, after(pieces, parts), 0, n)
    attention, weights = [attended], [list(exps)]
    for g in range(1, PARTS):
        attended, exps, _ = attention_call(place, kept, g, n)
        attention.append(attended)
        weights.append(list(exps))

    def both_ways(forward, back):
        return line_move(forward, "dp", "ctx", True), line_move(back, "dp", "ctx", False)

    def items(s):
        if s == 0:
            return [(a, a) for a in attention]
        return [(got[g][n - s - 1][0], got[g][s - 1][1]) for g in range(PARTS)]

    got = [[both_ways(a, a)] for a in attention]
    for t in range(1, n):
        sent = [line_payload(place, got[g][-1], parts, g, t, n) for g in range(PARTS)]
        for g in range(PARTS):
            got[g].append(both_ways(*sent[g]))
    steps = sorted(range(n), key=lambda s: max(s, n - s) if s else 0)
    keep, send = weight_grad_call(place, steps, [items(s) for s in steps], d_proj, n)
    received = swap(send, "dp", 1)
    behind = [[got[g][i][0] for i in range(n - 1)] for g in range(PARTS)]
    front = [[got[g][i][1] for i in range(n - 1)] for g in range(PARTS)]
    d_terms = [[got[g][-1][i] for g in range(PARTS)] for i in range(2)]

    grads = attention_grad_call(place, kept, weights, attention, parts, d_terms, n)
    received = after(received, grads)
    far = add_rounded(keep[2:], received[2:])
    grads = [grads[0]] + [shift(grads[s], "ctx", -s) for s in range(1, n)]
    far = chip_swap(far, "dp", 0)
    near = keep[:2].astype(F32) + received[:2].astype(F32) + far.astype(F32)
    halves = jnp.split(near[1].astype(BF16), 2, axis=0)
    last = jnp.concatenate([chip_swap(x, "dp", 1) for x in halves], axis=0)
    grad_weight = near[0] + last.astype(F32)

    gate_row = after(gate_row, near)
    branch_out = projection_call(place, attention, behind, front, shards, gate_row, n)[None]
    grad_query, grad_key, grad_value = assemble_call(place, after(grads, branch_out))
    return (branch_out, grad_query[None], grad_key[None], grad_value[None], grad_weight)


def by_tokens(query, key_in, value, gate_table, timestep, out_weight, grad_out):
    slab_rows = query.shape[1]
    attn_width = query.shape[2]
    head_count = attn_width // HEAD_DIM
    score_scale = HEAD_DIM ** (-0.5)
    query_heads = query[0].reshape(slab_rows, head_count, HEAD_DIM)
    keys_whole, values_whole = (
        lax.all_gather(key_in, "ctx", axis=1, tiled=True),
        lax.all_gather(value, "ctx", axis=1, tiled=True),
    )
    keys_all = keys_whole[0]
    values_all = values_whole[0]
    scores = (
        jnp.einsum(
            "qhd,khd->hqk",
            query_heads,
            keys_all.reshape(keys_all.shape[0], head_count, HEAD_DIM),
            preferred_element_type=jnp.float32,
        )
        * score_scale
    )
    length = keys_all.shape[0]
    key_heads = keys_all.reshape(length, head_count, HEAD_DIM)
    value_heads = values_all.reshape(length, head_count, HEAD_DIM)
    row_max = jnp.max(scores, axis=2, keepdims=True)
    exp_scores = jnp.exp(scores - row_max)
    probability = exp_scores / jnp.sum(exp_scores, axis=2, keepdims=True)
    prob_half = probability.astype(jnp.bfloat16)
    attention = jnp.einsum(
        "hqk,khd->qhd", prob_half, value_heads, preferred_element_type=jnp.float32
    )
    attention = attention.reshape(slab_rows, attn_width).astype(jnp.bfloat16)
    marker = (
        timestep[:, None] == jnp.arange(gate_table.shape[0], dtype=jnp.int32)[None, :]
    ).astype(jnp.float32)
    gate_row = jnp.dot(marker, gate_table, precision=lax.Precision.HIGHEST)
    attn_rows = lax.all_gather(attention, "ctx", axis=0, tiled=True)
    columns = attn_rows
    projected = jnp.dot(
        columns,
        lax.all_gather(out_weight, "dp", axis=0, tiled=True),
        preferred_element_type=jnp.float32,
    )
    branch_out = (projected * gate_row).astype(jnp.bfloat16)[None]
    d_proj = (grad_out[0].astype(jnp.float32) * gate_row).astype(jnp.bfloat16)
    partial_rows = jnp.einsum(
        "td,rd->tr",
        d_proj,
        lax.all_gather(out_weight, "dp", axis=0, tiled=True),
        preferred_element_type=jnp.float32,
    )
    d_attn = lax.psum_scatter(
        partial_rows.astype(jnp.bfloat16), "ctx", scatter_dimension=0, tiled=True
    ).astype(jnp.float32)
    d_attn = d_attn.astype(jnp.bfloat16)
    columns = attn_rows
    grad_weight = lax.psum_scatter(
        jnp.einsum("tr,td->rd", columns, d_proj, preferred_element_type=jnp.float32).astype(
            jnp.bfloat16
        ),
        "dp",
        scatter_dimension=0,
        tiled=True,
    ).astype(jnp.float32)
    d_heads = d_attn.reshape(slab_rows, head_count, HEAD_DIM)
    out_heads = attention.reshape(slab_rows, head_count, HEAD_DIM)
    row_delta = jnp.einsum("qhd,qhd->hq", d_heads, out_heads, preferred_element_type=jnp.float32)
    d_scores = jnp.einsum("qhd,khd->hqk", d_heads, value_heads, preferred_element_type=jnp.float32)
    d_half = (probability * (d_scores - row_delta[:, :, None]) * score_scale).astype(jnp.bfloat16)
    grad_query = jnp.einsum("hqk,khd->qhd", d_half, key_heads, preferred_element_type=jnp.float32)
    grad_query = grad_query.reshape(slab_rows, attn_width).astype(jnp.bfloat16)
    key_part = jnp.einsum(
        "hqk,qhd->khd", d_half, query_heads, preferred_element_type=jnp.float32
    ).reshape(slab_rows * lax.axis_size("ctx"), attn_width)
    value_part = jnp.einsum(
        "hqk,qhd->khd", prob_half, d_heads, preferred_element_type=jnp.float32
    ).reshape(slab_rows * lax.axis_size("ctx"), attn_width)
    key_sums = lax.psum_scatter(
        jnp.concatenate([key_part, value_part], axis=1).astype(jnp.bfloat16),
        "ctx",
        scatter_dimension=0,
        tiled=True,
    ).astype(jnp.float32)
    grad_key = key_sums[:, :attn_width].astype(jnp.bfloat16)
    grad_value = key_sums[:, attn_width:].astype(jnp.bfloat16)
    return (branch_out, grad_query[None], grad_key[None], grad_value[None], grad_weight)


def on_device(query, key_in, value, gate_table, timestep, out_weight, grad_out):
    n, dp = lax.axis_size("ctx"), lax.axis_size("dp")
    heads = query.shape[2] // HEAD_DIM
    fits = heads % n == 0 and dp == 8 and dp == 2 * n
    fits = fits and out_weight.shape[0] * dp == query.shape[2]
    plan = by_heads if fits else by_tokens
    return plan(query, key_in, value, gate_table, timestep, out_weight, grad_out)


def solution(mesh):
    in_specs = (
        P("dp", "ctx", None),
        P("dp", "ctx", None),
        P("dp", "ctx", None),
        P(None, "ctx"),
        P("dp"),
        P("dp", "ctx"),
        P("dp", None, "ctx"),
    )
    out_specs = (
        P("dp", None, "ctx"),
        P("dp", "ctx", None),
        P("dp", "ctx", None),
        P("dp", "ctx", None),
        P("dp", "ctx"),
    )
    return jax.shard_map(
        on_device, mesh=mesh, in_specs=in_specs, out_specs=out_specs, check_vma=False
    )
```
